32 devices in a mesh: seq: 8 (over y, x, core), tp: 4 (over z).
Axes of the slice: x: 2, y: 2, z: 4, core: 2. Of those that a mesh axis runs over, the one named last changes fastest.
Arguments:
- inputs: bfloat16 [4096, 2048], P(('seq', 'tp')), may hold values from -6 to 6
- segment_ids: int32 [4096], P('seq'), may hold values from 0 to 15, as said below
- cotangent: bfloat16 [4096, 2048], P(('seq', 'tp')), may hold values from -6 to 6
- qkv_weight: bfloat16 [3, 2048, 2048], P(None, None, 'tp'), may hold values from -0.125 to 0.125
- qkv_bias: bfloat16 [3, 2048], P(None, 'tp'), may hold values from -3 to 3
- out_weight: bfloat16 [2048, 2048], P('tp'), may hold values from -0.125 to 0.125
- out_bias: bfloat16 [2048], replicated, may hold values from -3 to 3
- up_weight: bfloat16 [2048, 8192], P(None, 'tp'), may hold values from -0.125 to 0.125
- up_bias: bfloat16 [8192], P('tp'), may hold values from -3 to 3
- down_weight: bfloat16 [8192, 2048], P('tp'), may hold values from -0.0625 to 0.0625
- down_bias: bfloat16 [2048], replicated, may hold values from -3 to 3
- input_gain: bfloat16 [2048], replicated, may hold values from 0.25 to 1.75
- input_bias: bfloat16 [2048], replicated, may hold values from -2 to 2
- mixed_gain: bfloat16 [2048], P('tp'), may hold values from 0.25 to 1.75
- mixed_bias: bfloat16 [2048], P('tp'), may hold values from -2 to 2
- middle_gain: bfloat16 [2048], replicated, may hold values from 0.25 to 1.75
- middle_bias: bfloat16 [2048], replicated, may hold values from -2 to 2
- hidden_gain: bfloat16 [8192], P('tp'), may hold values from 0.25 to 1.75
- hidden_bias: bfloat16 [8192], P('tp'), may hold values from -2 to 2
- qkv_average: float32 [3, 2048, 2048], P(None, 'seq', 'tp'), may hold values from -0.125 to 0.125
- out_average: float32 [2048, 2048], P('tp', 'seq'), may hold values from -0.125 to 0.125
- up_average: float32 [2048, 8192], P('seq', 'tp'), may hold values from -0.125 to 0.125
- down_average: float32 [8192, 2048], P('tp', 'seq'), may hold values from -0.0625 to 0.0625
- decay_rate: float32 [1], replicated, may hold values from 0.5 to 0.8
Outputs:
- layer_out: bfloat16 [4096, 2048], P(('seq', 'tp'))
- input_grad: bfloat16 [4096, 2048], P(('seq', 'tp'))
- qkv_grad: float32 [3, 2048, 2048], P(None, 'seq', 'tp')
- qkvbias_grad: float32 [3, 2048], P(None, ('tp', 'seq'))
- out_grad: float32 [2048, 2048], P('tp', 'seq')
- outbias_grad: float32 [2048], P(('seq', 'tp'))
- up_grad: float32 [2048, 8192], P('seq', 'tp')
- upbias_grad: float32 [8192], P(('tp', 'seq'))
- down_grad: float32 [8192, 2048], P('tp', 'seq')
- downbias_grad: float32 [2048], P(('seq', 'tp'))
- inputgain_grad: float32 [2048], P(('seq', 'tp'))
- inputbias_grad: float32 [2048], P(('seq', 'tp'))
- mixedgain_grad: float32 [2048], P(('tp', 'seq'))
- mixedbias_grad: float32 [2048], P(('tp', 'seq'))
- middlegain_grad: float32 [2048], P(('seq', 'tp'))
- middlebias_grad: float32 [2048], P(('seq', 'tp'))
- hiddengain_grad: float32 [8192], P(('tp', 'seq'))
- hiddenbias_grad: float32 [8192], P(('tp', 'seq'))
- qkv_new: float32 [3, 2048, 2048], P(None, 'seq', 'tp')
- out_new: float32 [2048, 2048], P('tp', 'seq')
- up_new: float32 [2048, 8192], P('seq', 'tp')
- down_new: float32 [8192, 2048], P('tp', 'seq')
The draws below stay inside these ranges and needn't reach their ends.
Inputs may be any that keep to these rules, and one draw needn't show every extreme that they name: `segment_ids`: the tokens form one packed row of 4096 tokens holding exactly 16 documents; segment ids start at 0 and rise by one at each new document; one document begins within the first 512 tokens and ends within the last 512 tokens.
All inputs are finite; a program needn't handle non-finite values.
Results may differ from the reference program's by a relative error of at most 0.014.
Values may be sent and summed in bfloat16 or wider, within the bound.
No kernel may reach another device: no remote copies, remote signals or barrier semaphores. Data moves between devices by JAX's collectives and lax.ppermute only.
A program may use at most 256 MiB of HBM per device.

```python
import math
import jax
import jax.numpy as jnp
from jax import lax

D = 2048
H = 32
FF = 8192
TOK_SEQ = 512
COUNT = 16
HD = 64
TOKENS = 4096


def draw_segment_ids(key, part):
    early_cuts = jax.random.permutation(jax.random.fold_in(key, 11), TOK_SEQ - 1)[:COUNT - 2] + 1
    late_cut = TOKENS - jax.random.randint(jax.random.fold_in(key, 13), (), 1, TOK_SEQ)
    marks = jnp.zeros((TOKENS,), jnp.int32).at[early_cuts].set(1)
    marks = marks.at[late_cut].set(1)
    return jnp.cumsum(marks).astype(jnp.int32)


def level_of(key, extent, split, least, top_value):
    level = 1.0
    for dim, shards_of in split:
        heights = jax.random.uniform(jax.random.fold_in(jax.random.fold_in(key, 6), dim), (shards_of,), jnp.float32, least / len(split), top_value / len(split))
        level = level * jnp.repeat(jnp.exp(heights), extent[dim] // shards_of).reshape((-1,) + (1,) * (len(extent) - 1 - dim))
    return level


def scatter_about(rng, dims, scale, reach, pieces=(), held_as=jnp.bfloat16):
    drawn = scale * jax.random.normal(rng, dims, jnp.float32)
    if pieces:
        drawn = drawn * level_of(rng, dims, pieces, -0.22, 0.18)
    return jnp.clip(drawn, -reach, reach).astype(held_as)


def setup_inputs(seed: int = 0) -> dict:
    seeds = jax.random.split(jax.random.key(seed), 25)
    return {
        "inputs": scatter_about(seeds[0], (TOKENS, D), 1.0, 6.0, ((0, 32),)),
        "segment_ids": draw_segment_ids(jax.random.fold_in(seeds[24], 71), 0),
        "cotangent": scatter_about(seeds[2], (TOKENS, D), 1.0, 6.0, ((0, 32),)),
        "qkv_weight": scatter_about(seeds[3], (3, D, D), D ** -0.5, 0.125, ((2, 4),)),
        "qkv_bias": scatter_about(seeds[4], (3, D), 0.5, 3.0, ((1, 4),)),
        "out_weight": scatter_about(seeds[5], (D, D), D ** -0.5, 0.125, ((0, 4),)),
        "out_bias": scatter_about(seeds[6], (D,), 0.5, 3.0),
        "up_weight": scatter_about(seeds[7], (D, FF), D ** -0.5, 0.125, ((1, 4),)),
        "up_bias": scatter_about(seeds[8], (FF,), 0.5, 3.0, ((0, 4),)),
        "down_weight": scatter_about(seeds[9], (FF, D), FF ** -0.5, 0.0625, ((0, 4),)),
        "down_bias": scatter_about(seeds[10], (D,), 0.5, 3.0),
        "input_gain": jnp.clip(1.0 + 0.15 * jax.random.normal(seeds[11], (D,), jnp.float32), 0.25, 1.75).astype(jnp.bfloat16),
        "input_bias": scatter_about(seeds[12], (D,), 0.3, 2.0),
        "mixed_gain": jnp.clip(1.0 + 0.15 * jax.random.normal(seeds[13], (D,), jnp.float32), 0.25, 1.75).astype(jnp.bfloat16),
        "mixed_bias": scatter_about(seeds[14], (D,), 0.3, 2.0, ((0, 4),)),
        "middle_gain": jnp.clip(1.0 + 0.15 * jax.random.normal(seeds[15], (D,), jnp.float32), 0.25, 1.75).astype(jnp.bfloat16),
        "middle_bias": scatter_about(seeds[16], (D,), 0.3, 2.0),
        "hidden_gain": jnp.clip(1.0 + 0.15 * jax.random.normal(seeds[17], (FF,), jnp.float32), 0.25, 1.75).astype(jnp.bfloat16),
        "hidden_bias": scatter_about(seeds[18], (FF,), 0.3, 2.0, ((0, 4),)),
        "qkv_average": scatter_about(seeds[19], (3, D, D), D ** -0.5, 0.125, ((1, 8), (2, 4)), jnp.float32),
        "out_average": scatter_about(seeds[20], (D, D), D ** -0.5, 0.125, ((0, 4), (1, 8)), jnp.float32),
        "up_average": scatter_about(seeds[21], (D, FF), D ** -0.5, 0.125, ((0, 8), (1, 4)), jnp.float32),
        "down_average": scatter_about(seeds[22], (FF, D), FF ** -0.5, 0.0625, ((0, 4), (1, 8)), jnp.float32),
        "decay_rate": jnp.clip(jax.random.uniform(seeds[23], (1,), jnp.float32, 0.5, 0.8), 0.5, 0.8),
    }


SCALE = 0.125
EPSILON = 1e-05
NEGATIVE = -1e+30
HIGHEST = lax.Precision.HIGHEST

@jax.custom_vjp
def low(v):
    return lax.optimization_barrier(v.astype(jnp.bfloat16)).astype(jnp.float32)

@jax.custom_vjp
def low_back(v):
    return v

def low_keep(v):
    return (low(v), None)

def low_pass(kept, grad):
    return (grad,)

def back_keep(v):
    return (v, None)

def back_low(kept, grad):
    return (low(grad),)
low.defvjp(low_keep, low_pass)
low_back.defvjp(back_keep, back_low)

def xpos_tables(positions, head_size):
    half = head_size // 2
    index = jnp.arange(half, dtype=jnp.float32)
    frequency = jnp.exp(index * (-2.0 * math.log(10000.0) / head_size))
    zeta = (index * (2.0 / head_size) + 0.4) / 1.4
    places = positions.astype(jnp.float32)[:, None]
    angle = places * frequency[None, :]
    growth = jnp.exp(places * (jnp.log(zeta)[None, :] / 512.0))
    return (jnp.cos(angle), jnp.sin(angle), growth)

def turn(values, cosine, sine, scale, head_size):
    rows = values.shape[0]
    shaped = values.reshape(rows, -1, head_size)
    half = head_size // 2
    first = shaped[:, :, :half]
    second = shaped[:, :, half:]
    cosine = cosine[:, None, :]
    sine = sine[:, None, :]
    scale = scale[:, None, :]
    turned = jnp.concatenate([(first * cosine - second * sine) * scale, (second * cosine + first * sine) * scale], axis=2)
    return turned.reshape(values.shape)

def norm_rows(values, gain, shift):
    center = lax.optimization_barrier(jnp.mean(values, axis=-1, keepdims=True))
    spread = lax.optimization_barrier(jnp.mean(values * values, axis=-1, keepdims=True)) - center * center
    return (values - center) * lax.rsqrt(spread + EPSILON) * gain + shift

def product(left, right):
    return jnp.dot(left, right, precision=HIGHEST)

def reference(inputs, segment_ids, cotangent, qkv_weight, qkv_bias, out_weight, out_bias, up_weight, up_bias, down_weight, down_bias, input_gain, input_bias, mixed_gain, mixed_bias, middle_gain, middle_bias, hidden_gain, hidden_bias, qkv_average, out_average, up_average, down_average, decay_rate):
    index = jnp.arange(TOKENS, dtype=jnp.int32)
    fresh = jnp.concatenate([jnp.ones((1,), dtype=bool), segment_ids[1:] != segment_ids[:-1]])
    row_start = lax.cummax(jnp.where(fresh, index, 0), axis=0)
    cosine, sine, growth = xpos_tables(index - row_start, HD)
    shrink = 1.0 / growth
    block = min(512, TOKENS)
    block_count = TOKENS // block

    def attend(queries, rows, starts, keys, values):
        raw = low_back(jnp.einsum('qhd,khd->hqk', queries, keys, precision=HIGHEST) * SCALE)
        allowed = (index[None, :] <= rows[:, None]) & (index[None, :] >= starts[:, None])
        probs = jax.nn.softmax(jnp.where(allowed[None], raw, NEGATIVE), axis=-1)
        return jnp.einsum('hqk,khd->qhd', low(probs), values, precision=HIGHEST)
    attend_saved = jax.checkpoint(attend)

    def forward(inputs_wide, qkv_weight, qkv_bias, out_weight, out_bias, up_weight, up_bias, down_weight, down_bias, input_gain, input_bias, mixed_gain, mixed_bias, middle_gain, middle_bias, hidden_gain, hidden_bias):
        attn_in = low(norm_rows(inputs_wide, input_gain, input_bias))
        projected = jnp.einsum('rd,cdf->crf', attn_in, qkv_weight, precision=HIGHEST) + qkv_bias[:, None, :]
        query = low_back(projected[0])
        key = low_back(projected[1])
        value = low(low_back(projected[2]))
        query_turned = low(turn(query, cosine, sine, growth, HD)).reshape(block_count, block, H, HD)
        key_turned = low(turn(key, cosine, sine, shrink, HD)).reshape(TOKENS, H, HD)
        value_heads = value.reshape(TOKENS, H, HD)
        mixed = lax.map(lambda item: attend_saved(item[0], item[1], item[2], key_turned, value_heads), (query_turned, index.reshape(block_count, block), row_start.reshape(block_count, block)))
        mixed = low_back(mixed.reshape(TOKENS, D))
        mixed_normed = low(norm_rows(mixed, mixed_gain, mixed_bias))
        middle = inputs_wide + low_back(product(mixed_normed, out_weight) + out_bias)
        ffn_in = low(norm_rows(middle, middle_gain, middle_bias))
        up_value = low_back(product(ffn_in, up_weight) + up_bias)
        hidden = low(norm_rows(jax.nn.gelu(up_value, approximate=False), hidden_gain, hidden_bias))
        return middle + product(hidden, down_weight) + down_bias
    params = tuple((item.astype(jnp.float32) for item in (inputs, qkv_weight, qkv_bias, out_weight, out_bias, up_weight, up_bias, down_weight, down_bias, input_gain, input_bias, mixed_gain, mixed_bias, middle_gain, middle_bias, hidden_gain, hidden_bias)))
    layer_out, pullback = jax.vjp(forward, *params)
    grads = pullback(cotangent.astype(jnp.float32))
    rate = decay_rate[0]
    qkv_new = rate * qkv_average + (1.0 - rate) * qkv_weight.astype(jnp.float32)
    out_new = rate * out_average + (1.0 - rate) * out_weight.astype(jnp.float32)
    up_new = rate * up_average + (1.0 - rate) * up_weight.astype(jnp.float32)
    down_new = rate * down_average + (1.0 - rate) * down_weight.astype(jnp.float32)
    return (layer_out.astype(jnp.bfloat16), grads[0].astype(jnp.bfloat16), grads[1], grads[2], grads[3], grads[4], grads[5], grads[6], grads[7], grads[8], grads[9], grads[10], grads[11], grads[12], grads[13], grads[14], grads[15], grads[16], qkv_new, out_new, up_new, down_new)
```

```python
import functools
import math

import jax
import jax.numpy as jnp
from jax import lax
from jax.experimental import pallas as pl
from jax.experimental.pallas import tpu as pltpu
from jax.sharding import PartitionSpec as P

FF = 8192
COUNT = 16
HD = 64

SCALE = 0.125
LOG2E = 1.4426950408889634
EPSILON = 1e-05
OUTSIDE = -2e30
LOWEST = -1e30
LARGEST = 1 << 30
WIDE = jnp.float32
NARROW = jnp.bfloat16
MIB = 1 << 20


def xpos_tables(positions, head_size):
    half = head_size // 2
    index = jnp.arange(half, dtype=jnp.float32)
    frequency = jnp.exp(index * (-2.0 * math.log(10000.0) / head_size))
    zeta = (index * (2.0 / head_size) + 0.4) / 1.4
    places = positions.astype(jnp.float32)[:, None]
    angle = places * frequency[None, :]
    growth = jnp.exp(places * (jnp.log(zeta)[None, :] / 512.0))
    return (jnp.cos(angle), jnp.sin(angle), growth)


def norm_rows(values, gain, shift):
    center = jnp.mean(values, axis=-1, keepdims=True)
    spread = jnp.mean(values * values, axis=-1, keepdims=True) - center * center
    return (values - center) * lax.rsqrt(spread + EPSILON) * gain + shift


def exact_gelu(values):
    return jax.nn.gelu(values, approximate=False)


def gather_rows(values):
    return lax.all_gather(values, "tp", axis=0, tiled=True)


def scatter_rows(values):
    return lax.psum_scatter(values.astype(NARROW), "tp", scatter_dimension=0, tiled=True).astype(WIDE)


def hop(values, axis, mask, count):
    return lax.ppermute(values, axis, [(i, i ^ mask) for i in range(count)])


def tp_total(values):
    count = lax.axis_size("tp")
    if count & (count - 1):
        return lax.psum(values, "tp")
    total = values
    for mask in range(1, count):
        total = total + hop(values, "tp", mask, count)
    return total


def after(value, *others):
    return lax.optimization_barrier((value,) + others)[0]


def halving(values, bits, count):
    axes = sorted(bits, reverse=True)
    for bit in bits:
        axis = axes.index(bit)
        keep = lax.index_in_dim(values, 0, axis, keepdims=False)
        send = lax.index_in_dim(values, 1, axis, keepdims=False)
        got = hop(send, "seq", 1 << bit, count)
        values = keep.astype(WIDE) + got.astype(WIDE)
        axes.remove(bit)
        if axes:
            values = values.astype(NARROW)
    return values


def vector_scatter(values, rank, count):
    bit = count // 2
    while bit:
        pair = values.reshape(2, bit, -1)
        mine = (rank & bit) // bit
        send = lax.dynamic_index_in_dim(pair, 1 - mine, 0, keepdims=False)
        keep = lax.dynamic_index_in_dim(pair, mine, 0, keepdims=False)
        values = keep + hop(send, "seq", bit, count)
        bit //= 2
    return values.reshape(-1)


def tp_scatter(values):
    count = lax.axis_size("tp")
    rank = lax.axis_index("tp")
    if count & (count - 1):
        return lax.psum_scatter(values, "tp", scatter_dimension=0)
    total = lax.dynamic_index_in_dim(values, rank, 0, keepdims=False)
    for mask in range(1, count):
        part = lax.dynamic_index_in_dim(values, rank ^ mask, 0, keepdims=False)
        total = total + hop(part, "tp", mask, count)
    return total


def sent_kernel(place, left, right, out, *, tall):
    if tall:
        out[0] = lax.dot_general(
            left[...], right[...], (((0,), (0,)), ((), ())), preferred_element_type=WIDE
        ).astype(NARROW)
    else:
        turned = right[...].T
        for c in range(left.shape[0]):
            out[0, c] = jnp.dot(turned, left[c], preferred_element_type=WIDE).astype(NARROW)


def kept_kernel(place, left, right, got, first, second, *, tall):
    if tall:
        total = lax.dot_general(
            left[...], right[...], (((0,), (0,)), ((), ())), preferred_element_type=WIDE
        ) + got[0].astype(WIDE)
        cut = total.shape[0] // 2
        first[0] = total[:cut].astype(NARROW)
        second[0] = total[cut:].astype(NARROW)
    else:
        turned = right[...].T
        cut = turned.shape[0] // 2
        for c in range(left.shape[0]):
            total = jnp.dot(turned, left[c], preferred_element_type=WIDE) + got[0, c].astype(WIDE)
            first[0, c] = total[:cut].astype(NARROW)
            second[0, c] = total[cut:].astype(NARROW)


def gradient_blocks(seat, left, right, count, tall, got=None):
    rows = right.shape[0]
    part = right.shape[1] // count
    slots = count // 2
    if tall:
        block = (left.shape[1], part)
        half = (left.shape[1] // 2, part)
        left_spec = pl.BlockSpec(left.shape, lambda k, seat: (0, 0))
    else:
        block = (left.shape[0], part, left.shape[2])
        half = (left.shape[0], part // 2, left.shape[2])
        left_spec = pl.BlockSpec(left.shape, lambda k, seat: (0, 0, 0))
    zeros = (0,) * len(block)
    if part % 128:
        order = 2 * (jnp.arange(slots, dtype=jnp.int32) ^ seat[0]) + seat[1]
        right = right.reshape(rows, count, part)[:, order].transpose(1, 0, 2)
        right_spec = pl.BlockSpec((None, rows, part), lambda k, seat: (k, 0, 0))
    else:
        right_spec = pl.BlockSpec((rows, part), lambda k, seat: (0, 2 * (k ^ seat[0]) + seat[1]))
    block_spec = pl.BlockSpec((1,) + block, lambda k, seat: (k,) + zeros)
    half_spec = pl.BlockSpec((1,) + half, lambda k, seat: (k,) + zeros)
    whole = jax.ShapeDtypeStruct((slots,) + block, NARROW)
    piece = jax.ShapeDtypeStruct((slots,) + half, NARROW)
    flops = left.size * part * slots * 2
    moved = 2 * left.size + right.size + 2 * left.size // rows * part * slots
    return pl.pallas_call(
        functools.partial(sent_kernel if got is None else kept_kernel, tall=tall),
        grid_spec=pltpu.PrefetchScalarGridSpec(
            num_scalar_prefetch=1,
            grid=(slots,),
            in_specs=[left_spec, right_spec] + ([] if got is None else [block_spec]),
            out_specs=block_spec if got is None else (half_spec, half_spec),
        ),
        out_shape=whole if got is None else (piece, piece),
        compiler_params=params(32),
        cost_estimate=pl.CostEstimate(flops=flops, bytes_accessed=moved, transcendentals=0),
    )(seat, left, right, *([] if got is None else [got]))


def seq_gradient(left, right, rank, count, tall):
    own = rank >> 1
    side = rank & 1
    sent = gradient_blocks(jnp.stack([own, 1 - side]), left, right, count, tall)
    got = hop(sent, "seq", 1, count)
    pieces = gradient_blocks(jnp.stack([own, side]), left, right, count, tall, got)
    return pieces


def finish_gradient(pieces, count, axis):
    levels = count.bit_length() - 2
    bits = list(range(1, levels + 1))
    first, second = (p.reshape((2,) * levels + p.shape[1:]) for p in pieces)
    return jnp.concatenate(
        [halving(first, bits, count), halving(second, bits[::-1], count)], axis=axis
    )


def whole_spec():
    return pl.BlockSpec(memory_space=pltpu.VMEM)


def scalar_spec():
    return pl.BlockSpec(memory_space=pltpu.SMEM)


def params(mib):
    return pltpu.CompilerParams(vmem_limit_bytes=mib * MIB)


def turn_packed(values, straight, crossed):
    lane = lax.broadcasted_iota(jnp.int32, values.shape, 1)
    ahead = pltpu.roll(values, 2 * HD - HD // 2, 1)
    behind = pltpu.roll(values, HD // 2, 1)
    partner = jnp.where((lane & (HD // 2)) == 0, ahead, behind)
    return values * straight + partner * crossed


def pack_kernel(place, rows, weight, bias, straight, crossed, *rest):
    outs, held = rest[:-1], rest[-1]
    count = len(outs)
    half = rows.shape[0] // 2
    total = rows.shape[0]
    for pair in range(count // 2):
        cols = slice(pair * 2 * HD, (pair + 1) * 2 * HD)
        query, key, value = (
            jnp.dot(rows[...], weight[c, :, cols], preferred_element_type=WIDE)
            + bias[c : c + 1, cols]
            for c in range(3)
        )
        for side in range(2):
            part = slice(side * HD, (side + 1) * HD)
            both = jnp.concatenate([query[:, part], key[:, part]], axis=1)
            held[2 * pair + side, :total, :] = turn_packed(
                both, straight[...], crossed[...]
            ).astype(NARROW)
            one = value[:, part]
            held[2 * pair + side, total:, :] = jnp.concatenate(
                [one[:half], one[half:]], axis=1
            ).astype(NARROW)
    me = place[0]
    for slot in range(count):
        outs[slot][...] = held[me ^ slot]


def pack_heads(place, rows, weight, bias, straight, crossed, count):
    total = rows.shape[0]
    shape = jax.ShapeDtypeStruct((total + total // 2, 2 * HD), NARROW)
    return pl.pallas_call(
        pack_kernel,
        out_shape=(shape,) * count,
        in_specs=[scalar_spec()] + [whole_spec()] * 5,
        out_specs=(whole_spec(),) * count,
        scratch_shapes=[pltpu.VMEM((count,) + shape.shape, NARROW)],
        compiler_params=params(48),
        cost_estimate=pl.CostEstimate(
            flops=2 * total * weight.size, bytes_accessed=weight.size * 2 + 8 * MIB, transcendentals=0
        ),
    )(place, rows, weight, bias, straight, crossed)


def split_chunk(chunk):
    block = chunk.shape[0] * 2 // 3
    both = chunk[:block, :]
    packed = chunk[block:, :]
    value = jnp.concatenate([packed[:, :HD], packed[:, HD:]], axis=0)
    return both[:, :HD], both[:, HD:], value


def allowed_mask(begin, q_begin, starts, shape):
    keys = begin + lax.broadcasted_iota(jnp.int32, shape, 0)
    queries = q_begin + lax.broadcasted_iota(jnp.int32, shape, 1)
    return (keys >= starts) & (keys <= queries)


def key_ranges(info, index, first_block, block):
    here = first_block + index
    low = info[2 + 2 * index] // block
    clear = jnp.minimum((info[3 + 2 * index] + block - 1) // block, here)
    return low, clear, here


def forward_kernel(info, starts, *refs, groups, spread):
    count = groups
    chunks = refs[:count]
    at = count + (1 if spread else 0)
    outs = refs[at : at + count]
    mixed, logs, keys, values, queries = refs[at + count :]
    me = info[0]
    first_block = info[1]
    block = starts.shape[2]
    for slot in range(count):
        query, key, value = split_chunk(chunks[slot][...])
        queries[me ^ slot] = query.T
        if not spread:
            keys[me ^ slot] = key
            values[me ^ slot] = value.T
    if spread:

        @pl.loop(0, keys.shape[0])
        def _(kb):
            _, key, value = split_chunk(refs[count][kb])
            keys[kb] = key
            values[kb] = value.T

    @pl.loop(0, count)
    def _(index):
        low, clear, here = key_ranges(info, index, first_block, block)
        query = queries[index]
        begins = starts[index]

        def step(kb, carry, masked):
            top, total, accum = carry
            raw = jnp.dot(keys[kb], query, preferred_element_type=WIDE)
            if masked:
                raw = jnp.where(
                    allowed_mask(kb * block, here * block, begins, raw.shape), raw, OUTSIDE
                )
            fresh = jnp.maximum(top, jnp.max(raw, axis=0, keepdims=True) * (SCALE * LOG2E))
            kept = jnp.exp2(raw * (SCALE * LOG2E) - fresh)
            fade = jnp.exp2(top - fresh)
            total = total * fade + jnp.sum(kept, axis=0, keepdims=True)
            accum = accum * fade + jnp.dot(
                values[kb], kept.astype(NARROW), preferred_element_type=WIDE
            )
            return fresh, total, accum

        carry = (
            jnp.full((1, block), LOWEST, WIDE),
            jnp.zeros((1, block), WIDE),
            jnp.zeros((HD, block), WIDE),
        )
        carry = lax.fori_loop(low, clear, functools.partial(step, masked=True), carry)
        carry = lax.fori_loop(clear, here, functools.partial(step, masked=False), carry)
        top, total, accum = step(here, carry, True)
        mixed[index] = accum / total
        logs[index] = top + jnp.log2(total)

    for slot in range(count):
        outs[slot][...] = mixed[me ^ slot].astype(NARROW)


def attend_forward(info, starts, chunks, everyone):
    count = len(chunks)
    block = starts.shape[2]
    spread = everyone is not None
    blocks = everyone.shape[0] if spread else count
    pairs = count * block * blocks * block // 2
    extra = [everyone] if spread else []
    return pl.pallas_call(
        functools.partial(forward_kernel, groups=count, spread=spread),
        out_shape=(jax.ShapeDtypeStruct((HD, block), NARROW),) * count
        + (
            jax.ShapeDtypeStruct((count, HD, block), WIDE),
            jax.ShapeDtypeStruct((count, 1, block), WIDE),
        ),
        in_specs=[scalar_spec()] + [whole_spec()] * (1 + count + len(extra)),
        out_specs=(whole_spec(),) * (count + 2),
        scratch_shapes=[
            pltpu.VMEM((blocks, block, HD), NARROW),
            pltpu.VMEM((blocks, HD, block), NARROW),
            pltpu.VMEM((count, HD, block), NARROW),
        ],
        compiler_params=params(48),
        cost_estimate=pl.CostEstimate(
            flops=16 * HD * pairs, bytes_accessed=4 * MIB, transcendentals=pairs
        ),
    )(info, starts, *chunks, *extra)


def backward_kernel(info, starts, logs, mixed, *refs, groups, spread):
    count = groups
    chunks = refs[:count]
    grads = refs[count : 2 * count]
    at = 2 * count
    if spread:
        everyone = refs[at]
        at += 1
    outs = refs[at : at + (1 if spread else count)]
    at += len(outs)
    keys, keys_up, values, queries, queries_up, downs, downs_up, key_sum, value_sum, query_sum = refs[at:]
    me = info[0]
    first_block = info[1]
    block = starts.shape[2]
    blocks = keys.shape[0]
    for slot in range(count):
        query, key, value = split_chunk(chunks[slot][...])
        place = me ^ slot
        queries[place] = query
        queries_up[place] = query.T
        down = grads[slot][...]
        downs_up[place] = down
        downs[place] = down.T
        if not spread:
            keys[place] = key
            keys_up[place] = key.T
            values[place] = value
    if spread:

        @pl.loop(0, blocks)
        def _(kb):
            _, key, value = split_chunk(everyone[kb])
            keys[kb] = key
            keys_up[kb] = key.T
            values[kb] = value

    key_sum[...] = jnp.zeros_like(key_sum)
    value_sum[...] = jnp.zeros_like(value_sum)

    @pl.loop(0, count)
    def _(index):
        low, clear, here = key_ranges(info, index, first_block, block)
        query_up = queries_up[index]
        down_up = downs_up[index]
        begins = starts[index]
        log = logs[index]
        delta = jnp.sum(down_up.astype(WIDE) * mixed[index], axis=0, keepdims=True)

        def step(kb, accum, masked):
            raw = jnp.dot(keys[kb], query_up, preferred_element_type=WIDE)
            probs = jnp.exp2(raw * (SCALE * LOG2E) - log)
            if masked:
                probs = jnp.where(
                    allowed_mask(kb * block, here * block, begins, raw.shape), probs, 0.0
                )
            grad_probs = jnp.dot(values[kb], down_up, preferred_element_type=WIDE)
            grad_scores = (probs * (grad_probs - delta)).astype(NARROW)
            value_sum[kb] += jnp.dot(
                probs.astype(NARROW), downs[index], preferred_element_type=WIDE
            )
            key_sum[kb] += jnp.dot(grad_scores, queries[index], preferred_element_type=WIDE)
            return accum + jnp.dot(keys_up[kb], grad_scores, preferred_element_type=WIDE)

        accum = jnp.zeros((HD, block), WIDE)
        accum = lax.fori_loop(low, clear, functools.partial(step, masked=True), accum)
        accum = lax.fori_loop(clear, here, functools.partial(step, masked=False), accum)
        query_sum[index] = step(here, accum, True)

    half = block // 2

    def packed(kb, query):
        both = jnp.concatenate([query, key_sum[kb]], axis=1) * SCALE
        one = value_sum[kb]
        return both.astype(NARROW), jnp.concatenate([one[:half], one[half:]], axis=1).astype(NARROW)

    if spread:

        @pl.loop(0, blocks)
        def _(kb):
            inside = (kb >= first_block) & (kb < first_block + count)
            query = query_sum[jnp.clip(kb - first_block, 0, count - 1)]
            both, value = packed(kb, jnp.where(inside, query, 0.0).T)
            outs[0][kb, :block, :] = both
            outs[0][kb, block:, :] = value

    else:
        for slot in range(count):
            place = me ^ slot
            both, value = packed(place, query_sum[place].T)
            outs[slot][:block, :] = both
            outs[slot][block:, :] = value


def attend_backward(info, starts, logs, mixed, chunks, grads, everyone):
    count = len(chunks)
    block = starts.shape[2]
    spread = everyone is not None
    blocks = everyone.shape[0] if spread else count
    pairs = count * block * blocks * block // 2
    extra = [everyone] if spread else []
    rows = block + block // 2
    if spread:
        shapes = (jax.ShapeDtypeStruct((blocks, rows, 2 * HD), NARROW),)
    else:
        shapes = (jax.ShapeDtypeStruct((rows, 2 * HD), NARROW),) * count
    tall = (block, HD)
    flat = (HD, block)
    return pl.pallas_call(
        functools.partial(backward_kernel, groups=count, spread=spread),
        out_shape=shapes,
        in_specs=[scalar_spec()] + [whole_spec()] * (3 + 2 * count + len(extra)),
        out_specs=(whole_spec(),) * len(shapes),
        scratch_shapes=[
            pltpu.VMEM((blocks,) + tall, NARROW),
            pltpu.VMEM((blocks,) + flat, NARROW),
            pltpu.VMEM((blocks,) + tall, NARROW),
            pltpu.VMEM((count,) + tall, NARROW),
            pltpu.VMEM((count,) + flat, NARROW),
            pltpu.VMEM((count,) + tall, NARROW),
            pltpu.VMEM((count,) + flat, NARROW),
            pltpu.VMEM((blocks,) + tall, WIDE),
            pltpu.VMEM((blocks,) + tall, WIDE),
            pltpu.VMEM((count,) + flat, WIDE),
        ],
        compiler_params=params(56),
        cost_estimate=pl.CostEstimate(
            flops=40 * HD * pairs, bytes_accessed=6 * MIB, transcendentals=pairs
        ),
    )(info, starts, logs, mixed, *chunks, *grads, *extra)


def join_kernel(place, *refs):
    count = len(refs) - 3
    chunks, out, sums, held = refs[:count], refs[count], refs[count + 1], refs[count + 2]
    me = place[0]
    total = 0.0
    squares = 0.0
    for slot in range(count):
        held[me ^ slot] = chunks[slot][...]
        wide = chunks[slot][...].astype(WIDE)
        total = total + jnp.sum(wide, axis=0, keepdims=True)
        squares = squares + jnp.sum(wide * wide, axis=0, keepdims=True)
    sums[0:1, :] = total
    sums[1:2, :] = squares
    for pair in range(count // 2):
        both = jnp.concatenate([held[2 * pair], held[2 * pair + 1]], axis=0)
        out[:, pair * 2 * HD : (pair + 1) * 2 * HD] = both.T


def join_heads(place, chunks):
    count = len(chunks)
    block = chunks[0].shape[1]
    return pl.pallas_call(
        join_kernel,
        out_shape=(
            jax.ShapeDtypeStruct((block, count * HD), NARROW),
            jax.ShapeDtypeStruct((2, block), WIDE),
        ),
        in_specs=[scalar_spec()] + [whole_spec()] * count,
        out_specs=(whole_spec(),) * 2,
        scratch_shapes=[pltpu.VMEM((count, HD, block), NARROW)],
        compiler_params=params(16),
        cost_estimate=pl.CostEstimate(flops=MIB, bytes_accessed=MIB, transcendentals=0),
    )(place, *chunks)


def cut_kernel(place, rows, *refs):
    outs, held = refs[:-1], refs[-1]
    me = place[0]
    count = len(outs)
    for pair in range(count // 2):
        both = rows[:, pair * 2 * HD : (pair + 1) * 2 * HD].T
        held[2 * pair] = both[:HD]
        held[2 * pair + 1] = both[HD:]
    for slot in range(count):
        outs[slot][...] = held[me ^ slot]


def cut_heads(place, rows, count):
    block = rows.shape[0]
    return pl.pallas_call(
        cut_kernel,
        out_shape=(jax.ShapeDtypeStruct((HD, block), NARROW),) * count,
        in_specs=[scalar_spec(), whole_spec()],
        out_specs=(whole_spec(),) * count,
        scratch_shapes=[pltpu.VMEM((count, HD, block), NARROW)],
        compiler_params=params(16),
        cost_estimate=pl.CostEstimate(flops=MIB, bytes_accessed=MIB, transcendentals=0),
    )(place, rows)


def unpack_kernel(place, straight, crossed, *refs):
    count = len(refs) - 3
    chunks, out, sums, held = refs[:count], refs[count], refs[count + 1], refs[count + 2]
    me = place[0]
    block = straight.shape[0]
    for slot in range(count):
        both = turn_packed(chunks[slot][:block, :].astype(WIDE), straight[...], -crossed[...])
        held[me ^ slot, :block, :] = both.astype(NARROW)
        held[me ^ slot, block:, :] = chunks[slot][block:, :]
    for pair in range(count // 2):
        parts = [split_chunk(held[2 * pair + side]) for side in range(2)]
        cols = slice(pair * 2 * HD, (pair + 1) * 2 * HD)
        for c in range(3):
            joined = jnp.concatenate([parts[0][c], parts[1][c]], axis=1)
            out[c, :, cols] = joined
            sums[c : c + 1, cols] = jnp.sum(joined.astype(WIDE), axis=0, keepdims=True)


def unpack_heads(place, straight, crossed, chunks):
    count = len(chunks)
    block = straight.shape[0]
    return pl.pallas_call(
        unpack_kernel,
        out_shape=(
            jax.ShapeDtypeStruct((3, block, count * HD), NARROW),
            jax.ShapeDtypeStruct((3, count * HD), WIDE),
        ),
        in_specs=[scalar_spec()] + [whole_spec()] * (2 + count),
        out_specs=(whole_spec(),) * 2,
        scratch_shapes=[pltpu.VMEM((count,) + chunks[0].shape, NARROW)],
        compiler_params=params(24),
        cost_estimate=pl.CostEstimate(flops=MIB, bytes_accessed=3 * MIB, transcendentals=0),
    )(place, straight, crossed, *chunks)


def shards(
    inputs,
    segment_ids,
    cotangent,
    qkv_weight,
    qkv_bias,
    out_weight,
    out_bias,
    up_weight,
    up_bias,
    down_weight,
    down_bias,
    input_gain,
    input_bias,
    mixed_gain,
    mixed_bias,
    middle_gain,
    middle_bias,
    hidden_gain,
    hidden_bias,
    qkv_average,
    out_average,
    up_average,
    down_average,
    decay_rate,
):
    seq_count = lax.axis_size("seq")
    seq_rank = lax.axis_index("seq")
    local_rows = segment_ids.shape[0]
    model_width = inputs.shape[1]
    local_width = qkv_weight.shape[2]
    heads_here = local_width // HD
    team = heads_here
    teams = seq_count // team
    place = seq_rank % team
    home = seq_rank - place

    def trade(chunks):
        return [chunks[0]] + [hop(chunks[m], "seq", m, seq_count) for m in range(1, team)]

    row_index = seq_rank * local_rows + jnp.arange(local_rows, dtype=jnp.int32)
    documents = jnp.arange(COUNT, dtype=jnp.int32)
    member = segment_ids[:, None] == documents[None, :]
    first_all = jnp.min(jnp.where(member, row_index[:, None], LARGEST), axis=0)
    bit = 1
    while bit < seq_count:
        first_all = jnp.minimum(first_all, hop(first_all, "seq", bit, seq_count))
        bit *= 2

    def starts_of(rows):
        earlier = first_all[None, :] <= rows[:, None]
        return jnp.max(jnp.where(earlier, first_all[None, :], 0), axis=1)

    cosine, sine, growth = xpos_tables(row_index - starts_of(row_index), HD)
    shrink = 1.0 / growth
    straight = jnp.concatenate([cosine * growth] * 2 + [cosine * shrink] * 2, axis=1)
    crossed = jnp.concatenate(
        [-sine * growth, sine * growth, -sine * shrink, sine * shrink], axis=1
    )
    team_rows = home * local_rows + jnp.arange(team * local_rows, dtype=jnp.int32)
    team_starts = starts_of(team_rows).reshape(team, local_rows)
    spans = jnp.stack([jnp.min(team_starts, axis=1), jnp.max(team_starts, axis=1)], axis=1)
    info = jnp.concatenate([jnp.stack([place, home]).astype(jnp.int32), spans.reshape(-1)])
    team_starts = team_starts.reshape(team, 1, local_rows)
    seat = jnp.reshape(place, (1,)).astype(jnp.int32)

    inputs_wide = inputs.astype(WIDE)
    input_normed, input_back = jax.vjp(
        norm_rows, inputs_wide, input_gain.astype(WIDE), input_bias.astype(WIDE)
    )
    attn_in = gather_rows(input_normed.astype(NARROW))
    rate = decay_rate[0]
    seq_part = model_width // seq_count
    offset = seq_rank * seq_part

    def average(old, weight, axis):
        piece = lax.dynamic_slice_in_dim(weight, offset, seq_part, axis).astype(WIDE)
        return rate * old + (1.0 - rate) * piece

    qkv_new = average(qkv_average, qkv_weight, 1)
    out_new = average(out_average, out_weight, 1)
    up_new = average(up_average, up_weight, 0)
    down_new = average(down_average, down_weight, 1)
    attn_in = after(attn_in, qkv_new, out_new, up_new, down_new)
    grad_rows = gather_rows(after(cotangent, attn_in))

    packs = pack_heads(
        seat, attn_in, qkv_weight, qkv_bias.astype(WIDE), straight, crossed, team
    )
    chunks = trade(packs)
    everyone = None
    if teams > 1:
        rings = [[j + team * t for t in range(teams)] for j in range(team)]
        natural = jnp.stack(chunks)[jnp.arange(team) ^ place]
        everyone = lax.all_gather(
            natural, "seq", axis=0, tiled=True, axis_index_groups=rings
        )
    *mixed_out, mixed_wide, logs = attend_forward(info, team_starts, chunks, everyone)
    mixed_got = trade(mixed_out)
    mixed_got[0] = after(mixed_got[0], grad_rows)
    mixed, mixed_sums = join_heads(seat, mixed_got)
    mixed_sums = tp_total(mixed_sums) / model_width
    mixed_center = mixed_sums[0][:, None]
    mixed_factor = lax.rsqrt(mixed_sums[1][:, None] - mixed_center * mixed_center + EPSILON)
    mixed_unit = (mixed.astype(WIDE) - mixed_center) * mixed_factor
    mixed_low = (mixed_unit * mixed_gain + mixed_bias).astype(NARROW)
    grad_hidden = jnp.einsum("rd,fd->rf", grad_rows, down_weight, preferred_element_type=WIDE)
    out_rows = scatter_rows(jnp.dot(mixed_low, out_weight, preferred_element_type=WIDE))
    out_rows = after(out_rows, grad_hidden)
    middle = inputs_wide + out_rows + out_bias.astype(WIDE)
    middle_normed, middle_back = jax.vjp(
        norm_rows, middle, middle_gain.astype(WIDE), middle_bias.astype(WIDE)
    )
    ffn_in = gather_rows(middle_normed.astype(NARROW))
    up_value = jnp.dot(ffn_in, up_weight, preferred_element_type=WIDE) + up_bias.astype(WIDE)
    activated, gelu_back = jax.vjp(exact_gelu, up_value)
    scaled = grad_hidden * hidden_gain.astype(WIDE)
    sums = jnp.stack(
        [
            jnp.sum(activated, axis=1),
            jnp.sum(activated * activated, axis=1),
            jnp.sum(scaled, axis=1),
            jnp.sum(scaled * activated, axis=1),
        ]
    )
    sums = tp_total(sums) / FF
    center = sums[0][:, None]
    factor = lax.rsqrt(sums[1][:, None] - center * center + EPSILON)
    lean = sums[2][:, None]
    cross = (sums[3][:, None] - center * lean) * factor
    unit = (activated - center) * factor
    hidden_low = (unit * hidden_gain + hidden_bias).astype(NARROW)
    grad_active = (scaled - lean - unit * cross) * factor
    grad_up = gelu_back(grad_active)[0].astype(NARROW)
    hiddengain_part = jnp.sum(grad_hidden * unit, axis=0)
    hiddenbias_part = jnp.sum(grad_hidden, axis=0)
    upbias_part = jnp.sum(grad_up, axis=0, dtype=WIDE)

    grad_ffn_in = scatter_rows(
        jnp.einsum("rf,df->rd", grad_up, up_weight, preferred_element_type=WIDE)
    )
    down_pieces = seq_gradient(hidden_low, grad_rows, seq_rank, seq_count, True)
    grad_ffn_in = after(grad_ffn_in, *down_pieces)
    grad_middle_norm, middlegain_part, middlebias_part = middle_back(grad_ffn_in)
    grad_middle = cotangent.astype(WIDE) + grad_middle_norm
    grad_middle_low = grad_middle.astype(NARROW)
    grad_mixed_rows = gather_rows(grad_middle_low)
    up_pieces = seq_gradient(grad_up[None], ffn_in, seq_rank, seq_count, False)
    down_grad = finish_gradient(down_pieces, seq_count, 0)
    grad_mixed_rows = after(grad_mixed_rows, down_grad, *up_pieces)
    outbias_part = jnp.sum(grad_middle_low, axis=0, dtype=WIDE)
    downbias_part = jnp.sum(cotangent, axis=0, dtype=WIDE)
    grad_mixed_norm = jnp.einsum(
        "rd,fd->rf", grad_mixed_rows, out_weight, preferred_element_type=WIDE
    )
    mixed_scaled = grad_mixed_norm * mixed_gain.astype(WIDE)
    back_sums = tp_total(
        jnp.stack([jnp.sum(mixed_scaled, axis=1), jnp.sum(mixed_scaled * mixed_unit, axis=1)])
    )
    back_sums = back_sums / model_width
    grad_mixed = (
        (mixed_scaled - back_sums[0][:, None] - mixed_unit * back_sums[1][:, None]) * mixed_factor
    ).astype(NARROW)
    mixedgain_part = jnp.sum(grad_mixed_norm * mixed_unit, axis=0)
    mixedbias_part = jnp.sum(grad_mixed_norm, axis=0)
    up_grad = finish_gradient(up_pieces, seq_count, 1)[0]
    out_pieces = seq_gradient(mixed_low, grad_mixed_rows, seq_rank, seq_count, True)

    def spread_norms(parts):
        tp_count = lax.axis_size("tp")
        both = jnp.stack(parts).reshape(len(parts), seq_count, tp_count, -1)
        mine = tp_scatter(both.transpose(2, 1, 0, 3))
        return mine.reshape(seq_count, -1)

    early = jnp.concatenate(
        [
            item.reshape(seq_count, -1)
            for item in (
                upbias_part,
                hiddengain_part,
                hiddenbias_part,
                mixedgain_part,
                mixedbias_part,
            )
        ]
        + [spread_norms([middlegain_part, middlebias_part, outbias_part, downbias_part])],
        axis=1,
    )
    early_sums = vector_scatter(early, seq_rank, seq_count)
    layer_out = (
        middle
        + scatter_rows(jnp.dot(hidden_low, down_weight, preferred_element_type=WIDE))
        + down_bias.astype(WIDE)
    ).astype(NARROW)

    grad_chunks = trade(cut_heads(seat, grad_mixed, team))
    pieces = attend_backward(
        info,
        team_starts,
        logs,
        mixed_wide,
        chunks,
        grad_chunks,
        everyone,
    )
    pieces = list(pieces)
    pieces[0] = after(pieces[0], up_grad, layer_out, early_sums, *out_pieces)
    out_grad = finish_gradient(out_pieces, seq_count, 0)
    if teams > 1:
        natural = lax.psum_scatter(
            pieces[0], "seq", scatter_dimension=0, tiled=True, axis_index_groups=rings
        )
        pieces = [
            lax.dynamic_index_in_dim(natural, place ^ m, 0, keepdims=False) for m in range(team)
        ]
    parts_got = trade(pieces)
    parts_got[0] = after(parts_got[0], out_grad)
    stacked, qkvbias_part = unpack_heads(seat, straight, crossed, parts_got)
    grad_attn_in = scatter_rows(
        jnp.einsum("crf,cdf->rd", stacked, qkv_weight, preferred_element_type=WIDE)
    )
    grad_input_norm, inputgain_part, inputbias_part = input_back(grad_attn_in)
    input_grad = (grad_middle + grad_input_norm).astype(NARROW)

    qkv_pieces = seq_gradient(stacked, attn_in, seq_rank, seq_count, False)
    qkv_grad = finish_gradient(qkv_pieces, seq_count, 1)
    late = jnp.concatenate(
        [
            qkvbias_part.reshape(3, seq_count, -1).transpose(1, 0, 2).reshape(seq_count, -1),
            spread_norms([inputgain_part, inputbias_part]),
        ],
        axis=1,
    )
    late_sums = vector_scatter(late, seq_rank, seq_count)
    narrow_part = local_width // seq_count
    wide_part = up_bias.shape[0] // seq_count
    norm_part = model_width // (seq_count * lax.axis_size("tp"))

    def cuts(vector, widths):
        begin = 0
        pieces = []
        for width in widths:
            pieces.append(vector[begin : begin + width])
            begin += width
        return pieces

    q_bias, k_bias, v_bias, inputgain_grad, inputbias_grad = cuts(
        late_sums, (narrow_part,) * 3 + (norm_part,) * 2
    )
    (
        upbias_grad,
        hiddengain_grad,
        hiddenbias_grad,
        mixedgain_grad,
        mixedbias_grad,
        middlegain_grad,
        middlebias_grad,
        outbias_grad,
        downbias_grad,
    ) = cuts(early_sums, (wide_part,) * 3 + (narrow_part,) * 2 + (norm_part,) * 4)
    return (
        layer_out,
        input_grad,
        qkv_grad,
        jnp.stack([q_bias, k_bias, v_bias]),
        out_grad,
        outbias_grad,
        up_grad,
        upbias_grad,
        down_grad,
        downbias_grad,
        inputgain_grad,
        inputbias_grad,
        mixedgain_grad,
        mixedbias_grad,
        middlegain_grad,
        middlebias_grad,
        hiddengain_grad,
        hiddenbias_grad,
        qkv_new,
        out_new,
        up_new,
        down_new,
    )


def solution(mesh):
    in_specs = (
        P(("seq", "tp"), None),
        P("seq"),
        P(("seq", "tp"), None),
        P(None, None, "tp"),
        P(None, "tp"),
        P("tp", None),
        P(),
        P(None, "tp"),
        P("tp"),
        P("tp", None),
        P(),
        P(),
        P(),
        P("tp"),
        P("tp"),
        P(),
        P(),
        P("tp"),
        P("tp"),
        P(None, "seq", "tp"),
        P("tp", "seq"),
        P("seq", "tp"),
        P("tp", "seq"),
        P(),
    )
    out_specs = (
        P(("seq", "tp"), None),
        P(("seq", "tp"), None),
        P(None, "seq", "tp"),
        P(None, ("tp", "seq")),
        P("tp", "seq"),
        P(("seq", "tp")),
        P("seq", "tp"),
        P(("tp", "seq")),
        P("tp", "seq"),
        P(("seq", "tp")),
        P(("seq", "tp")),
        P(("seq", "tp")),
        P(("tp", "seq")),
        P(("tp", "seq")),
        P(("seq", "tp")),
        P(("seq", "tp")),
        P(("tp", "seq")),
        P(("tp", "seq")),
        P(None, "seq", "tp"),
        P("tp", "seq"),
        P("seq", "tp"),
        P("tp", "seq"),
    )
    return jax.shard_map(shards, mesh=mesh, in_specs=in_specs, out_specs=out_specs, check_vma=False)
```

```python
import functools
import math

import jax
import jax.numpy as jnp
from jax import lax
from jax.experimental import pallas as pl
from jax.experimental.pallas import tpu as pltpu
from jax.sharding import PartitionSpec as P

FF = 8192
COUNT = 16
HD = 64

SCALE = 0.125
LOG2E = 1.4426950408889634
EPSILON = 1e-05
OUTSIDE = -2e30
LOWEST = -1e30
LARGEST = 1 << 30
WIDE = jnp.float32
NARROW = jnp.bfloat16
MIB = 1 << 20
SMALL = pl.CostEstimate(flops=1 << 20, bytes_accessed=1 << 16, transcendentals=0)


def xpos_tables(positions, head_size):
    half = head_size // 2
    index = jnp.arange(half, dtype=jnp.float32)
    frequency = jnp.exp(index * (-2.0 * math.log(10000.0) / head_size))
    zeta = (index * (2.0 / head_size) + 0.4) / 1.4
    places = positions.astype(jnp.float32)[:, None]
    angle = places * frequency[None, :]
    growth = jnp.exp(places * (jnp.log(zeta)[None, :] / 512.0))
    return (jnp.cos(angle), jnp.sin(angle), growth)


def norm_rows(values, gain, shift):
    center = jnp.mean(values, axis=-1, keepdims=True)
    spread = jnp.mean(values * values, axis=-1, keepdims=True) - center * center
    return (values - center) * lax.rsqrt(spread + EPSILON) * gain + shift


def exact_gelu(values):
    return jax.nn.gelu(values, approximate=False)


def gather_rows(values):
    return lax.all_gather(values, "tp", axis=0, tiled=True)


def ring_order(count):
    return [0] + list(range(1, count, 2)) + list(range(2, count, 2))[::-1]


def gather_parts(values):
    order = ring_order(lax.axis_size("tp"))
    parts = [values]
    for _ in order[1:]:
        pairs = [(a, b) for a, b in zip(order, order[1:] + order[:1])]
        parts.append(lax.ppermute(parts[-1], "tp", pairs))
    return parts


def part_owners():
    order = ring_order(lax.axis_size("tp"))
    count = len(order)
    spot = jnp.array([order.index(rank) for rank in range(count)], jnp.int32)[lax.axis_index("tp")]
    ranks = jnp.array(order, jnp.int32)
    return [ranks[(spot + count - slot) % count] for slot in range(count)]


def scatter_rows(values):
    return lax.psum_scatter(values.astype(NARROW), "tp", scatter_dimension=0, tiled=True).astype(WIDE)


def hop(values, axis, mask, count):
    return lax.ppermute(values, axis, [(i, i ^ mask) for i in range(count)])


def tp_total(values):
    count = lax.axis_size("tp")
    if count & (count - 1):
        return lax.psum(values, "tp")
    total = values
    for mask in range(1, count):
        total = total + hop(values, "tp", mask, count)
    return total


def after(value, *others):
    return lax.optimization_barrier((value,) + others)[0]


def vector_scatter(values, rank, count):
    bit = count // 2
    while bit:
        pair = values.reshape(2, bit, -1)
        mine = (rank & bit) // bit
        send = lax.dynamic_index_in_dim(pair, 1 - mine, 0, keepdims=False)
        keep = lax.dynamic_index_in_dim(pair, mine, 0, keepdims=False)
        values = keep + hop(send, "seq", bit, count)
        bit //= 2
    return values.reshape(-1)


def tp_scatter(values):
    count = lax.axis_size("tp")
    rank = lax.axis_index("tp")
    if count & (count - 1):
        return lax.psum_scatter(values, "tp", scatter_dimension=0)
    total = lax.dynamic_index_in_dim(values, rank, 0, keepdims=False)
    for mask in range(1, count):
        part = lax.dynamic_index_in_dim(values, rank ^ mask, 0, keepdims=False)
        total = total + hop(part, "tp", mask, count)
    return total


def sent_kernel(place, left, right, out, *, tall):
    if tall:
        out[0] = lax.dot_general(
            left[...], right[...], (((0,), (0,)), ((), ())), preferred_element_type=WIDE
        ).astype(NARROW)
    else:
        turned = right[...].T
        for c in range(left.shape[0]):
            out[0, c] = jnp.dot(turned, left[c], preferred_element_type=WIDE).astype(NARROW)


def kept_kernel(seat, left, right, got, *outs, tall, crossing):
    slots = pl.num_programs(0)
    step = pl.program_id(0)
    if tall:
        total = lax.dot_general(
            left[...], right[...], (((0,), (0,)), ((), ())), preferred_element_type=WIDE
        ) + got[0].astype(WIDE)
        rows = total.shape[0]
    else:
        turned = right[...].T
        total = jnp.stack(
            [
                jnp.dot(turned, left[c], preferred_element_type=WIDE) + got[0, c].astype(WIDE)
                for c in range(left.shape[0])
            ]
        )
        rows = total.shape[1]

    def at(slot):
        return pl.when(step == (slot - 1) % slots)

    @at(0)
    def _():
        outs[0][...] = total

    if crossing:
        cut = rows // 2
        low = total.astype(NARROW)
        first, second = (low[:cut], low[cut:]) if tall else (low[:, :cut], low[:, cut:])
        across, along, keep_first, keep_second = outs[1:]

        @at(1)
        def _():
            across[0] = first
            keep_second[...] = second

        @at(2)
        def _():
            keep_first[...] = first
            along[0] = second

        @at(3)
        def _():
            across[1] = first
            along[1] = second

    else:
        for slot in range(1, len(outs)):

            @at(slot)
            def _():
                outs[slot][...] = total.astype(NARROW)


def gradient_blocks(seat, left, right, count, tall, got=None, crossing=False):
    rows = right.shape[0]
    part = right.shape[1] // count
    slots = count // 2
    if tall:
        block = (left.shape[1], part)
        half = (left.shape[1] // 2, part)
    else:
        block = (left.shape[0], part, left.shape[2])
        half = (left.shape[0], part // 2, left.shape[2])
    first = 0 if got is None else 1
    slot_of = lambda k: (k + first) & (slots - 1)
    left_spec = pl.BlockSpec(left.shape, lambda k, seat: (0,) * left.ndim)
    if part % 128:
        order = 2 * (jnp.arange(slots, dtype=jnp.int32) ^ seat[0]) + seat[1]
        right = right.reshape(rows, count, part)[:, order].transpose(1, 0, 2)
        right_spec = pl.BlockSpec((None, rows, part), lambda k, seat: (slot_of(k), 0, 0))
    else:
        right_spec = pl.BlockSpec(
            (rows, part), lambda k, seat: (0, 2 * (slot_of(k) ^ seat[0]) + seat[1])
        )

    def fixed(shape):
        return pl.BlockSpec(shape, lambda k, seat: (0,) * len(shape))

    block_spec = pl.BlockSpec((1,) + block, lambda k, seat: (slot_of(k),) + (0,) * len(block))
    if got is None:
        shapes = [jax.ShapeDtypeStruct((slots,) + block, NARROW)]
        specs = [block_spec]
    else:
        rest = [(2,) + half, (2,) + half, half, half] if crossing else [block] * (slots - 1)
        shapes = [jax.ShapeDtypeStruct(block, WIDE)]
        shapes += [jax.ShapeDtypeStruct(shape, NARROW) for shape in rest]
        specs = [fixed(shape.shape) for shape in shapes]
    kernel = (
        functools.partial(sent_kernel, tall=tall)
        if got is None
        else functools.partial(kept_kernel, tall=tall, crossing=crossing)
    )
    return pl.pallas_call(
        kernel,
        name="sent" if got is None else "kept",
        grid_spec=pltpu.PrefetchScalarGridSpec(
            num_scalar_prefetch=1,
            grid=(slots,),
            in_specs=[left_spec, right_spec] + ([] if got is None else [block_spec]),
            out_specs=tuple(specs),
        ),
        out_shape=tuple(shapes),
        compiler_params=params(40),
        cost_estimate=SMALL,
    )(seat, left, right, *([] if got is None else [got]))


def send_gradient(left, right, rank, count, tall):
    seat = jnp.stack([rank >> 1, 1 - (rank & 1)])
    return gradient_blocks(seat, left, right, count, tall)[0]


def keep_gradient(left, right, got, rank, count, tall, crossing=False):
    seat = jnp.stack([rank >> 1, rank & 1])
    return gradient_blocks(
        seat, left, right, count, tall, got, crossing=crossing and count == 8
    )


def finish_gradient(pieces, count, arrived=None):
    total = pieces[0]
    if count == 8 and pieces[1].ndim > total.ndim:
        _, across, along, keep_first, keep_second = pieces
        axis = total.ndim - 2
        across = hop(across, "seq", 2, count)
        along = hop(along, "seq", 4, count)
        if arrived is not None:
            arrived += [across, along]
        first = (keep_first.astype(WIDE) + across[1].astype(WIDE)).astype(NARROW)
        second = (keep_second.astype(WIDE) + along[1].astype(WIDE)).astype(NARROW)
        first = hop(first, "seq", 4, count).astype(WIDE) + across[0].astype(WIDE)
        second = hop(second, "seq", 2, count).astype(WIDE) + along[0].astype(WIDE)
        return total + jnp.concatenate([first, second], axis=axis)
    for slot in range(1, len(pieces)):
        total = total + hop(pieces[slot], "seq", 2 * slot, count).astype(WIDE)
    return total


def scalar_spec():
    return pl.BlockSpec(memory_space=pltpu.SMEM)


def full_spec(array):
    return pl.BlockSpec(array.shape, lambda i: (0,) * len(array.shape))


def local_call(kernel, name, scalars, inputs, heavy, outs, scratch, mib):
    return pl.pallas_call(
        kernel,
        name=name,
        grid=(1,),
        out_shape=tuple(outs),
        in_specs=[scalar_spec()] * len(scalars)
        + [full_spec(item) for item in inputs]
        + [pl.BlockSpec(memory_space=pl.ANY)] * len(heavy),
        out_specs=tuple(full_spec(item) for item in outs),
        scratch_shapes=list(scratch),
        compiler_params=params(mib),
        cost_estimate=SMALL,
    )(*scalars, *inputs, *heavy)


def shaped(shape, dtype):
    return jax.ShapeDtypeStruct(tuple(shape), dtype)


SPAN = 256


def span_of(step):
    return pl.ds(pl.multiple_of(step * SPAN, SPAN), SPAN)


def fetch(source, held, sems, step, axis):
    where = (slice(None),) * axis + (span_of(step),)
    return pltpu.make_async_copy(source.at[where], held.at[where], sems.at[step])


def fetch_all(source, held, sems, axis):
    for step in range(source.shape[axis] // SPAN):
        fetch(source, held, sems, step, axis).start()


def params(mib):
    return pltpu.CompilerParams(vmem_limit_bytes=mib * MIB)


def turn_packed(values, straight, crossed):
    lane = lax.broadcasted_iota(jnp.int32, values.shape, 1)
    ahead = pltpu.roll(values, 2 * HD - HD // 2, 1)
    behind = pltpu.roll(values, HD // 2, 1)
    partner = jnp.where((lane & (HD // 2)) == 0, ahead, behind)
    return values * straight + partner * crossed


def rows_at(owner, rows):
    return pl.ds(pl.multiple_of(owner * rows, rows), rows)


def pack_kernel(seat, *refs, parts, heads, merge):
    rows_in = refs[:parts]
    bias, straight, crossed = refs[parts : parts + 3]
    at = parts + 3
    if merge:
        earlier, earlier_rows = refs[at : at + 2]
        at += 2
    weight = refs[at]
    at += 1
    if merge:
        outs, rows_out = refs[at : at + heads], refs[at + heads]
    else:
        out, rows_out = refs[at], refs[at + 1]
    rows, held, kept, sems = refs[-4:]
    fetch_all(weight, kept, sems, 2)
    part = rows_in[0].shape[0]
    half = part // 2
    size = part + half
    for i in range(parts):
        rows[i * part : (i + 1) * part, :] = rows_in[i][...]
    straight, crossed = (
        jnp.concatenate([table[rows_at(seat[1 + i], part), :] for i in range(parts)], axis=0)
        for table in (straight, crossed)
    )
    for step in range(weight.shape[2] // SPAN):
        fetch(weight, kept, sems, step, 2).wait()
        cols = slice(step * SPAN, (step + 1) * SPAN)
        query, key, value = (
            jnp.dot(rows[...], kept[c, :, cols], preferred_element_type=WIDE)
            + bias[c : c + 1, cols]
            for c in range(3)
        )
        for side in range(SPAN // HD):
            lanes = slice(side * HD, (side + 1) * HD)
            head = step * (SPAN // HD) + side
            both = jnp.concatenate([query[:, lanes], key[:, lanes]], axis=1)
            both = turn_packed(both, straight, crossed).astype(NARROW)
            for i in range(parts):
                held[i, head, :part, :] = both[i * part : (i + 1) * part]
                one = value[i * part : (i + 1) * part, lanes]
                held[i, head, part:, :] = jnp.concatenate(
                    [one[:half], one[half:]], axis=1
                ).astype(NARROW)
    if merge:
        for i in range(parts):
            mine = rows_at(seat[1 + i], size)
            other = rows_at(seat[1 + parts + i], size)
            for slot in range(heads):
                outs[slot][mine, :] = held[i, seat[0] ^ slot]
                outs[slot][other, :] = earlier[i, seat[0] ^ slot]
            rows_out[rows_at(seat[1 + i], part), :] = rows[i * part : (i + 1) * part, :]
            rows_out[rows_at(seat[1 + parts + i], part), :] = earlier_rows[
                i * part : (i + 1) * part, :
            ]
    else:
        out[...] = held[...]
        rows_out[...] = rows[...]


def pack_heads(seat, parts, weight, bias, straight, crossed, heads, earlier=()):
    count = len(parts)
    part, depth = parts[0].shape
    size = part + part // 2
    if earlier:
        outs = [shaped((2 * count * size, 2 * HD), NARROW)] * heads
        outs += [shaped((2 * count * part, depth), NARROW)]
    else:
        outs = [shaped((count, heads, size, 2 * HD), NARROW), shaped((count * part, depth), NARROW)]
    return local_call(
        functools.partial(pack_kernel, parts=count, heads=heads, merge=bool(earlier)),
        "pack",
        [seat],
        [*parts, bias, straight, crossed, *earlier],
        [weight],
        outs,
        [
            pltpu.VMEM((count * part, depth), NARROW),
            pltpu.VMEM((count, heads, size, 2 * HD), NARROW),
            pltpu.VMEM(weight.shape, NARROW),
            pltpu.SemaphoreType.DMA((weight.shape[2] // SPAN,)),
        ],
        48,
    )


def split_chunk(chunk):
    block = chunk.shape[0] * 2 // 3
    both = chunk[:block, :]
    packed = chunk[block:, :]
    value = jnp.concatenate([packed[:, :HD], packed[:, HD:]], axis=0)
    return both[:, :HD], both[:, HD:], value


def allowed_mask(begin, q_begin, starts, shape):
    keys = begin + lax.broadcasted_iota(jnp.int32, shape, 0)
    queries = q_begin + lax.broadcasted_iota(jnp.int32, shape, 1)
    return (keys >= starts) & (keys <= queries)


def key_ranges(info, index, first_block, block):
    here = first_block + index
    low = info[2 + 2 * index] // block
    clear = jnp.minimum((info[3 + 2 * index] + block - 1) // block, here)
    return low, clear, here


def forward_kernel(info, starts, *refs, groups, spread, parts):
    count = groups
    chunks = refs[:count]
    at = count + (1 if spread else 0)
    outs = refs[at : at + count]
    mixed, logs, keys, values, queries = refs[at + count :]
    me = info[0]
    first_block = info[1]
    block = starts.shape[2]
    part = block // parts
    size = part + part // 2
    for slot in range(parts * count):
        side = slot // count
        query, key, value = split_chunk(chunks[slot % count][side * size : (side + 1) * size, :])
        place = me ^ (slot % count)
        rows = slice(side * part, (side + 1) * part)
        queries[place, :, rows] = query.T
        if not spread:
            keys[place, rows, :] = key
            values[place, :, rows] = value.T
    if spread:

        @pl.loop(0, keys.shape[0])
        def _(kb):
            for side in range(parts):
                _, key, value = split_chunk(refs[count][kb, side * size : (side + 1) * size, :])
                rows = slice(side * part, (side + 1) * part)
                keys[kb, rows, :] = key
                values[kb, :, rows] = value.T

    @pl.loop(0, count)
    def _(index):
        low, clear, here = key_ranges(info, index, first_block, block)
        query = queries[index]
        begins = starts[index]

        def step(kb, carry, masked):
            top, total, accum = carry
            raw = jnp.dot(keys[kb], query, preferred_element_type=WIDE)
            if masked:
                raw = jnp.where(
                    allowed_mask(kb * block, here * block, begins, raw.shape), raw, OUTSIDE
                )
            fresh = jnp.maximum(top, jnp.max(raw, axis=0, keepdims=True) * (SCALE * LOG2E))
            kept = jnp.exp2(raw * (SCALE * LOG2E) - fresh)
            fade = jnp.exp2(top - fresh)
            total = total * fade + jnp.sum(kept, axis=0, keepdims=True)
            accum = accum * fade + jnp.dot(
                values[kb], kept.astype(NARROW), preferred_element_type=WIDE
            )
            return fresh, total, accum

        carry = (
            jnp.full((1, block), LOWEST, WIDE),
            jnp.zeros((1, block), WIDE),
            jnp.zeros((HD, block), WIDE),
        )
        carry = lax.fori_loop(low, clear, functools.partial(step, masked=True), carry)
        carry = lax.fori_loop(clear, here, functools.partial(step, masked=False), carry)
        top, total, accum = step(here, carry, True)
        mixed[index] = accum / total
        logs[index] = top + jnp.log2(total)

    for slot in range(count):
        outs[slot][...] = mixed[me ^ slot].astype(NARROW)


def attend_forward(info, starts, chunks, everyone, parts):
    count = len(chunks)
    block = starts.shape[2]
    spread = everyone is not None
    blocks = everyone.shape[0] if spread else count
    return local_call(
        functools.partial(forward_kernel, groups=count, spread=spread, parts=parts),
        "forward",
        [info],
        [starts, *chunks] + ([everyone] if spread else []),
        [],
        [shaped((HD, block), NARROW)] * count
        + [shaped((count, HD, block), WIDE), shaped((count, 1, block), WIDE)],
        [
            pltpu.VMEM((blocks, block, HD), NARROW),
            pltpu.VMEM((blocks, HD, block), NARROW),
            pltpu.VMEM((count, HD, block), NARROW),
        ],
        48,
    )


def backward_kernel(info, starts, logs, mixed, *refs, groups, spread, parts):
    count = groups
    chunks = refs[:count]
    grads = refs[count : 2 * count]
    at = 2 * count
    if spread:
        everyone = refs[at]
        at += 1
    outs = refs[at : at + (1 if spread else count)]
    at += len(outs)
    keys, keys_up, values, queries, queries_up, downs, downs_up, key_sum, value_sum, query_sum = refs[at:]
    me = info[0]
    first_block = info[1]
    block = starts.shape[2]
    blocks = keys.shape[0]
    part = block // parts
    half = block // 2
    size = part + part // 2
    for slot in range(parts * count):
        side = slot // count
        query, key, value = split_chunk(chunks[slot % count][side * size : (side + 1) * size, :])
        place = me ^ (slot % count)
        rows = slice(side * part, (side + 1) * part)
        queries[place, rows, :] = query
        queries_up[place, :, rows] = query.T
        if not spread:
            keys[place, rows, :] = key
            keys_up[place, :, rows] = key.T
            values[place, rows, :] = value
    for slot in range(count):
        down = grads[slot][...]
        downs_up[me ^ slot] = down
        downs[me ^ slot] = down.T
    if spread:

        @pl.loop(0, blocks)
        def _(kb):
            for side in range(parts):
                _, key, value = split_chunk(everyone[kb, side * size : (side + 1) * size, :])
                rows = slice(side * part, (side + 1) * part)
                keys[kb, rows, :] = key
                keys_up[kb, :, rows] = key.T
                values[kb, rows, :] = value

    key_sum[...] = jnp.zeros_like(key_sum)
    value_sum[...] = jnp.zeros_like(value_sum)

    @pl.loop(0, count)
    def _(index):
        low, clear, here = key_ranges(info, index, first_block, block)
        query_up = queries_up[index]
        down_up = downs_up[index]
        begins = starts[index]
        log = logs[index]
        delta = jnp.sum(down_up.astype(WIDE) * mixed[index], axis=0, keepdims=True)

        def step(kb, accum, masked):
            raw = jnp.dot(keys[kb], query_up, preferred_element_type=WIDE)
            probs = jnp.exp2(raw * (SCALE * LOG2E) - log)
            if masked:
                probs = jnp.where(
                    allowed_mask(kb * block, here * block, begins, raw.shape), probs, 0.0
                )
            grad_probs = jnp.dot(values[kb], down_up, preferred_element_type=WIDE)
            grad_scores = (probs * (grad_probs - delta)).astype(NARROW)
            value_sum[kb] += jnp.dot(
                probs.astype(NARROW), downs[index], preferred_element_type=WIDE
            )
            key_sum[kb] += jnp.dot(grad_scores, queries[index], preferred_element_type=WIDE)
            return accum + jnp.dot(keys_up[kb], grad_scores, preferred_element_type=WIDE)

        accum = jnp.zeros((HD, block), WIDE)
        accum = lax.fori_loop(low, clear, functools.partial(step, masked=True), accum)
        accum = lax.fori_loop(clear, here, functools.partial(step, masked=False), accum)
        query_sum[index] = step(here, accum, True)

    def packed(kb, query):
        both = jnp.concatenate([query, key_sum[kb]], axis=1) * SCALE
        one = value_sum[kb]
        return both.astype(NARROW), jnp.concatenate([one[:half], one[half:]], axis=1).astype(NARROW)

    if spread:

        @pl.loop(0, blocks)
        def _(kb):
            inside = (kb >= first_block) & (kb < first_block + count)
            query = query_sum[jnp.clip(kb - first_block, 0, count - 1)]
            both, value = packed(kb, jnp.where(inside, query, 0.0).T)
            outs[0][kb, :block, :] = both
            outs[0][kb, block:, :] = value

    else:
        for slot in range(count):
            place = me ^ slot
            both, value = packed(place, query_sum[place].T)
            outs[slot][:block, :] = both
            outs[slot][block:, :] = value


def attend_backward(info, starts, logs, mixed, chunks, grads, everyone, parts):
    count = len(chunks)
    block = starts.shape[2]
    spread = everyone is not None
    blocks = everyone.shape[0] if spread else count
    rows = block + block // 2
    outs = [shaped((blocks, rows, 2 * HD), NARROW)] if spread else [shaped((rows, 2 * HD), NARROW)] * count
    tall = (block, HD)
    flat = (HD, block)
    return local_call(
        functools.partial(backward_kernel, groups=count, spread=spread, parts=parts),
        "backward",
        [info],
        [starts, logs, mixed, *chunks, *grads] + ([everyone] if spread else []),
        [],
        outs,
        [
            pltpu.VMEM((blocks,) + tall, NARROW),
            pltpu.VMEM((blocks,) + flat, NARROW),
            pltpu.VMEM((blocks,) + tall, NARROW),
            pltpu.VMEM((count,) + tall, NARROW),
            pltpu.VMEM((count,) + flat, NARROW),
            pltpu.VMEM((count,) + tall, NARROW),
            pltpu.VMEM((count,) + flat, NARROW),
            pltpu.VMEM((blocks,) + tall, WIDE),
            pltpu.VMEM((blocks,) + tall, WIDE),
            pltpu.VMEM((count,) + flat, WIDE),
        ],
        60,
    )


def join_kernel(place, *refs):
    count = len(refs) - 3
    chunks, out, sums, held = refs[:count], refs[count], refs[count + 1], refs[count + 2]
    me = place[0]
    total = 0.0
    squares = 0.0
    for slot in range(count):
        held[me ^ slot] = chunks[slot][...]
        wide = chunks[slot][...].astype(WIDE)
        total = total + jnp.sum(wide, axis=0, keepdims=True)
        squares = squares + jnp.sum(wide * wide, axis=0, keepdims=True)
    sums[0:1, :] = total
    sums[1:2, :] = squares
    for pair in range(count // 2):
        both = jnp.concatenate([held[2 * pair], held[2 * pair + 1]], axis=0)
        out[:, pair * 2 * HD : (pair + 1) * 2 * HD] = both.T


def join_heads(place, chunks):
    count = len(chunks)
    block = chunks[0].shape[1]
    return local_call(
        join_kernel,
        "join",
        [place],
        chunks,
        [],
        [shaped((block, count * HD), NARROW), shaped((2, block), WIDE)],
        [pltpu.VMEM((count, HD, block), NARROW)],
        16,
    )


def unpack_kernel(place, straight, crossed, *refs):
    count = len(refs) - 3
    chunks, out, sums, held = refs[:count], refs[count], refs[count + 1], refs[count + 2]
    me = place[0]
    block = straight.shape[0]
    for slot in range(count):
        both = turn_packed(chunks[slot][:block, :].astype(WIDE), straight[...], -crossed[...])
        held[me ^ slot, :block, :] = both.astype(NARROW)
        held[me ^ slot, block:, :] = chunks[slot][block:, :]
    for pair in range(count // 2):
        parts = [split_chunk(held[2 * pair + side]) for side in range(2)]
        cols = slice(pair * 2 * HD, (pair + 1) * 2 * HD)
        for c in range(3):
            joined = jnp.concatenate([parts[0][c], parts[1][c]], axis=1)
            out[c, :, cols] = joined
            sums[c : c + 1, cols] = jnp.sum(joined.astype(WIDE), axis=0, keepdims=True)


def unpack_heads(place, straight, crossed, chunks):
    count = len(chunks)
    block = straight.shape[0]
    return local_call(
        unpack_kernel,
        "unpack",
        [place],
        [straight, crossed, *chunks],
        [],
        [shaped((3, block, count * HD), NARROW), shaped((3, count * HD), WIDE)],
        [pltpu.VMEM((count,) + chunks[0].shape, NARROW)],
        24,
    )


def mixed_out_kernel(mixed, gain, bias, *refs, width):
    sums, weight = refs[:-6], refs[-6]
    out, low, stats, kept, sems = refs[-5:]
    fetch_all(weight, kept, sems, 1)
    total = sums[0][...]
    for other in sums[1:]:
        total = total + other[...]
    center = total[0:1] / width
    spread = total[1:2] / width - center * center
    factor = lax.rsqrt(spread + EPSILON)
    stats[...] = jnp.concatenate([center, factor], axis=0)
    columns = jnp.concatenate([center, factor, total, total, total], axis=0).T
    unit = (mixed[...].astype(WIDE) - columns[:, 0:1]) * columns[:, 1:2]
    low[...] = (unit * gain[...] + bias[...]).astype(NARROW)
    for step in range(weight.shape[1] // SPAN):
        cols = slice(step * SPAN, (step + 1) * SPAN)
        fetch(weight, kept, sems, step, 1).wait()
        out[:, cols] = jnp.dot(low[...], kept[:, cols], preferred_element_type=WIDE).astype(NARROW)


def mixed_out_product(mixed, sums, gain, bias, weight):
    rows = mixed.shape[0]
    return local_call(
        functools.partial(mixed_out_kernel, width=weight.shape[1]),
        "mixed_out",
        [],
        [mixed, gain, bias, *sums],
        [weight],
        [shaped((rows, weight.shape[1]), NARROW), shaped(mixed.shape, NARROW), shaped((2, rows), WIDE)],
        [
            pltpu.VMEM(weight.shape, NARROW),
            pltpu.SemaphoreType.DMA((weight.shape[1] // SPAN,)),
        ],
        24,
    )


def fold_lanes(values):
    total = values[:, :128]
    for begin in range(128, values.shape[1], 128):
        total = total + values[:, begin : begin + 128]
    return total


def up_kernel(seat, *refs, parts, merge):
    rows_in = refs[:parts]
    bias, gain, grad = refs[parts : parts + 3]
    earlier = refs[parts + 3 : parts + 5] if merge else ()
    weight, active_out, slope_out, rows_out, stats, rows, sums, kept, sems = refs[-9:]
    fetch_all(weight, kept, sems, 1)
    part = rows_in[0].shape[0]
    own = [slice(i * part, (i + 1) * part) for i in range(parts)]
    for i in range(parts):
        rows[own[i], :] = rows_in[i][...]
    if merge:
        for i in range(parts):
            rows_out[rows_at(seat[i], part), :] = rows_in[i][...]
            rows_out[rows_at(seat[parts + i], part), :] = earlier[0][own[i], :]
    else:
        rows_out[...] = rows[...]
    sums[...] = jnp.zeros_like(sums)

    @pl.loop(0, weight.shape[1] // SPAN)
    def _(step):
        fetch(weight, kept, sems, step, 1).wait()
        cols = span_of(step)
        value = jnp.dot(rows[...], kept[:, cols], preferred_element_type=WIDE) + bias[:, cols]
        below = 0.5 + 0.5 * lax.erf(value * math.sqrt(0.5))
        active = value * below
        slope = below + value * (
            jnp.exp(-0.5 * value * value) * (1.0 / math.sqrt(2.0 * math.pi))
        )
        active_out[:, cols] = active.astype(NARROW)
        slope_out[:, cols] = slope.astype(NARROW)
        back = jnp.concatenate([grad[rows_at(seat[i], part), cols] for i in range(parts)], axis=0)
        scaled = back.astype(WIDE) * gain[:, cols]
        sums[0] += fold_lanes(active)
        sums[1] += fold_lanes(active * active)
        sums[2] += fold_lanes(scaled)
        sums[3] += fold_lanes(scaled * active)

    lines = jnp.concatenate([jnp.sum(sums[i].T, axis=0, keepdims=True) for i in range(4)], axis=0)
    if merge:
        for i in range(parts):
            stats[:, rows_at(seat[i], part)] = lines[:, own[i]]
            stats[:, rows_at(seat[parts + i], part)] = earlier[1][:, own[i]]
    else:
        stats[...] = lines


def up_product(seat, parts, weight, bias, gain, grad, earlier=()):
    count = len(parts)
    rows = count * parts[0].shape[0]
    depth, width = weight.shape
    both = rows * (2 if earlier else 1)
    return local_call(
        functools.partial(up_kernel, parts=count, merge=bool(earlier)),
        "up",
        [seat],
        [*parts, bias, gain, grad, *earlier],
        [weight],
        [
            shaped((rows, width), NARROW),
            shaped((rows, width), NARROW),
            shaped((both, depth), NARROW),
            shaped((4, both), WIDE),
        ],
        [
            pltpu.VMEM((rows, depth), NARROW),
            pltpu.VMEM((4, rows, 128), WIDE),
            pltpu.VMEM(weight.shape, NARROW),
            pltpu.SemaphoreType.DMA((width // SPAN,)),
        ],
        48,
    )


def ffn_back_kernel(seat, *refs, count, parts, width):
    sums = refs[:count]
    halves = refs[count : count + 2], refs[count + 2 : count + 4]
    grad, gain, shift, weight = refs[count + 4 : count + 8]
    hidden_out, grad_out, product, lines, columns, total, kept, sems = refs[count + 8 :]
    fetch_all(weight, kept, sems, 1)
    part = grad.shape[0] // parts
    whole = sums[0][...]
    for other in sums[1:]:
        whole = whole + other[...]
    whole = whole / width
    center, square, lean, cross = (whole[i : i + 1] for i in range(4))
    factor = lax.rsqrt(square - center * center + EPSILON)
    cross = (cross - center * lean) * factor
    columns[...] = jnp.concatenate([center, factor, lean, cross, whole], axis=0).T
    total[...] = jnp.zeros_like(total)

    @pl.loop(0, weight.shape[1] // SPAN)
    def _(step):
        cols = span_of(step)
        line = [0.0, 0.0, 0.0]
        grads = []
        for i in range(parts):
            active, slope = halves[i // (parts // 2)]
            own = i % (parts // 2)
            own = slice(own * part, (own + 1) * part)
            rows = rows_at(seat[i], part)
            center, factor, lean, cross = (columns[rows, k : k + 1] for k in range(4))
            unit = (active[own, cols].astype(WIDE) - center) * factor
            hidden_out[rows, cols] = (unit * gain[:, cols] + shift[:, cols]).astype(NARROW)
            back = grad[rows, cols].astype(WIDE)
            grad_active = (back * gain[:, cols] - lean - unit * cross) * factor
            grad_up = (grad_active * slope[own, cols].astype(WIDE)).astype(NARROW)
            grad_out[rows, cols] = grad_up
            grads.append(grad_up)
            line[0] = line[0] + jnp.sum(grad_up.astype(WIDE), axis=0, keepdims=True)
            line[1] = line[1] + jnp.sum(back * unit, axis=0, keepdims=True)
            line[2] = line[2] + jnp.sum(back, axis=0, keepdims=True)
        lines[:, cols] = jnp.concatenate(line, axis=0)
        fetch(weight, kept, sems, step, 1).wait()
        total[...] += lax.dot_general(
            jnp.concatenate(grads, axis=0),
            kept[:, cols],
            (((1,), (1,)), ((), ())),
            preferred_element_type=WIDE,
        )

    for i in range(parts):
        product[rows_at(seat[i], part), :] = total[i * part : (i + 1) * part, :].astype(NARROW)


def ffn_back_product(seat, sums, near, far, grad, gain, shift, weight, width):
    rows, local = grad.shape
    depth = weight.shape[0]
    both = shaped((rows, local), NARROW)
    return local_call(
        functools.partial(
            ffn_back_kernel, count=len(sums), parts=seat.shape[0], width=width
        ),
        "ffn_back",
        [seat],
        [*sums, *near, *far, grad, gain, shift],
        [weight],
        [both, both, shaped((rows, depth), NARROW), shaped((3, local), WIDE)],
        [
            pltpu.VMEM((rows, 8), WIDE),
            pltpu.VMEM((rows, depth), WIDE),
            pltpu.VMEM(weight.shape, NARROW),
            pltpu.SemaphoreType.DMA((local // SPAN,)),
        ],
        56,
    )


def mixed_back_kernel(seat, *refs, parts):
    mixed, stats, gain, weight, grad, rows, sums, lines, kept, sem = refs[parts:]
    copy = pltpu.make_async_copy(weight, kept, sem)
    copy.start()
    part = refs[0].shape[0]
    for i in range(parts):
        rows[rows_at(seat[i], part), :] = refs[i][...]
    columns = jnp.concatenate([stats[...]] * 4, axis=0).T
    unit = (mixed[...].astype(WIDE) - columns[:, 0:1]) * columns[:, 1:2]
    copy.wait()
    back = lax.dot_general(
        rows[...], kept[...], (((1,), (1,)), ((), ())), preferred_element_type=WIDE
    )
    grad[...] = back
    lines[0:1, :] = jnp.sum(back * unit, axis=0, keepdims=True)
    lines[1:2, :] = jnp.sum(back, axis=0, keepdims=True)
    scaled = back * gain[...]
    sums[0:1, :] = jnp.sum(fold_lanes(scaled).T, axis=0, keepdims=True)
    sums[1:2, :] = jnp.sum(fold_lanes(scaled * unit).T, axis=0, keepdims=True)


def mixed_back_product(seat, parts, mixed, stats, gain, weight):
    rows, local = mixed.shape
    return local_call(
        functools.partial(mixed_back_kernel, parts=len(parts)),
        "mixed_back",
        [seat],
        [*parts, mixed, stats, gain],
        [weight],
        [
            shaped((rows, local), WIDE),
            shaped((rows, weight.shape[1]), NARROW),
            shaped((2, rows), WIDE),
            shaped((2, local), WIDE),
        ],
        [pltpu.VMEM(weight.shape, NARROW), pltpu.SemaphoreType.DMA],
        24,
    )


def cut_kernel(seat, grad, mixed, stats, gain, *refs, count, width):
    sums = refs[:count]
    outs, held = refs[count:-1], refs[-1]
    total = sums[0][...]
    for other in sums[1:]:
        total = total + other[...]
    total = total / width
    columns = jnp.concatenate([stats[...], total] * 2, axis=0).T
    factor = columns[:, 1:2]
    unit = (mixed[...].astype(WIDE) - columns[:, 0:1]) * factor
    result = (grad[...] * gain[...] - columns[:, 2:3] - unit * columns[:, 3:4]) * factor
    result = result.astype(NARROW)
    heads = len(outs)
    for pair in range(heads // 2):
        both = result[:, pair * 2 * HD : (pair + 1) * 2 * HD].T
        held[2 * pair] = both[:HD]
        held[2 * pair + 1] = both[HD:]
    for slot in range(heads):
        outs[slot][...] = held[seat[0] ^ slot]


def cut_heads(seat, grad, mixed, stats, gain, sums, heads, width):
    block = grad.shape[0]
    return local_call(
        functools.partial(cut_kernel, count=len(sums), width=width),
        "cut",
        [seat],
        [grad, mixed, stats, gain, *sums],
        [],
        [shaped((HD, block), NARROW)] * heads,
        [pltpu.VMEM((heads, HD, block), NARROW)],
        16,
    )


def attn_back_kernel(grads, rows, gain, bias, weight, product, lines, kept, sems):
    fetch_all(weight, kept, sems, 1)

    @pl.loop(0, product.shape[1] // SPAN)
    def _(step):
        cols = span_of(step)
        fetch(weight, kept, sems, step, 1).wait()
        total = 0.0
        for c in range(grads.shape[0]):
            total = total + lax.dot_general(
                grads[c], kept[c, cols, :], (((1,), (1,)), ((), ())), preferred_element_type=WIDE
            )
        product[:, cols] = total.astype(NARROW)
        unit = (rows[:, cols].astype(WIDE) - bias[:, cols]) / gain[:, cols]
        lines[0:1, cols] = jnp.sum(total * unit, axis=0, keepdims=True)
        lines[1:2, cols] = jnp.sum(total, axis=0, keepdims=True)


def attn_back_product(grads, rows, gain, bias, weight):
    count, depth = rows.shape
    return local_call(
        attn_back_kernel,
        "attn_back",
        [],
        [grads, rows, gain, bias],
        [weight],
        [shaped((count, depth), NARROW), shaped((2, depth), WIDE)],
        [
            pltpu.VMEM(weight.shape, NARROW),
            pltpu.SemaphoreType.DMA((depth // SPAN,)),
        ],
        32,
    )


def shards(
    inputs,
    segment_ids,
    cotangent,
    qkv_weight,
    qkv_bias,
    out_weight,
    out_bias,
    up_weight,
    up_bias,
    down_weight,
    down_bias,
    input_gain,
    input_bias,
    mixed_gain,
    mixed_bias,
    middle_gain,
    middle_bias,
    hidden_gain,
    hidden_bias,
    qkv_average,
    out_average,
    up_average,
    down_average,
    decay_rate,
):
    seq_count = lax.axis_size("seq")
    seq_rank = lax.axis_index("seq")
    local_rows = segment_ids.shape[0]
    model_width = inputs.shape[1]
    local_width = qkv_weight.shape[2]
    heads_here = local_width // HD
    team = heads_here
    teams = seq_count // team
    place = seq_rank % team
    home = seq_rank - place

    def trade(chunks):
        return [chunks[0]] + [hop(chunks[m], "seq", m, seq_count) for m in range(1, team)]

    row_index = seq_rank * local_rows + jnp.arange(local_rows, dtype=jnp.int32)
    documents = jnp.arange(COUNT, dtype=jnp.int32)
    member = segment_ids[:, None] == documents[None, :]
    first_all = jnp.min(jnp.where(member, row_index[:, None], LARGEST), axis=0)
    bit = 1
    while bit < seq_count:
        first_all = jnp.minimum(first_all, hop(first_all, "seq", bit, seq_count))
        bit *= 2

    def starts_of(rows):
        earlier = first_all[None, :] <= rows[:, None]
        return jnp.max(jnp.where(earlier, first_all[None, :], 0), axis=1)

    cosine, sine, growth = xpos_tables(row_index - starts_of(row_index), HD)
    shrink = 1.0 / growth
    straight = jnp.concatenate([cosine * growth] * 2 + [cosine * shrink] * 2, axis=1)
    crossed = jnp.concatenate(
        [-sine * growth, sine * growth, -sine * shrink, sine * shrink], axis=1
    )
    team_rows = home * local_rows + jnp.arange(team * local_rows, dtype=jnp.int32)
    team_starts = starts_of(team_rows).reshape(team, local_rows)
    spans = jnp.stack([jnp.min(team_starts, axis=1), jnp.max(team_starts, axis=1)], axis=1)
    info = jnp.concatenate(
        [jnp.stack([place, home]).astype(jnp.int32), spans.reshape(-1)]
    )
    team_starts = team_starts.reshape(team, 1, local_rows)
    seat = jnp.reshape(place, (1,)).astype(jnp.int32)

    tp_count = lax.axis_size("tp")
    tp_rank = lax.axis_index("tp")
    inner = tp_count // 2
    owners = part_owners()
    near_first = owners[:inner] + owners[inner:]
    far_first = owners[inner:] + owners[:inner]

    def line(vector):
        return vector.astype(WIDE).reshape(1, -1)

    def exchange(values):
        mask = 1
        while 2 * mask < tp_count:
            values = values + hop(values, "tp", mask, tp_count)
            mask *= 2
        return [values, hop(values, "tp", mask, tp_count)]

    inputs_wide = inputs.astype(WIDE)
    input_normed, input_back = jax.vjp(
        norm_rows, inputs_wide, input_gain.astype(WIDE), input_bias.astype(WIDE)
    )
    attn_parts = gather_parts(input_normed.astype(NARROW))
    rate = decay_rate[0]
    seq_part = model_width // seq_count
    offset = seq_rank * seq_part

    def average(old, weight, axis):
        piece = lax.dynamic_slice_in_dim(weight, offset, seq_part, axis).astype(WIDE)
        return rate * old + (1.0 - rate) * piece

    qkv_new = average(qkv_average, qkv_weight, 1)
    out_new = average(out_average, out_weight, 1)
    up_new = average(up_average, up_weight, 0)
    down_new = average(down_average, down_weight, 1)
    attn_parts[0] = after(attn_parts[0], straight, crossed)

    def pack(parts, chairs, earlier=()):
        chair = jnp.stack([place.astype(jnp.int32)] + chairs)
        return pack_heads(
            chair, parts, qkv_weight, qkv_bias.astype(WIDE), straight, crossed, team, earlier
        )

    packed = pack(attn_parts[:inner], near_first)
    attn_parts[inner] = after(attn_parts[inner], *packed)
    *packs, attn_in = pack(attn_parts[inner:], far_first, packed)
    grad_rows = gather_rows(after(cotangent, packs[0]))
    chunks = trade(packs)
    everyone = None
    if teams > 1:
        rings = [[j + team * t for t in range(teams)] for j in range(team)]
        natural = jnp.stack(chunks)[jnp.arange(team) ^ place]
        everyone = lax.all_gather(
            natural, "seq", axis=0, tiled=True, axis_index_groups=rings
        )
    *mixed_out, mixed_wide, logs = attend_forward(info, team_starts, chunks, everyone, tp_count)
    mixed_got = trade(mixed_out)

    mixed_got[0] = after(mixed_got[0], grad_rows)
    mixed, mixed_sums = join_heads(seat, mixed_got)
    out_product, mixed_low, mixed_stats = mixed_out_product(
        mixed, exchange(mixed_sums), line(mixed_gain), line(mixed_bias), out_weight
    )
    grad_hidden = jnp.einsum(
        "rd,fd->rf", grad_rows, down_weight, preferred_element_type=WIDE
    ).astype(NARROW)
    summed = after(scatter_rows(out_product), grad_hidden, qkv_new, out_new, up_new, down_new)
    middle = inputs_wide + summed + out_bias.astype(WIDE)
    normed, middle_back = jax.vjp(
        norm_rows, middle, middle_gain.astype(WIDE), middle_bias.astype(WIDE)
    )
    ffn_parts = gather_parts(normed.astype(NARROW))
    gain_line = line(hidden_gain)

    def up(parts, chairs, earlier=()):
        return up_product(
            jnp.stack(chairs), parts, up_weight, line(up_bias), gain_line, grad_hidden, earlier
        )

    *up_near, ffn_near, sums_near = up(ffn_parts[:inner], near_first)
    ffn_parts[inner] = after(ffn_parts[inner], sums_near)
    *up_far, ffn_in, sums = up(ffn_parts[inner:], far_first, (ffn_near, sums_near))
    hidden_low, grad_up, ffn_back, hidden_lines = ffn_back_product(
        jnp.stack(owners),
        exchange(sums),
        up_near,
        up_far,
        grad_hidden,
        gain_line,
        line(hidden_bias),
        up_weight,
        FF,
    )
    upbias_part, hiddengain_part, hiddenbias_part = hidden_lines
    down_product = jnp.dot(hidden_low, down_weight, preferred_element_type=WIDE).astype(NARROW)
    late_rows = after(grad_rows, down_product)
    down_sent = send_gradient(hidden_low, late_rows, seq_rank, seq_count, True)
    up_sent = send_gradient(after(grad_up, down_product)[None], ffn_in, seq_rank, seq_count, False)
    summed = after(scatter_rows(ffn_back), down_sent, up_sent)
    norm_grad, middlegain_part, middlebias_part = middle_back(summed)
    grad_middle = cotangent.astype(WIDE) + norm_grad
    grad_low = grad_middle.astype(NARROW)
    middle_parts = gather_parts(grad_low)
    down_got = after(hop(down_sent, "seq", 1, seq_count), grad_low)
    up_got = hop(up_sent, "seq", 1, seq_count)
    down_pieces = keep_gradient(hidden_low, grad_rows, down_got, seq_rank, seq_count, True, True)
    up_pieces = keep_gradient(grad_up[None], ffn_in, up_got, seq_rank, seq_count, False)
    arrived = []
    down_grad = finish_gradient(down_pieces, seq_count, arrived)
    middle_parts[-1] = after(middle_parts[-1], *up_pieces, *arrived)
    outbias_part = jnp.sum(grad_low, axis=0, dtype=WIDE)
    downbias_part = jnp.sum(cotangent, axis=0, dtype=WIDE)
    grad_mixed_norm, grad_mixed_rows, back_sums, mixed_lines = mixed_back_product(
        jnp.stack(owners),
        middle_parts,
        mixed,
        mixed_stats,
        line(mixed_gain),
        out_weight,
    )
    mixedgain_part, mixedbias_part = mixed_lines
    grad_cuts = cut_heads(
        seat,
        grad_mixed_norm,
        mixed,
        mixed_stats,
        line(mixed_gain),
        exchange(back_sums),
        team,
        model_width,
    )
    grad_cuts = list(grad_cuts)
    grad_cuts[0] = after(grad_cuts[0], down_grad)
    grad_chunks = trade(grad_cuts)
    up_pieces = list(up_pieces)
    for slot in range(1, len(up_pieces)):
        up_pieces[slot] = after(up_pieces[slot], *grad_chunks)
    up_grad = finish_gradient(up_pieces, seq_count)[0]
    layer_out = (
        middle
        + scatter_rows(after(down_product, grad_mixed_norm))
        + down_bias.astype(WIDE)
    ).astype(NARROW)
    out_sent = send_gradient(mixed_low, grad_mixed_rows, seq_rank, seq_count, True)
    out_got = hop(out_sent, "seq", 1, seq_count)
    out_pieces = keep_gradient(mixed_low, grad_mixed_rows, out_got, seq_rank, seq_count, True)
    grad_chunks[0] = after(grad_chunks[0], *out_pieces)
    pieces = attend_backward(
        info,
        team_starts,
        logs,
        mixed_wide,
        chunks,
        grad_chunks,
        everyone,
        tp_count,
    )
    pieces = list(pieces)
    pieces[0] = after(pieces[0], layer_out, up_grad)
    if teams > 1:
        natural = lax.psum_scatter(
            pieces[0], "seq", scatter_dimension=0, tiled=True, axis_index_groups=rings
        )
        pieces = [
            lax.dynamic_index_in_dim(natural, place ^ m, 0, keepdims=False) for m in range(team)
        ]
    parts_got = trade(pieces)
    out_pieces = list(out_pieces)
    for slot in range(1, len(out_pieces)):
        out_pieces[slot] = after(out_pieces[slot], *parts_got)
    out_grad = finish_gradient(out_pieces, seq_count)
    stacked, qkvbias_part = unpack_heads(seat, straight, crossed, parts_got)
    qkv_got = hop(send_gradient(stacked, attn_in, seq_rank, seq_count, False), "seq", 1, seq_count)
    attn_back, attn_lines = attn_back_product(
        stacked, attn_in, line(input_gain), line(input_bias), qkv_weight
    )
    inputgain_part, inputbias_part = attn_lines
    grad_attn_in = scatter_rows(attn_back)
    qkv_pieces = keep_gradient(stacked, attn_in, qkv_got, seq_rank, seq_count, False, True)
    arrived = []
    qkv_grad = finish_gradient(qkv_pieces, seq_count, arrived)

    def spread_norms(parts):
        both = jnp.stack(parts).reshape(len(parts), seq_count, tp_count, -1)
        mine = tp_scatter(both.transpose(2, 1, 0, 3))
        return mine.reshape(seq_count, -1)

    vectors = jnp.concatenate(
        [
            item.reshape(seq_count, -1)
            for item in (
                upbias_part,
                hiddengain_part,
                hiddenbias_part,
                mixedgain_part,
                mixedbias_part,
                qkvbias_part[0],
                qkvbias_part[1],
                qkvbias_part[2],
            )
        ]
        + [
            spread_norms(
                [
                    middlegain_part,
                    middlebias_part,
                    outbias_part,
                    downbias_part,
                    inputgain_part,
                    inputbias_part,
                ]
            )
        ],
        axis=1,
    )
    vector_sums = vector_scatter(after(vectors, *arrived), seq_rank, seq_count)
    grad_attn_in = after(grad_attn_in, vector_sums)
    grad_input_norm, _, _ = input_back(grad_attn_in)
    input_grad = (grad_middle + grad_input_norm).astype(NARROW)
    narrow_part = local_width // seq_count
    wide_part = up_bias.shape[0] // seq_count
    norm_part = model_width // (seq_count * lax.axis_size("tp"))

    def cuts(vector, widths):
        begin = 0
        pieces = []
        for width in widths:
            pieces.append(vector[begin : begin + width])
            begin += width
        return pieces

    (
        upbias_grad,
        hiddengain_grad,
        hiddenbias_grad,
        mixedgain_grad,
        mixedbias_grad,
        q_bias,
        k_bias,
        v_bias,
        middlegain_grad,
        middlebias_grad,
        outbias_grad,
        downbias_grad,
        inputgain_grad,
        inputbias_grad,
    ) = cuts(vector_sums, (wide_part,) * 3 + (narrow_part,) * 5 + (norm_part,) * 6)
    return (
        layer_out,
        input_grad,
        qkv_grad,
        jnp.stack([q_bias, k_bias, v_bias]),
        out_grad,
        outbias_grad,
        up_grad,
        upbias_grad,
        down_grad,
        downbias_grad,
        inputgain_grad,
        inputbias_grad,
        mixedgain_grad,
        mixedbias_grad,
        middlegain_grad,
        middlebias_grad,
        hiddengain_grad,
        hiddenbias_grad,
        qkv_new,
        out_new,
        up_new,
        down_new,
    )


def solution(mesh):
    in_specs = (
        P(("seq", "tp"), None),
        P("seq"),
        P(("seq", "tp"), None),
        P(None, None, "tp"),
        P(None, "tp"),
        P("tp", None),
        P(),
        P(None, "tp"),
        P("tp"),
        P("tp", None),
        P(),
        P(),
        P(),
        P("tp"),
        P("tp"),
        P(),
        P(),
        P("tp"),
        P("tp"),
        P(None, "seq", "tp"),
        P("tp", "seq"),
        P("seq", "tp"),
        P("tp", "seq"),
        P(),
    )
    out_specs = (
        P(("seq", "tp"), None),
        P(("seq", "tp"), None),
        P(None, "seq", "tp"),
        P(None, ("tp", "seq")),
        P("tp", "seq"),
        P(("seq", "tp")),
        P("seq", "tp"),
        P(("tp", "seq")),
        P("tp", "seq"),
        P(("seq", "tp")),
        P(("seq", "tp")),
        P(("seq", "tp")),
        P(("tp", "seq")),
        P(("tp", "seq")),
        P(("seq", "tp")),
        P(("seq", "tp")),
        P(("tp", "seq")),
        P(("tp", "seq")),
        P(None, "seq", "tp"),
        P("tp", "seq"),
        P("seq", "tp"),
        P("tp", "seq"),
    )
    return jax.shard_map(shards, mesh=mesh, in_specs=in_specs, out_specs=out_specs, check_vma=False)
```

```python
import functools
import math

import jax
import jax.numpy as jnp
from jax import lax
from jax.experimental import pallas as pl
from jax.experimental.pallas import tpu as pltpu
from jax.sharding import PartitionSpec as P

FF = 8192
COUNT = 16
HD = 64

SCALE = 0.125
LOG2E = 1.4426950408889634
EPSILON = 1e-05
OUTSIDE = -2e30
LOWEST = -1e30
LARGEST = 1 << 30
WIDE = jnp.float32
NARROW = jnp.bfloat16
MIB = 1 << 20
SMALL = pl.CostEstimate(flops=1 << 20, bytes_accessed=1 << 16, transcendentals=0)


def xpos_tables(positions, head_size):
    half = head_size // 2
    index = jnp.arange(half, dtype=jnp.float32)
    frequency = jnp.exp(index * (-2.0 * math.log(10000.0) / head_size))
    zeta = (index * (2.0 / head_size) + 0.4) / 1.4
    places = positions.astype(jnp.float32)[:, None]
    angle = places * frequency[None, :]
    growth = jnp.exp(places * (jnp.log(zeta)[None, :] / 512.0))
    return (jnp.cos(angle), jnp.sin(angle), growth)


def norm_rows(values, gain, shift):
    center = jnp.mean(values, axis=-1, keepdims=True)
    spread = jnp.mean(values * values, axis=-1, keepdims=True) - center * center
    return (values - center) * lax.rsqrt(spread + EPSILON) * gain + shift


def exact_gelu(values):
    return jax.nn.gelu(values, approximate=False)


def gather_rows(values):
    return lax.all_gather(values, "tp", axis=0, tiled=True)


def ring_order(count):
    return [0] + list(range(1, count, 2)) + list(range(2, count, 2))[::-1]


def gather_parts(values):
    order = ring_order(lax.axis_size("tp"))
    parts = [values]
    for _ in order[1:]:
        pairs = [(a, b) for a, b in zip(order, order[1:] + order[:1])]
        parts.append(lax.ppermute(parts[-1], "tp", pairs))
    return parts


def part_owners(first):
    order = ring_order(lax.axis_size("tp"))
    count = len(order)
    rows = [
        [order[(order.index(rank) - first - slot) % count] for slot in range(count)]
        for rank in range(count)
    ]
    table = jnp.array(rows, jnp.int32)
    return lax.dynamic_index_in_dim(table, lax.axis_index("tp"), 0, keepdims=False)


def scatter_rows(values):
    return lax.psum_scatter(values.astype(NARROW), "tp", scatter_dimension=0, tiled=True).astype(WIDE)


def hop(values, axis, mask, count):
    return lax.ppermute(values, axis, [(i, i ^ mask) for i in range(count)])


def tp_total(values):
    count = lax.axis_size("tp")
    if count & (count - 1):
        return lax.psum(values, "tp")
    total = values
    for mask in range(1, count):
        total = total + hop(values, "tp", mask, count)
    return total


def after(value, *others):
    return lax.optimization_barrier((value,) + others)[0]


def vector_scatter(values, rank, count):
    bit = count // 2
    while bit:
        pair = values.reshape(2, bit, -1)
        mine = (rank & bit) // bit
        send = lax.dynamic_index_in_dim(pair, 1 - mine, 0, keepdims=False)
        keep = lax.dynamic_index_in_dim(pair, mine, 0, keepdims=False)
        values = keep + hop(send, "seq", bit, count)
        bit //= 2
    return values.reshape(-1)


def tp_scatter(values):
    count = lax.axis_size("tp")
    rank = lax.axis_index("tp")
    if count & (count - 1):
        return lax.psum_scatter(values, "tp", scatter_dimension=0)
    total = lax.dynamic_index_in_dim(values, rank, 0, keepdims=False)
    for mask in range(1, count):
        part = lax.dynamic_index_in_dim(values, rank ^ mask, 0, keepdims=False)
        total = total + hop(part, "tp", mask, count)
    return total


def sent_kernel(place, left, right, out, *, tall):
    if tall:
        out[0] = lax.dot_general(
            left[...], right[...], (((0,), (0,)), ((), ())), preferred_element_type=WIDE
        ).astype(NARROW)
    else:
        turned = right[...].T
        for c in range(left.shape[0]):
            out[0, c] = jnp.dot(turned, left[c], preferred_element_type=WIDE).astype(NARROW)


def kept_kernel(seat, left, right, got, *outs, tall, crossing):
    slots = pl.num_programs(0)
    step = pl.program_id(0)
    if tall:
        total = lax.dot_general(
            left[...], right[...], (((0,), (0,)), ((), ())), preferred_element_type=WIDE
        ) + got[0].astype(WIDE)
        rows = total.shape[0]
    else:
        turned = right[...].T
        total = jnp.stack(
            [
                jnp.dot(turned, left[c], preferred_element_type=WIDE) + got[0, c].astype(WIDE)
                for c in range(left.shape[0])
            ]
        )
        rows = total.shape[1]

    def at(slot):
        return pl.when(step == (slot - 1) % slots)

    @at(0)
    def _():
        outs[0][...] = total

    if crossing:
        cut = rows // 2
        low = total.astype(NARROW)
        first, second = (low[:cut], low[cut:]) if tall else (low[:, :cut], low[:, cut:])
        across, along, keep_first, keep_second = outs[1:]

        @at(1)
        def _():
            across[0] = first
            keep_second[...] = second

        @at(2)
        def _():
            keep_first[...] = first
            along[0] = second

        @at(3)
        def _():
            across[1] = first
            along[1] = second

    else:
        for slot in range(1, len(outs)):

            @at(slot)
            def _():
                outs[slot][...] = total.astype(NARROW)


def gradient_blocks(seat, left, right, count, tall, got=None, crossing=False):
    rows = right.shape[0]
    part = right.shape[1] // count
    slots = count // 2
    if tall:
        block = (left.shape[1], part)
        half = (left.shape[1] // 2, part)
    else:
        block = (left.shape[0], part, left.shape[2])
        half = (left.shape[0], part // 2, left.shape[2])
    first = 0 if got is None else 1
    slot_of = lambda k: (k + first) & (slots - 1)
    left_spec = pl.BlockSpec(left.shape, lambda k, seat: (0,) * left.ndim)
    if part % 128:
        order = 2 * (jnp.arange(slots, dtype=jnp.int32) ^ seat[0]) + seat[1]
        right = right.reshape(rows, count, part)[:, order].transpose(1, 0, 2)
        right_spec = pl.BlockSpec((None, rows, part), lambda k, seat: (slot_of(k), 0, 0))
    else:
        right_spec = pl.BlockSpec(
            (rows, part), lambda k, seat: (0, 2 * (slot_of(k) ^ seat[0]) + seat[1])
        )

    def fixed(shape):
        return pl.BlockSpec(shape, lambda k, seat: (0,) * len(shape))

    block_spec = pl.BlockSpec((1,) + block, lambda k, seat: (slot_of(k),) + (0,) * len(block))
    if got is None:
        shapes = [jax.ShapeDtypeStruct((slots,) + block, NARROW)]
        specs = [block_spec]
    else:
        rest = [(2,) + half, (2,) + half, half, half] if crossing else [block] * (slots - 1)
        shapes = [jax.ShapeDtypeStruct(block, WIDE)]
        shapes += [jax.ShapeDtypeStruct(shape, NARROW) for shape in rest]
        specs = [fixed(shape.shape) for shape in shapes]
    kernel = (
        functools.partial(sent_kernel, tall=tall)
        if got is None
        else functools.partial(kept_kernel, tall=tall, crossing=crossing)
    )
    return pl.pallas_call(
        kernel,
        name="sent" if got is None else "kept",
        grid_spec=pltpu.PrefetchScalarGridSpec(
            num_scalar_prefetch=1,
            grid=(slots,),
            in_specs=[left_spec, right_spec] + ([] if got is None else [block_spec]),
            out_specs=tuple(specs),
        ),
        out_shape=tuple(shapes),
        compiler_params=params(40),
        cost_estimate=SMALL,
    )(seat, left, right, *([] if got is None else [got]))


def send_gradient(left, right, rank, count, tall):
    seat = jnp.stack([rank >> 1, 1 - (rank & 1)])
    return gradient_blocks(seat, left, right, count, tall)[0]


def keep_gradient(left, right, got, rank, count, tall, crossing=False):
    seat = jnp.stack([rank >> 1, rank & 1])
    return gradient_blocks(
        seat, left, right, count, tall, got, crossing=crossing and count == 8
    )


def add_gradient(rest, *earlier):
    if isinstance(rest, list):
        total = after(rest[0], *earlier) if earlier else rest[0]
        for got in rest[1:]:
            total = total + got.astype(WIDE)
        return total
    total, first, first_own, second, second_own, axis = rest
    if earlier:
        total = after(total, *earlier)
    first = first.astype(WIDE) + first_own.astype(WIDE)
    second = second.astype(WIDE) + second_own.astype(WIDE)
    return total + jnp.concatenate([first, second], axis=axis)


def start_gradient(pieces, count):
    if count != 8:
        return pieces
    total, across, along, keep_first, keep_second = pieces
    return total, hop(across, "seq", 2, count), hop(along, "seq", 4, count), keep_first, keep_second


def finish_gradient(pieces, count, sent=None):
    total = pieces[0]
    if count == 8 and pieces[1].ndim > total.ndim:
        _, across, along, keep_first, keep_second = pieces
        axis = total.ndim - 2
        first = (keep_first.astype(WIDE) + across[1].astype(WIDE)).astype(NARROW)
        second = (keep_second.astype(WIDE) + along[1].astype(WIDE)).astype(NARROW)
        if sent is not None:
            sent += [first, second]
        first = hop(first, "seq", 4, count)
        second = hop(second, "seq", 2, count)
        return total, first, across[0], second, along[0], axis
    return [total] + [hop(pieces[slot], "seq", 2 * slot, count) for slot in range(1, len(pieces))]


def scalar_spec():
    return pl.BlockSpec(memory_space=pltpu.SMEM)


def full_spec(array):
    return pl.BlockSpec(array.shape, lambda i: (0,) * len(array.shape))


def local_call(kernel, name, scalars, inputs, heavy, outs, scratch, mib):
    return pl.pallas_call(
        kernel,
        name=name,
        grid=(1,),
        out_shape=tuple(outs),
        in_specs=[scalar_spec()] * len(scalars)
        + [full_spec(item) for item in inputs]
        + [pl.BlockSpec(memory_space=pl.ANY)] * len(heavy),
        out_specs=tuple(full_spec(item) for item in outs),
        scratch_shapes=list(scratch),
        compiler_params=params(mib),
        cost_estimate=SMALL,
    )(*scalars, *inputs, *heavy)


def resident_call(kernel, name, scalars, remote, inputs, outs, remote_outs, scratch, mib):
    return pl.pallas_call(
        kernel,
        name=name,
        out_shape=tuple(outs) + tuple(remote_outs),
        in_specs=[scalar_spec()] * len(scalars)
        + [pl.BlockSpec(memory_space=pl.ANY)] * len(remote)
        + [pl.BlockSpec(memory_space=pltpu.VMEM)] * len(inputs),
        out_specs=(pl.BlockSpec(memory_space=pltpu.VMEM),) * len(outs)
        + (pl.BlockSpec(memory_space=pl.ANY),) * len(remote_outs),
        scratch_shapes=list(scratch),
        compiler_params=params(mib),
        cost_estimate=SMALL,
    )(*scalars, *remote, *inputs)


def shaped(shape, dtype):
    return jax.ShapeDtypeStruct(tuple(shape), dtype)


SPAN = 256


def span_of(step):
    return pl.ds(pl.multiple_of(step * SPAN, SPAN), SPAN)


def fetch(source, held, sems, step, axis):
    where = (slice(None),) * axis + (span_of(step),)
    return pltpu.make_async_copy(source.at[where], held.at[where], sems.at[step])


def fetch_all(source, held, sems, axis):
    for step in range(source.shape[axis] // SPAN):
        fetch(source, held, sems, step, axis).start()


def params(mib):
    return pltpu.CompilerParams(vmem_limit_bytes=mib * MIB)


def turn_packed(values, straight, crossed):
    lane = lax.broadcasted_iota(jnp.int32, values.shape, 1)
    ahead = pltpu.roll(values, 2 * HD - HD // 2, 1)
    behind = pltpu.roll(values, HD // 2, 1)
    partner = jnp.where((lane & (HD // 2)) == 0, ahead, behind)
    return values * straight + partner * crossed


def rows_at(owner, rows):
    return pl.ds(pl.multiple_of(owner * rows, rows), rows)


def pack_kernel(place, owners, *refs, parts, heads, merge):
    rows_in = refs[:parts]
    at = parts
    if merge:
        earlier, earlier_rows = refs[at : at + 2]
        at += 2
    sources = refs[at : at + 4]
    at += 4
    if merge:
        outs, rows_out = refs[at : at + heads], refs[at + heads]
    else:
        out, rows_out = refs[at], refs[at + 1]
    if merge:
        held_before, rows_before, *rest = refs[-10:]
    else:
        rest = refs[-8:]
    weight, bias, straight, crossed, rows, held, sems, more_sems = rest
    count = weight.shape[0]
    loads = [
        pltpu.make_async_copy(sources[0].at[c], weight.at[c], more_sems.at[c]) for c in range(count)
    ] + [
        pltpu.make_async_copy(source, target, more_sems.at[count + k])
        for k, (source, target) in enumerate(zip(sources[1:], (bias, straight, crossed)))
    ]
    part = rows_in[0].shape[0]
    half = part // 2
    size = part + half
    incoming = [
        pltpu.make_async_copy(rows_in[i], rows.at[i * part : (i + 1) * part, :], sems.at[0, i])
        for i in range(parts)
    ]
    outgoing = []

    def send(source, target, *where):
        copy = pltpu.make_async_copy(source, target, sems.at[where])
        copy.start()
        outgoing.append(copy)

    for copy in incoming + loads:
        copy.start()
    for copy in incoming:
        copy.wait()
    if merge:
        before = [
            pltpu.make_async_copy(earlier, held_before, sems.at[0, 3 * parts]),
            pltpu.make_async_copy(earlier_rows, rows_before, sems.at[0, 3 * parts + 1]),
        ]
        for copy in before:
            copy.start()
    for i in range(parts):
        mine = rows_at(owners[i], part) if merge else slice(i * part, (i + 1) * part)
        send(rows.at[i * part : (i + 1) * part, :], rows_out.at[mine, :], 0, 2 * parts + i)
    for copy in loads[count:]:
        copy.wait()
    straight, crossed = (
        jnp.concatenate([table[rows_at(owners[i], part), :] for i in range(parts)], axis=0)
        for table in (straight, crossed)
    )
    projected = []
    for c in range(count):
        loads[c].wait()
        projected.append(
            jnp.dot(rows[...], weight[c], preferred_element_type=WIDE) + bias[c : c + 1, :]
        )
    for step in range(weight.shape[2] // SPAN):
        cols = slice(step * SPAN, (step + 1) * SPAN)
        query, key, value = (item[:, cols] for item in projected)
        for side in range(SPAN // HD):
            lanes = slice(side * HD, (side + 1) * HD)
            head = step * (SPAN // HD) + side
            both = jnp.concatenate([query[:, lanes], key[:, lanes]], axis=1)
            both = turn_packed(both, straight, crossed).astype(NARROW)
            for i in range(parts):
                held[i, head, :part, :] = both[i * part : (i + 1) * part]
                one = value[i * part : (i + 1) * part, lanes]
                held[i, head, part:, :] = jnp.concatenate(
                    [one[:half], one[half:]], axis=1
                ).astype(NARROW)
    if merge:
        for copy in before:
            copy.wait()
        for i in range(parts):
            other = owners[parts + i]
            send(
                rows_before.at[i * part : (i + 1) * part, :],
                rows_out.at[rows_at(other, part), :],
                0,
                parts + i,
            )
            for slot in range(heads):
                send(
                    held_before.at[i, place[0] ^ slot],
                    outs[slot].at[rows_at(other, size), :],
                    1 + i,
                    slot,
                )
                send(
                    held.at[i, place[0] ^ slot],
                    outs[slot].at[rows_at(owners[i], size), :],
                    1 + parts + i,
                    slot,
                )
    else:
        for i in range(parts):
            send(held.at[i], out.at[i], 1, i)
    for copy in outgoing:
        copy.wait()


def pack_heads(place, owners, parts, weight, bias, straight, crossed, heads, earlier=()):
    count = len(parts)
    part, depth = parts[0].shape
    size = part + part // 2
    if earlier:
        outs = [shaped((2 * count * size, 2 * HD), NARROW)] * heads
        outs += [shaped((2 * count * part, depth), NARROW)]
    else:
        outs = [shaped((count, heads, size, 2 * HD), NARROW), shaped((count * part, depth), NARROW)]
    return resident_call(
        functools.partial(pack_kernel, parts=count, heads=heads, merge=bool(earlier)),
        "pack",
        [place, owners],
        [*parts, *earlier, weight, bias, straight, crossed],
        [],
        [],
        outs,
        [pltpu.VMEM(item.shape, NARROW) for item in earlier]
        + [
            pltpu.VMEM(weight.shape, NARROW),
            pltpu.VMEM(bias.shape, WIDE),
            pltpu.VMEM(straight.shape, WIDE),
            pltpu.VMEM(crossed.shape, WIDE),
            pltpu.VMEM((count * part, depth), NARROW),
            pltpu.VMEM((count, heads, size, 2 * HD), NARROW),
            pltpu.SemaphoreType.DMA((1 + 2 * count, max(heads, 3 * count + 2))),
            pltpu.SemaphoreType.DMA((weight.shape[0] + 3,)),
        ],
        54,
    )


def split_chunk(chunk):
    block = chunk.shape[0] * 2 // 3
    both = chunk[:block, :]
    packed = chunk[block:, :]
    value = jnp.concatenate([packed[:, :HD], packed[:, HD:]], axis=0)
    return both[:, :HD], both[:, HD:], value


def allowed_mask(begin, q_begin, starts, shape):
    keys = begin + lax.broadcasted_iota(jnp.int32, shape, 0)
    queries = q_begin + lax.broadcasted_iota(jnp.int32, shape, 1)
    return (keys >= starts) & (keys <= queries)


def key_ranges(info, index, first_block, block):
    here = first_block + index
    low = info[2 + 2 * index] // block
    clear = jnp.minimum((info[3 + 2 * index] + block - 1) // block, here)
    return low, clear, here


def forward_kernel(info, starts, *refs, groups, spread, parts):
    count = groups
    chunks = refs[:count]
    at = count + (1 if spread else 0)
    outs = refs[at : at + count]
    mixed, logs, keys, values, queries = refs[at + count :]
    me = info[0]
    first_block = info[1]
    block = starts.shape[2]
    part = block // parts
    size = part + part // 2
    for slot in range(parts * count):
        side = slot // count
        query, key, value = split_chunk(chunks[slot % count][side * size : (side + 1) * size, :])
        place = me ^ (slot % count)
        rows = slice(side * part, (side + 1) * part)
        queries[place, :, rows] = query.T
        if not spread:
            keys[place, rows, :] = key
            values[place, :, rows] = value.T
    if spread:

        @pl.loop(0, keys.shape[0])
        def _(kb):
            for side in range(parts):
                _, key, value = split_chunk(refs[count][kb, side * size : (side + 1) * size, :])
                rows = slice(side * part, (side + 1) * part)
                keys[kb, rows, :] = key
                values[kb, :, rows] = value.T

    @pl.loop(0, count)
    def _(index):
        low, clear, here = key_ranges(info, index, first_block, block)
        query = queries[index]
        begins = starts[index]

        def step(kb, carry, masked):
            top, total, accum = carry
            raw = jnp.dot(keys[kb], query, preferred_element_type=WIDE)
            if masked:
                raw = jnp.where(
                    allowed_mask(kb * block, here * block, begins, raw.shape), raw, OUTSIDE
                )
            fresh = jnp.maximum(top, jnp.max(raw, axis=0, keepdims=True) * (SCALE * LOG2E))
            kept = jnp.exp2(raw * (SCALE * LOG2E) - fresh)
            fade = jnp.exp2(top - fresh)
            total = total * fade + jnp.sum(kept, axis=0, keepdims=True)
            accum = accum * fade + jnp.dot(
                values[kb], kept.astype(NARROW), preferred_element_type=WIDE
            )
            return fresh, total, accum

        carry = (
            jnp.full((1, block), LOWEST, WIDE),
            jnp.zeros((1, block), WIDE),
            jnp.zeros((HD, block), WIDE),
        )
        carry = lax.fori_loop(low, clear, functools.partial(step, masked=True), carry)
        carry = lax.fori_loop(clear, here, functools.partial(step, masked=False), carry)
        top, total, accum = step(here, carry, True)
        mixed[index] = accum / total
        logs[index] = top + jnp.log2(total)

    for slot in range(count):
        outs[slot][...] = mixed[me ^ slot].astype(NARROW)


def attend_forward(info, starts, chunks, everyone, parts):
    count = len(chunks)
    block = starts.shape[2]
    spread = everyone is not None
    blocks = everyone.shape[0] if spread else count
    return local_call(
        functools.partial(forward_kernel, groups=count, spread=spread, parts=parts),
        "forward",
        [info],
        [starts, *chunks] + ([everyone] if spread else []),
        [],
        [shaped((HD, block), NARROW)] * count
        + [shaped((count, HD, block), WIDE), shaped((count, 1, block), WIDE)],
        [
            pltpu.VMEM((blocks, block, HD), NARROW),
            pltpu.VMEM((blocks, HD, block), NARROW),
            pltpu.VMEM((count, HD, block), NARROW),
        ],
        60,
    )


def backward_kernel(info, starts, logs, mixed, *refs, groups, spread, parts):
    count = groups
    chunks = refs[:count]
    grads = refs[count : 2 * count]
    at = 2 * count
    if spread:
        everyone = refs[at]
        at += 1
    outs = refs[at : at + (1 if spread else count)]
    at += len(outs)
    keys, keys_up, values, queries, queries_up, downs, downs_up, key_sum, value_sum, query_sum = refs[at:]
    me = info[0]
    first_block = info[1]
    block = starts.shape[2]
    blocks = keys.shape[0]
    part = block // parts
    half = block // 2
    size = part + part // 2
    for slot in range(parts * count):
        side = slot // count
        query, key, value = split_chunk(chunks[slot % count][side * size : (side + 1) * size, :])
        place = me ^ (slot % count)
        rows = slice(side * part, (side + 1) * part)
        queries[place, rows, :] = query
        queries_up[place, :, rows] = query.T
        if not spread:
            keys[place, rows, :] = key
            keys_up[place, :, rows] = key.T
            values[place, rows, :] = value
    for slot in range(count):
        down = grads[slot][...]
        downs_up[me ^ slot] = down
        downs[me ^ slot] = down.T
    if spread:

        @pl.loop(0, blocks)
        def _(kb):
            for side in range(parts):
                _, key, value = split_chunk(everyone[kb, side * size : (side + 1) * size, :])
                rows = slice(side * part, (side + 1) * part)
                keys[kb, rows, :] = key
                keys_up[kb, :, rows] = key.T
                values[kb, rows, :] = value

    key_sum[...] = jnp.zeros_like(key_sum)
    value_sum[...] = jnp.zeros_like(value_sum)

    @pl.loop(0, count)
    def _(index):
        low, clear, here = key_ranges(info, index, first_block, block)
        query_up = queries_up[index]
        down_up = downs_up[index]
        begins = starts[index]
        log = logs[index]
        delta = jnp.sum(down_up.astype(WIDE) * mixed[index], axis=0, keepdims=True)

        def step(kb, accum, masked):
            raw = jnp.dot(keys[kb], query_up, preferred_element_type=WIDE)
            probs = jnp.exp2(raw * (SCALE * LOG2E) - log)
            if masked:
                probs = jnp.where(
                    allowed_mask(kb * block, here * block, begins, raw.shape), probs, 0.0
                )
            grad_probs = jnp.dot(values[kb], down_up, preferred_element_type=WIDE)
            grad_scores = (probs * (grad_probs - delta)).astype(NARROW)
            value_sum[kb] += jnp.dot(
                probs.astype(NARROW), downs[index], preferred_element_type=WIDE
            )
            key_sum[kb] += jnp.dot(grad_scores, queries[index], preferred_element_type=WIDE)
            return accum + jnp.dot(keys_up[kb], grad_scores, preferred_element_type=WIDE)

        accum = jnp.zeros((HD, block), WIDE)
        accum = lax.fori_loop(low, clear, functools.partial(step, masked=True), accum)
        accum = lax.fori_loop(clear, here, functools.partial(step, masked=False), accum)
        query_sum[index] = step(here, accum, True)

    def packed(kb, query):
        both = jnp.concatenate([query, key_sum[kb]], axis=1) * SCALE
        one = value_sum[kb]
        return both.astype(NARROW), jnp.concatenate([one[:half], one[half:]], axis=1).astype(NARROW)

    if spread:

        @pl.loop(0, blocks)
        def _(kb):
            inside = (kb >= first_block) & (kb < first_block + count)
            query = query_sum[jnp.clip(kb - first_block, 0, count - 1)]
            both, value = packed(kb, jnp.where(inside, query, 0.0).T)
            outs[0][kb, :block, :] = both
            outs[0][kb, block:, :] = value

    else:
        for slot in range(count):
            place = me ^ slot
            both, value = packed(place, query_sum[place].T)
            outs[slot][:block, :] = both
            outs[slot][block:, :] = value


def attend_backward(info, starts, logs, mixed, chunks, grads, everyone, parts):
    count = len(chunks)
    block = starts.shape[2]
    spread = everyone is not None
    blocks = everyone.shape[0] if spread else count
    rows = block + block // 2
    outs = [shaped((blocks, rows, 2 * HD), NARROW)] if spread else [shaped((rows, 2 * HD), NARROW)] * count
    tall = (block, HD)
    flat = (HD, block)
    return local_call(
        functools.partial(backward_kernel, groups=count, spread=spread, parts=parts),
        "backward",
        [info],
        [starts, logs, mixed, *chunks, *grads] + ([everyone] if spread else []),
        [],
        outs,
        [
            pltpu.VMEM((blocks,) + tall, NARROW),
            pltpu.VMEM((blocks,) + flat, NARROW),
            pltpu.VMEM((blocks,) + tall, NARROW),
            pltpu.VMEM((count,) + tall, NARROW),
            pltpu.VMEM((count,) + flat, NARROW),
            pltpu.VMEM((count,) + tall, NARROW),
            pltpu.VMEM((count,) + flat, NARROW),
            pltpu.VMEM((blocks,) + tall, WIDE),
            pltpu.VMEM((blocks,) + tall, WIDE),
            pltpu.VMEM((count,) + flat, WIDE),
        ],
        60,
    )


def join_kernel(place, *refs):
    count = len(refs) - 3
    chunks, out, sums, held = refs[:count], refs[count], refs[count + 1], refs[count + 2]
    me = place[0]
    total = 0.0
    squares = 0.0
    for slot in range(count):
        held[me ^ slot] = chunks[slot][...]
        wide = chunks[slot][...].astype(WIDE)
        total = total + jnp.sum(wide, axis=0, keepdims=True)
        squares = squares + jnp.sum(wide * wide, axis=0, keepdims=True)
    sums[0:1, :] = total
    sums[1:2, :] = squares
    for pair in range(count // 2):
        both = jnp.concatenate([held[2 * pair], held[2 * pair + 1]], axis=0)
        out[:, pair * 2 * HD : (pair + 1) * 2 * HD] = both.T


def join_heads(place, chunks):
    count = len(chunks)
    block = chunks[0].shape[1]
    return local_call(
        join_kernel,
        "join",
        [place],
        chunks,
        [],
        [shaped((block, count * HD), NARROW), shaped((2, block), WIDE)],
        [pltpu.VMEM((count, HD, block), NARROW)],
        60,
    )


def unpack_kernel(place, straight, crossed, *refs):
    count = len(refs) - 3
    chunks, out, sums, held = refs[:count], refs[count], refs[count + 1], refs[count + 2]
    me = place[0]
    block = straight.shape[0]
    for slot in range(count):
        both = turn_packed(chunks[slot][:block, :].astype(WIDE), straight[...], -crossed[...])
        held[me ^ slot, :block, :] = both.astype(NARROW)
        held[me ^ slot, block:, :] = chunks[slot][block:, :]
    for pair in range(count // 2):
        parts = [split_chunk(held[2 * pair + side]) for side in range(2)]
        cols = slice(pair * 2 * HD, (pair + 1) * 2 * HD)
        for c in range(3):
            joined = jnp.concatenate([parts[0][c], parts[1][c]], axis=1)
            out[c, :, cols] = joined
            sums[c : c + 1, cols] = jnp.sum(joined.astype(WIDE), axis=0, keepdims=True)


def unpack_heads(place, straight, crossed, chunks):
    count = len(chunks)
    block = straight.shape[0]
    return local_call(
        unpack_kernel,
        "unpack",
        [place],
        [straight, crossed, *chunks],
        [],
        [shaped((3, block, count * HD), NARROW), shaped((3, count * HD), WIDE)],
        [pltpu.VMEM((count,) + chunks[0].shape, NARROW)],
        60,
    )


def mixed_out_kernel(mixed, gain, bias, *refs, width):
    sums, weight = refs[:-6], refs[-6]
    out, low, stats, kept, sems = refs[-5:]
    fetch_all(weight, kept, sems, 1)
    total = sums[0][...]
    for other in sums[1:]:
        total = total + other[...]
    center = total[0:1] / width
    spread = total[1:2] / width - center * center
    factor = lax.rsqrt(spread + EPSILON)
    stats[...] = jnp.concatenate([center, factor], axis=0)
    columns = jnp.concatenate([center, factor, total, total, total], axis=0).T
    unit = (mixed[...].astype(WIDE) - columns[:, 0:1]) * columns[:, 1:2]
    low[...] = (unit * gain[...] + bias[...]).astype(NARROW)
    for step in range(weight.shape[1] // SPAN):
        cols = slice(step * SPAN, (step + 1) * SPAN)
        fetch(weight, kept, sems, step, 1).wait()
        out[:, cols] = jnp.dot(low[...], kept[:, cols], preferred_element_type=WIDE).astype(NARROW)


def mixed_out_product(mixed, sums, gain, bias, weight):
    rows = mixed.shape[0]
    return local_call(
        functools.partial(mixed_out_kernel, width=weight.shape[1]),
        "mixed_out",
        [],
        [mixed, gain, bias, *sums],
        [weight],
        [shaped((rows, weight.shape[1]), NARROW), shaped(mixed.shape, NARROW), shaped((2, rows), WIDE)],
        [
            pltpu.VMEM(weight.shape, NARROW),
            pltpu.SemaphoreType.DMA((weight.shape[1] // SPAN,)),
        ],
        24,
    )


def fold_lanes(values):
    total = values[:, :128]
    for begin in range(128, values.shape[1], 128):
        total = total + values[:, begin : begin + 128]
    return total


def up_kernel(owners, *refs, parts, merge):
    rows_in = refs[:parts]
    bias, gain, grad, weight = refs[parts : parts + 4]
    earlier = refs[parts + 4 : parts + 6] if merge else ()
    active_out, slope_out, rows_out, stats, rows, sums, sems = refs[-7:]
    part = rows_in[0].shape[0]
    own = [slice(i * part, (i + 1) * part) for i in range(parts)]
    copies = [
        pltpu.make_async_copy(rows_in[i], rows.at[own[i], :], sems.at[i]) for i in range(parts)
    ]
    for copy in copies:
        copy.start()
    sums[...] = jnp.zeros_like(sums)
    for copy in copies:
        copy.wait()

    @pl.loop(0, weight.shape[1] // SPAN)
    def _(step):
        cols = span_of(step)
        value = jnp.dot(rows[...], weight[:, cols], preferred_element_type=WIDE) + bias[:, cols]
        below = 0.5 + 0.5 * lax.erf(value * math.sqrt(0.5))
        active = value * below
        slope = below + value * (
            jnp.exp(-0.5 * value * value) * (1.0 / math.sqrt(2.0 * math.pi))
        )
        active_out[:, cols] = active.astype(NARROW)
        slope_out[:, cols] = slope.astype(NARROW)
        back = jnp.concatenate([grad[rows_at(owners[i], part), cols] for i in range(parts)], axis=0)
        scaled = back.astype(WIDE) * gain[:, cols]
        sums[0] += fold_lanes(active)
        sums[1] += fold_lanes(active * active)
        sums[2] += fold_lanes(scaled)
        sums[3] += fold_lanes(scaled * active)

    lines = jnp.concatenate([jnp.sum(sums[i].T, axis=0, keepdims=True) for i in range(4)], axis=0)
    if merge:
        for i in range(parts):
            mine = rows_at(owners[i], part)
            other = rows_at(owners[parts + i], part)
            stats[:, mine] = lines[:, own[i]]
            stats[:, other] = earlier[1][:, own[i]]
            rows_out[mine, :] = rows[own[i], :]
            rows_out[other, :] = earlier[0][own[i], :]
    else:
        stats[...] = lines
        rows_out[...] = rows[...]


def up_product(owners, parts, weight, bias, gain, grad, earlier=()):
    count = len(parts)
    rows = count * parts[0].shape[0]
    depth, width = weight.shape
    both = rows * (2 if earlier else 1)
    return resident_call(
        functools.partial(up_kernel, parts=count, merge=bool(earlier)),
        "up",
        [owners],
        parts,
        [bias, gain, grad, weight, *earlier],
        [
            shaped((rows, width), NARROW),
            shaped((rows, width), NARROW),
            shaped((both, depth), NARROW),
            shaped((4, both), WIDE),
        ],
        [],
        [
            pltpu.VMEM((rows, depth), NARROW),
            pltpu.VMEM((4, rows, 128), WIDE),
            pltpu.SemaphoreType.DMA((count,)),
        ],
        20,
    )


def ffn_back_kernel(owners, got, mine, *refs, parts, width):
    halves = refs[:2], refs[2:4]
    grad, gain, shift, weight, hidden_out, grad_out, lines, product = refs[4:12]
    columns, total, sums, low, sems = refs[12:]
    part = grad.shape[0] // parts
    copy = pltpu.make_async_copy(got, sums, sems.at[0])
    copy.start()
    total[...] = jnp.zeros_like(total)
    copy.wait()
    whole = (mine[...] + sums[...]) / width
    center, square, lean, cross = (whole[i : i + 1] for i in range(4))
    factor = lax.rsqrt(square - center * center + EPSILON)
    cross = (cross - center * lean) * factor
    columns[...] = jnp.concatenate([center, factor, lean, cross, whole], axis=0).T

    @pl.loop(0, weight.shape[1] // SPAN)
    def _(step):
        cols = span_of(step)
        line = [0.0, 0.0, 0.0]
        grads = []
        for i in range(parts):
            active, slope = halves[i // (parts // 2)]
            own = i % (parts // 2)
            own = slice(own * part, (own + 1) * part)
            rows = rows_at(owners[i], part)
            center, factor, lean, cross = (columns[rows, k : k + 1] for k in range(4))
            unit = (active[own, cols].astype(WIDE) - center) * factor
            hidden_out[rows, cols] = (unit * gain[:, cols] + shift[:, cols]).astype(NARROW)
            back = grad[rows, cols].astype(WIDE)
            grad_active = (back * gain[:, cols] - lean - unit * cross) * factor
            grad_up = (grad_active * slope[own, cols].astype(WIDE)).astype(NARROW)
            grad_out[rows, cols] = grad_up
            grads.append(grad_up)
            line[0] = line[0] + jnp.sum(grad_up.astype(WIDE), axis=0, keepdims=True)
            line[1] = line[1] + jnp.sum(back * unit, axis=0, keepdims=True)
            line[2] = line[2] + jnp.sum(back, axis=0, keepdims=True)
        lines[:, cols] = jnp.concatenate(line, axis=0)
        total[...] += lax.dot_general(
            jnp.concatenate(grads, axis=0),
            weight[:, cols],
            (((1,), (1,)), ((), ())),
            preferred_element_type=WIDE,
        )

    outgoing = []
    for i in range(parts):
        low[i * part : (i + 1) * part, :] = total[i * part : (i + 1) * part, :].astype(NARROW)
        copy = pltpu.make_async_copy(
            low.at[i * part : (i + 1) * part, :],
            product.at[rows_at(owners[i], part), :],
            sems.at[1 + i],
        )
        copy.start()
        outgoing.append(copy)
    for copy in outgoing:
        copy.wait()


def ffn_back_product(owners, sums, near, far, grad, gain, shift, weight, width):
    rows, local = grad.shape
    depth = weight.shape[0]
    both = shaped((rows, local), NARROW)
    parts = owners.shape[0]
    mine, got = sums
    hidden, grad_up, lines, product = resident_call(
        functools.partial(ffn_back_kernel, parts=parts, width=width),
        "ffn_back",
        [owners],
        [got],
        [mine, *near, *far, grad, gain, shift, weight],
        [both, both, shaped((3, local), WIDE)],
        [shaped((rows, depth), NARROW)],
        [
            pltpu.VMEM((rows, 8), WIDE),
            pltpu.VMEM((rows, depth), WIDE),
            pltpu.VMEM(mine.shape, WIDE),
            pltpu.VMEM((rows, depth), NARROW),
            pltpu.SemaphoreType.DMA((1 + parts,)),
        ],
        24,
    )
    return hidden, grad_up, product, lines


def mixed_back_kernel(seat, *refs, parts):
    mixed, stats, gain, weight, grad, rows, sums, lines, kept, sem = refs[parts:]
    copy = pltpu.make_async_copy(weight, kept, sem)
    copy.start()
    part = refs[0].shape[0]
    for i in range(parts):
        rows[rows_at(seat[i], part), :] = refs[i][...]
    columns = jnp.concatenate([stats[...]] * 4, axis=0).T
    unit = (mixed[...].astype(WIDE) - columns[:, 0:1]) * columns[:, 1:2]
    copy.wait()
    back = lax.dot_general(
        rows[...], kept[...], (((1,), (1,)), ((), ())), preferred_element_type=WIDE
    )
    grad[...] = back
    lines[0:1, :] = jnp.sum(back * unit, axis=0, keepdims=True)
    lines[1:2, :] = jnp.sum(back, axis=0, keepdims=True)
    scaled = back * gain[...]
    sums[0:1, :] = jnp.sum(fold_lanes(scaled).T, axis=0, keepdims=True)
    sums[1:2, :] = jnp.sum(fold_lanes(scaled * unit).T, axis=0, keepdims=True)


def mixed_back_product(seat, parts, mixed, stats, gain, weight):
    rows, local = mixed.shape
    return local_call(
        functools.partial(mixed_back_kernel, parts=len(parts)),
        "mixed_back",
        [seat],
        [*parts, mixed, stats, gain],
        [weight],
        [
            shaped((rows, local), WIDE),
            shaped((rows, weight.shape[1]), NARROW),
            shaped((2, rows), WIDE),
            shaped((2, local), WIDE),
        ],
        [pltpu.VMEM(weight.shape, NARROW), pltpu.SemaphoreType.DMA],
        24,
    )


def cut_kernel(seat, grad, mixed, stats, gain, *refs, count, width):
    sums = refs[:count]
    outs, held = refs[count:-1], refs[-1]
    total = sums[0][...]
    for other in sums[1:]:
        total = total + other[...]
    total = total / width
    columns = jnp.concatenate([stats[...], total] * 2, axis=0).T
    factor = columns[:, 1:2]
    unit = (mixed[...].astype(WIDE) - columns[:, 0:1]) * factor
    result = (grad[...] * gain[...] - columns[:, 2:3] - unit * columns[:, 3:4]) * factor
    result = result.astype(NARROW)
    heads = len(outs)
    for pair in range(heads // 2):
        both = result[:, pair * 2 * HD : (pair + 1) * 2 * HD].T
        held[2 * pair] = both[:HD]
        held[2 * pair + 1] = both[HD:]
    for slot in range(heads):
        outs[slot][...] = held[seat[0] ^ slot]


def cut_heads(seat, grad, mixed, stats, gain, sums, heads, width):
    block = grad.shape[0]
    return local_call(
        functools.partial(cut_kernel, count=len(sums), width=width),
        "cut",
        [seat],
        [grad, mixed, stats, gain, *sums],
        [],
        [shaped((HD, block), NARROW)] * heads,
        [pltpu.VMEM((heads, HD, block), NARROW)],
        60,
    )


def attn_back_kernel(grads, rows, gain, bias, weight, product, lines, kept, sems):
    fetch_all(weight, kept, sems, 1)

    @pl.loop(0, product.shape[1] // SPAN)
    def _(step):
        cols = span_of(step)
        fetch(weight, kept, sems, step, 1).wait()
        total = 0.0
        for c in range(grads.shape[0]):
            total = total + lax.dot_general(
                grads[c], kept[c, cols, :], (((1,), (1,)), ((), ())), preferred_element_type=WIDE
            )
        product[:, cols] = total.astype(NARROW)
        unit = (rows[:, cols].astype(WIDE) - bias[:, cols]) / gain[:, cols]
        lines[0:1, cols] = jnp.sum(total * unit, axis=0, keepdims=True)
        lines[1:2, cols] = jnp.sum(total, axis=0, keepdims=True)


def attn_back_product(grads, rows, gain, bias, weight):
    count, depth = rows.shape
    return local_call(
        attn_back_kernel,
        "attn_back",
        [],
        [grads, rows, gain, bias],
        [weight],
        [shaped((count, depth), NARROW), shaped((2, depth), WIDE)],
        [
            pltpu.VMEM(weight.shape, NARROW),
            pltpu.SemaphoreType.DMA((depth // SPAN,)),
        ],
        60,
    )


def shards(
    inputs,
    segment_ids,
    cotangent,
    qkv_weight,
    qkv_bias,
    out_weight,
    out_bias,
    up_weight,
    up_bias,
    down_weight,
    down_bias,
    input_gain,
    input_bias,
    mixed_gain,
    mixed_bias,
    middle_gain,
    middle_bias,
    hidden_gain,
    hidden_bias,
    qkv_average,
    out_average,
    up_average,
    down_average,
    decay_rate,
):
    seq_count = lax.axis_size("seq")
    seq_rank = lax.axis_index("seq")
    local_rows = segment_ids.shape[0]
    model_width = inputs.shape[1]
    local_width = qkv_weight.shape[2]
    heads_here = local_width // HD
    team = heads_here
    teams = seq_count // team
    place = seq_rank % team
    home = seq_rank - place

    def trade(chunks):
        got = {m: hop(chunks[m], "seq", m, seq_count) for m in range(2, team)}
        got[1] = hop(after(chunks[1], got[2]), "seq", 1, seq_count)
        return [chunks[0]] + [got[m] for m in range(1, team)]

    row_index = seq_rank * local_rows + jnp.arange(local_rows, dtype=jnp.int32)
    documents = jnp.arange(COUNT, dtype=jnp.int32)
    member = segment_ids[:, None] == documents[None, :]
    first_all = jnp.min(jnp.where(member, row_index[:, None], LARGEST), axis=0)
    bit = 1
    while bit < seq_count:
        first_all = jnp.minimum(first_all, hop(first_all, "seq", bit, seq_count))
        bit *= 2

    def starts_of(rows):
        earlier = first_all[None, :] <= rows[:, None]
        return jnp.max(jnp.where(earlier, first_all[None, :], 0), axis=1)

    cosine, sine, growth = xpos_tables(row_index - starts_of(row_index), HD)
    shrink = 1.0 / growth
    straight = jnp.concatenate([cosine * growth] * 2 + [cosine * shrink] * 2, axis=1)
    crossed = jnp.concatenate(
        [-sine * growth, sine * growth, -sine * shrink, sine * shrink], axis=1
    )
    team_rows = home * local_rows + jnp.arange(team * local_rows, dtype=jnp.int32)
    team_starts = starts_of(team_rows).reshape(team, local_rows)
    spans = jnp.stack([jnp.min(team_starts, axis=1), jnp.max(team_starts, axis=1)], axis=1)
    info = jnp.concatenate(
        [jnp.stack([place, home]).astype(jnp.int32), spans.reshape(-1)]
    )
    team_starts = team_starts.reshape(team, 1, local_rows)
    seat = jnp.reshape(place, (1,)).astype(jnp.int32)

    tp_count = lax.axis_size("tp")
    tp_rank = lax.axis_index("tp")
    inner = tp_count // 2
    near_first = part_owners(0)
    far_first = part_owners(inner)

    def line(vector):
        return vector.astype(WIDE).reshape(1, -1)

    def exchange(values):
        mask = 1
        while 2 * mask < tp_count:
            values = values + hop(values, "tp", mask, tp_count)
            mask *= 2
        return [values, hop(values, "tp", mask, tp_count)]

    inputs_wide = inputs.astype(WIDE)
    input_normed, input_back = jax.vjp(
        norm_rows, inputs_wide, input_gain.astype(WIDE), input_bias.astype(WIDE)
    )
    attn_parts = gather_parts(input_normed.astype(NARROW))
    rate = decay_rate[0]
    seq_part = model_width // seq_count
    offset = seq_rank * seq_part

    def average(old, weight, axis):
        piece = lax.dynamic_slice_in_dim(weight, offset, seq_part, axis).astype(WIDE)
        return rate * old + (1.0 - rate) * piece

    qkv_new = average(qkv_average, qkv_weight, 1)
    out_new = average(out_average, out_weight, 1)
    up_new = average(up_average, up_weight, 0)
    down_new = average(down_average, down_weight, 1)
    attn_parts[0] = after(attn_parts[0], straight, crossed)

    def pack(parts, chairs, earlier=()):
        return pack_heads(
            seat, chairs, parts, qkv_weight, qkv_bias.astype(WIDE), straight, crossed, team, earlier
        )

    packed = pack(attn_parts[:inner], near_first)
    attn_parts[inner] = after(attn_parts[inner], *packed)
    *packs, attn_in = pack(attn_parts[inner:], far_first, packed)
    grad_rows = gather_rows(after(cotangent, packs[0]))
    chunks = trade(packs)
    everyone = None
    if teams > 1:
        rings = [[j + team * t for t in range(teams)] for j in range(team)]
        natural = jnp.stack(chunks)[jnp.arange(team) ^ place]
        everyone = lax.all_gather(
            natural, "seq", axis=0, tiled=True, axis_index_groups=rings
        )
    *mixed_out, mixed_wide, logs = attend_forward(info, team_starts, chunks, everyone, tp_count)
    mixed_got = trade(mixed_out)

    mixed_got[0] = after(mixed_got[0], grad_rows)
    mixed, mixed_sums = join_heads(seat, mixed_got)
    out_product, mixed_low, mixed_stats = mixed_out_product(
        mixed, exchange(mixed_sums), line(mixed_gain), line(mixed_bias), out_weight
    )
    grad_hidden = jnp.einsum(
        "rd,fd->rf", grad_rows, down_weight, preferred_element_type=WIDE
    ).astype(NARROW)
    summed = after(scatter_rows(out_product), grad_hidden, qkv_new, out_new, up_new, down_new)
    middle = inputs_wide + summed + out_bias.astype(WIDE)
    normed, middle_back = jax.vjp(
        norm_rows, middle, middle_gain.astype(WIDE), middle_bias.astype(WIDE)
    )
    ffn_parts = gather_parts(normed.astype(NARROW))
    gain_line = line(hidden_gain)

    def up(parts, chairs, earlier=()):
        return up_product(
            chairs, parts, up_weight, line(up_bias), gain_line, grad_hidden, earlier
        )

    *up_near, ffn_near, sums_near = up(ffn_parts[:inner], near_first)
    ffn_parts[inner] = after(ffn_parts[inner], sums_near)
    *up_far, ffn_in, sums = up(ffn_parts[inner:], far_first, (ffn_near, sums_near))
    hidden_low, grad_up, ffn_back, hidden_lines = ffn_back_product(
        near_first,
        exchange(sums),
        up_near,
        up_far,
        grad_hidden,
        gain_line,
        line(hidden_bias),
        up_weight,
        FF,
    )
    upbias_part, hiddengain_part, hiddenbias_part = hidden_lines
    down_product = jnp.dot(hidden_low, down_weight, preferred_element_type=WIDE).astype(NARROW)
    late_rows = after(grad_rows, down_product)
    down_sent = send_gradient(hidden_low, late_rows, seq_rank, seq_count, True)
    up_sent = send_gradient(after(grad_up, down_product)[None], ffn_in, seq_rank, seq_count, False)
    summed = after(scatter_rows(ffn_back), down_sent, up_sent)
    norm_grad, middlegain_part, middlebias_part = middle_back(summed)
    grad_middle = cotangent.astype(WIDE) + norm_grad
    grad_low = grad_middle.astype(NARROW)
    middle_parts = gather_parts(grad_low)
    down_got = after(hop(down_sent, "seq", 1, seq_count), grad_low)
    up_got = hop(up_sent, "seq", 1, seq_count)
    down_pieces = keep_gradient(hidden_low, grad_rows, down_got, seq_rank, seq_count, True, True)
    up_pieces = keep_gradient(
        grad_up[None], ffn_in, up_got, seq_rank, seq_count, False, True
    )
    down_pieces = start_gradient(down_pieces, seq_count)
    middle_parts[-1] = after(middle_parts[-1], *up_pieces, *down_pieces)
    outbias_part = jnp.sum(grad_low, axis=0, dtype=WIDE)
    downbias_part = jnp.sum(cotangent, axis=0, dtype=WIDE)
    grad_mixed_norm, grad_mixed_rows, back_sums, mixed_lines = mixed_back_product(
        near_first,
        middle_parts,
        mixed,
        mixed_stats,
        line(mixed_gain),
        out_weight,
    )
    mixedgain_part, mixedbias_part = mixed_lines
    grad_cuts = cut_heads(
        seat,
        grad_mixed_norm,
        mixed,
        mixed_stats,
        line(mixed_gain),
        exchange(back_sums),
        team,
        model_width,
    )
    down_pieces = list(down_pieces)
    for slot in range(1, len(down_pieces)):
        down_pieces[slot] = after(down_pieces[slot], grad_mixed_norm)
    down_rest = finish_gradient(down_pieces, seq_count)
    grad_chunks = trade(grad_cuts)
    up_pieces = list(up_pieces)
    for slot in range(1, len(up_pieces)):
        up_pieces[slot] = after(up_pieces[slot], *grad_chunks)
    up_pieces = list(start_gradient(up_pieces, seq_count))
    layer_out = (
        middle
        + scatter_rows(after(down_product, grad_mixed_norm))
        + down_bias.astype(WIDE)
    ).astype(NARROW)
    pieces = attend_backward(
        info,
        team_starts,
        logs,
        mixed_wide,
        chunks,
        grad_chunks,
        everyone,
        tp_count,
    )
    pieces = list(pieces)
    down_grad = add_gradient(down_rest, pieces[0])
    arrived = list(down_rest[1:4:2]) + up_pieces[1:3]
    pieces = [after(piece, *arrived) for piece in pieces]
    out_sent = send_gradient(mixed_low, after(grad_mixed_rows, pieces[0]), seq_rank, seq_count, True)
    out_got = hop(out_sent, "seq", 1, seq_count)
    out_pieces = keep_gradient(mixed_low, grad_mixed_rows, out_got, seq_rank, seq_count, True)
    pieces[0] = after(pieces[0], layer_out)
    if teams > 1:
        natural = lax.psum_scatter(
            pieces[0], "seq", scatter_dimension=0, tiled=True, axis_index_groups=rings
        )
        pieces = [
            lax.dynamic_index_in_dim(natural, place ^ m, 0, keepdims=False) for m in range(team)
        ]
    parts_got = trade(pieces)
    parts_got[0] = after(parts_got[0], down_grad, *out_pieces)
    for slot in range(1, len(up_pieces)):
        up_pieces[slot] = after(up_pieces[slot], *parts_got)
    up_rest = finish_gradient(up_pieces, seq_count)
    out_pieces = list(out_pieces)
    for slot in range(1, len(out_pieces)):
        out_pieces[slot] = after(out_pieces[slot], *parts_got)
    out_grad = add_gradient(finish_gradient(out_pieces, seq_count))
    stacked, qkvbias_part = unpack_heads(seat, straight, crossed, parts_got)
    qkv_got = hop(send_gradient(stacked, attn_in, seq_rank, seq_count, False), "seq", 1, seq_count)
    attn_back, attn_lines = attn_back_product(
        stacked, attn_in, line(input_gain), line(input_bias), qkv_weight
    )
    inputgain_part, inputbias_part = attn_lines
    grad_attn_in = scatter_rows(attn_back)
    qkv_got = after(qkv_got, out_grad, attn_back, *(up_rest[1:4:2] if isinstance(up_rest, tuple) else ()))
    qkv_pieces = keep_gradient(stacked, attn_in, qkv_got, seq_rank, seq_count, False, True)
    qkv_pieces = start_gradient(qkv_pieces, seq_count)
    qkv_sent = []
    qkv_grad = add_gradient(finish_gradient(qkv_pieces, seq_count, qkv_sent))

    def spread_norms(parts):
        both = jnp.stack(parts).reshape(len(parts), seq_count, tp_count, -1)
        mine = tp_scatter(both.transpose(2, 1, 0, 3))
        return mine.reshape(seq_count, -1)

    inputgain_part = after(inputgain_part, qkv_pieces[0])
    vectors = jnp.concatenate(
        [
            item.reshape(seq_count, -1)
            for item in (
                upbias_part,
                hiddengain_part,
                hiddenbias_part,
                mixedgain_part,
                mixedbias_part,
                qkvbias_part[0],
                qkvbias_part[1],
                qkvbias_part[2],
            )
        ]
        + [
            spread_norms(
                [
                    middlegain_part,
                    middlebias_part,
                    outbias_part,
                    downbias_part,
                    inputgain_part,
                    inputbias_part,
                ]
            )
        ],
        axis=1,
    )
    vector_sums = vector_scatter(after(vectors, *qkv_sent), seq_rank, seq_count)
    up_grad = add_gradient(up_rest, vector_sums)[0]
    grad_attn_in = after(grad_attn_in, vector_sums)
    grad_input_norm, _, _ = input_back(grad_attn_in)
    input_grad = (grad_middle + grad_input_norm).astype(NARROW)
    narrow_part = local_width // seq_count
    wide_part = up_bias.shape[0] // seq_count
    norm_part = model_width // (seq_count * lax.axis_size("tp"))

    def cuts(vector, widths):
        begin = 0
        pieces = []
        for width in widths:
            pieces.append(vector[begin : begin + width])
            begin += width
        return pieces

    (
        upbias_grad,
        hiddengain_grad,
        hiddenbias_grad,
        mixedgain_grad,
        mixedbias_grad,
        q_bias,
        k_bias,
        v_bias,
        middlegain_grad,
        middlebias_grad,
        outbias_grad,
        downbias_grad,
        inputgain_grad,
        inputbias_grad,
    ) = cuts(vector_sums, (wide_part,) * 3 + (narrow_part,) * 5 + (norm_part,) * 6)
    return (
        layer_out,
        input_grad,
        qkv_grad,
        jnp.stack([q_bias, k_bias, v_bias]),
        out_grad,
        outbias_grad,
        up_grad,
        upbias_grad,
        down_grad,
        downbias_grad,
        inputgain_grad,
        inputbias_grad,
        mixedgain_grad,
        mixedbias_grad,
        middlegain_grad,
        middlebias_grad,
        hiddengain_grad,
        hiddenbias_grad,
        qkv_new,
        out_new,
        up_new,
        down_new,
    )


def solution(mesh):
    in_specs = (
        P(("seq", "tp"), None),
        P("seq"),
        P(("seq", "tp"), None),
        P(None, None, "tp"),
        P(None, "tp"),
        P("tp", None),
        P(),
        P(None, "tp"),
        P("tp"),
        P("tp", None),
        P(),
        P(),
        P(),
        P("tp"),
        P("tp"),
        P(),
        P(),
        P("tp"),
        P("tp"),
        P(None, "seq", "tp"),
        P("tp", "seq"),
        P("seq", "tp"),
        P("tp", "seq"),
        P(),
    )
    out_specs = (
        P(("seq", "tp"), None),
        P(("seq", "tp"), None),
        P(None, "seq", "tp"),
        P(None, ("tp", "seq")),
        P("tp", "seq"),
        P(("seq", "tp")),
        P("seq", "tp"),
        P(("tp", "seq")),
        P("tp", "seq"),
        P(("seq", "tp")),
        P(("seq", "tp")),
        P(("seq", "tp")),
        P(("tp", "seq")),
        P(("tp", "seq")),
        P(("seq", "tp")),
        P(("seq", "tp")),
        P(("tp", "seq")),
        P(("tp", "seq")),
        P(None, "seq", "tp"),
        P("tp", "seq"),
        P("seq", "tp"),
        P("tp", "seq"),
    )
    return jax.shard_map(shards, mesh=mesh, in_specs=in_specs, out_specs=out_specs, check_vma=False)
```

```python
import functools
import math

import jax
import jax.numpy as jnp
from jax import lax
from jax.experimental import pallas as pl
from jax.experimental.pallas import tpu as pltpu
from jax.sharding import PartitionSpec as P

FF = 8192
COUNT = 16
HD = 64

SCALE = 0.125
LOG2E = 1.4426950408889634
EPSILON = 1e-05
OUTSIDE = -2e30
LOWEST = -1e30
LARGEST = 1 << 30
WIDE = jnp.float32
NARROW = jnp.bfloat16
MIB = 1 << 20
SMALL = pl.CostEstimate(flops=1 << 20, bytes_accessed=1 << 16, transcendentals=0)


def xpos_tables(positions, head_size):
    half = head_size // 2
    index = jnp.arange(half, dtype=jnp.float32)
    frequency = jnp.exp(index * (-2.0 * math.log(10000.0) / head_size))
    zeta = (index * (2.0 / head_size) + 0.4) / 1.4
    places = positions.astype(jnp.float32)[:, None]
    angle = places * frequency[None, :]
    growth = jnp.exp(places * (jnp.log(zeta)[None, :] / 512.0))
    return (jnp.cos(angle), jnp.sin(angle), growth)


def norm_rows(values, gain, shift):
    center = jnp.mean(values, axis=-1, keepdims=True)
    spread = jnp.mean(values * values, axis=-1, keepdims=True) - center * center
    return (values - center) * lax.rsqrt(spread + EPSILON) * gain + shift


def exact_gelu(values):
    return jax.nn.gelu(values, approximate=False)


def gather_rows(values):
    return lax.all_gather(values, "tp", axis=0, tiled=True)


def ring_order(count):
    return [0] + list(range(1, count, 2)) + list(range(2, count, 2))[::-1]


def gather_parts(values):
    order = ring_order(lax.axis_size("tp"))
    parts = [values]
    for _ in order[1:]:
        pairs = [(a, b) for a, b in zip(order, order[1:] + order[:1])]
        parts.append(lax.ppermute(parts[-1], "tp", pairs))
    return parts


def part_owners(first):
    order = ring_order(lax.axis_size("tp"))
    count = len(order)
    rows = [
        [order[(order.index(rank) - first - slot) % count] for slot in range(count)]
        for rank in range(count)
    ]
    table = jnp.array(rows, jnp.int32)
    return lax.dynamic_index_in_dim(table, lax.axis_index("tp"), 0, keepdims=False)


def scatter_rows(values):
    return lax.psum_scatter(values.astype(NARROW), "tp", scatter_dimension=0, tiled=True).astype(WIDE)


def hop(values, axis, mask, count):
    return lax.ppermute(values, axis, [(i, i ^ mask) for i in range(count)])


def tp_total(values):
    count = lax.axis_size("tp")
    if count & (count - 1):
        return lax.psum(values, "tp")
    total = values
    for mask in range(1, count):
        total = total + hop(values, "tp", mask, count)
    return total


def after(value, *others):
    return lax.optimization_barrier((value,) + others)[0]


def vector_scatter(values, rank, count):
    bit = count // 2
    while bit:
        pair = values.reshape(2, bit, -1)
        mine = (rank & bit) // bit
        send = lax.dynamic_index_in_dim(pair, 1 - mine, 0, keepdims=False)
        keep = lax.dynamic_index_in_dim(pair, mine, 0, keepdims=False)
        values = keep + hop(send, "seq", bit, count)
        bit //= 2
    return values.reshape(-1)


def tp_scatter(values):
    count = lax.axis_size("tp")
    rank = lax.axis_index("tp")
    if count & (count - 1):
        return lax.psum_scatter(values, "tp", scatter_dimension=0)
    total = lax.dynamic_index_in_dim(values, rank, 0, keepdims=False)
    for mask in range(1, count):
        part = lax.dynamic_index_in_dim(values, rank ^ mask, 0, keepdims=False)
        total = total + hop(part, "tp", mask, count)
    return total


def sent_kernel(place, left, right, out, *, tall):
    if tall:
        out[0] = lax.dot_general(
            left[...], right[...], (((0,), (0,)), ((), ())), preferred_element_type=WIDE
        ).astype(NARROW)
    else:
        turned = right[...].T
        for c in range(left.shape[0]):
            out[0, c] = jnp.dot(turned, left[c], preferred_element_type=WIDE).astype(NARROW)


def kept_kernel(seat, left, right, got, *outs, tall, crossing):
    slots = pl.num_programs(0)
    step = pl.program_id(0)
    if tall:
        total = lax.dot_general(
            left[...], right[...], (((0,), (0,)), ((), ())), preferred_element_type=WIDE
        ) + got[0].astype(WIDE)
        rows = total.shape[0]
    else:
        turned = right[...].T
        total = jnp.stack(
            [
                jnp.dot(turned, left[c], preferred_element_type=WIDE) + got[0, c].astype(WIDE)
                for c in range(left.shape[0])
            ]
        )
        rows = total.shape[1]

    def at(slot):
        return pl.when(step == (slot - 1) % slots)

    @at(0)
    def _():
        outs[0][...] = total

    if crossing:
        cut = rows // 2
        low = total.astype(NARROW)
        first, second = (low[:cut], low[cut:]) if tall else (low[:, :cut], low[:, cut:])
        across, along, keep_first, keep_second = outs[1:]

        @at(1)
        def _():
            across[0] = first
            keep_second[...] = second

        @at(2)
        def _():
            keep_first[...] = first
            along[0] = second

        @at(3)
        def _():
            across[1] = first
            along[1] = second

    else:
        for slot in range(1, len(outs)):

            @at(slot)
            def _():
                outs[slot][...] = total.astype(NARROW)


def gradient_blocks(seat, left, right, count, tall, got=None, crossing=False):
    rows = right.shape[0]
    part = right.shape[1] // count
    slots = count // 2
    if tall:
        block = (left.shape[1], part)
        half = (left.shape[1] // 2, part)
    else:
        block = (left.shape[0], part, left.shape[2])
        half = (left.shape[0], part // 2, left.shape[2])
    first = 0 if got is None else 1
    slot_of = lambda k: (k + first) & (slots - 1)
    left_spec = pl.BlockSpec(left.shape, lambda k, seat: (0,) * left.ndim)
    if part % 128:
        order = 2 * (jnp.arange(slots, dtype=jnp.int32) ^ seat[0]) + seat[1]
        right = right.reshape(rows, count, part)[:, order].transpose(1, 0, 2)
        right_spec = pl.BlockSpec((None, rows, part), lambda k, seat: (slot_of(k), 0, 0))
    else:
        right_spec = pl.BlockSpec(
            (rows, part), lambda k, seat: (0, 2 * (slot_of(k) ^ seat[0]) + seat[1])
        )

    def fixed(shape):
        return pl.BlockSpec(shape, lambda k, seat: (0,) * len(shape))

    block_spec = pl.BlockSpec((1,) + block, lambda k, seat: (slot_of(k),) + (0,) * len(block))
    if got is None:
        shapes = [jax.ShapeDtypeStruct((slots,) + block, NARROW)]
        specs = [block_spec]
    else:
        rest = [(2,) + half, (2,) + half, half, half] if crossing else [block] * (slots - 1)
        shapes = [jax.ShapeDtypeStruct(block, WIDE)]
        shapes += [jax.ShapeDtypeStruct(shape, NARROW) for shape in rest]
        specs = [fixed(shape.shape) for shape in shapes]
    kernel = (
        functools.partial(sent_kernel, tall=tall)
        if got is None
        else functools.partial(kept_kernel, tall=tall, crossing=crossing)
    )
    return pl.pallas_call(
        kernel,
        name="sent" if got is None else "kept",
        grid_spec=pltpu.PrefetchScalarGridSpec(
            num_scalar_prefetch=1,
            grid=(slots,),
            in_specs=[left_spec, right_spec] + ([] if got is None else [block_spec]),
            out_specs=tuple(specs),
        ),
        out_shape=tuple(shapes),
        compiler_params=params(40),
        cost_estimate=SMALL,
    )(seat, left, right, *([] if got is None else [got]))


def send_gradient(left, right, rank, count, tall):
    seat = jnp.stack([rank >> 1, 1 - (rank & 1)])
    return gradient_blocks(seat, left, right, count, tall)[0]


def keep_gradient(left, right, got, rank, count, tall, crossing=False):
    seat = jnp.stack([rank >> 1, rank & 1])
    return gradient_blocks(
        seat, left, right, count, tall, got, crossing=crossing and count == 8
    )


def add_gradient(rest, *earlier):
    if isinstance(rest, list):
        total = after(rest[0], *earlier) if earlier else rest[0]
        for got in rest[1:]:
            total = total + got.astype(WIDE)
        return total
    total, first, first_own, second, second_own, axis = rest
    if earlier:
        total = after(total, *earlier)
    first = first.astype(WIDE) + first_own.astype(WIDE)
    second = second.astype(WIDE) + second_own.astype(WIDE)
    return total + jnp.concatenate([first, second], axis=axis)


def start_gradient(pieces, count):
    if count != 8:
        return pieces
    total, across, along, keep_first, keep_second = pieces
    return total, hop(across, "seq", 2, count), hop(along, "seq", 4, count), keep_first, keep_second


def finish_gradient(pieces, count, sent=None):
    total = pieces[0]
    if count == 8 and pieces[1].ndim > total.ndim:
        _, across, along, keep_first, keep_second = pieces
        axis = total.ndim - 2
        first = (keep_first.astype(WIDE) + across[1].astype(WIDE)).astype(NARROW)
        second = (keep_second.astype(WIDE) + along[1].astype(WIDE)).astype(NARROW)
        if sent is not None:
            sent += [first, second]
        first = hop(first, "seq", 4, count)
        second = hop(second, "seq", 2, count)
        return total, first, across[0], second, along[0], axis
    return [total] + [hop(pieces[slot], "seq", 2 * slot, count) for slot in range(1, len(pieces))]


def scalar_spec():
    return pl.BlockSpec(memory_space=pltpu.SMEM)


def full_spec(array):
    return pl.BlockSpec(array.shape, lambda i: (0,) * len(array.shape))


def local_call(kernel, name, scalars, inputs, heavy, outs, scratch, mib):
    return pl.pallas_call(
        kernel,
        name=name,
        grid=(1,),
        out_shape=tuple(outs),
        in_specs=[scalar_spec()] * len(scalars)
        + [full_spec(item) for item in inputs]
        + [pl.BlockSpec(memory_space=pl.ANY)] * len(heavy),
        out_specs=tuple(full_spec(item) for item in outs),
        scratch_shapes=list(scratch),
        compiler_params=params(mib),
        cost_estimate=SMALL,
    )(*scalars, *inputs, *heavy)


def resident_call(kernel, name, scalars, remote, inputs, outs, remote_outs, scratch, mib):
    return pl.pallas_call(
        kernel,
        name=name,
        out_shape=tuple(outs) + tuple(remote_outs),
        in_specs=[scalar_spec()] * len(scalars)
        + [pl.BlockSpec(memory_space=pl.ANY)] * len(remote)
        + [pl.BlockSpec(memory_space=pltpu.VMEM)] * len(inputs),
        out_specs=(pl.BlockSpec(memory_space=pltpu.VMEM),) * len(outs)
        + (pl.BlockSpec(memory_space=pl.ANY),) * len(remote_outs),
        scratch_shapes=list(scratch),
        compiler_params=params(mib),
        cost_estimate=SMALL,
    )(*scalars, *remote, *inputs)


def shaped(shape, dtype):
    return jax.ShapeDtypeStruct(tuple(shape), dtype)


SPAN = 256


def span_of(step):
    return pl.ds(pl.multiple_of(step * SPAN, SPAN), SPAN)


def fetch(source, held, sems, step, axis):
    where = (slice(None),) * axis + (span_of(step),)
    return pltpu.make_async_copy(source.at[where], held.at[where], sems.at[step])


def fetch_all(source, held, sems, axis):
    for step in range(source.shape[axis] // SPAN):
        fetch(source, held, sems, step, axis).start()


def params(mib):
    return pltpu.CompilerParams(vmem_limit_bytes=mib * MIB)


def turn_packed(values, straight, crossed):
    lane = lax.broadcasted_iota(jnp.int32, values.shape, 1)
    ahead = pltpu.roll(values, 2 * HD - HD // 2, 1)
    behind = pltpu.roll(values, HD // 2, 1)
    partner = jnp.where((lane & (HD // 2)) == 0, ahead, behind)
    return values * straight + partner * crossed


def rows_at(owner, rows):
    return pl.ds(pl.multiple_of(owner * rows, rows), rows)


def pack_kernel(place, owners, *refs, parts, heads, merge):
    rows_in = refs[:parts]
    at = parts
    if merge:
        earlier, earlier_rows = refs[at : at + 2]
        at += 2
    sources = refs[at : at + 4]
    at += 4
    if merge:
        outs, rows_out = refs[at : at + heads], refs[at + heads]
    else:
        out, rows_out = refs[at], refs[at + 1]
    if merge:
        held_before, rows_before, *rest = refs[-10:]
    else:
        rest = refs[-8:]
    weight, bias, straight, crossed, rows, held, sems, more_sems = rest
    count = weight.shape[0]
    loads = [
        pltpu.make_async_copy(sources[0].at[c], weight.at[c], more_sems.at[c]) for c in range(count)
    ] + [
        pltpu.make_async_copy(source, target, more_sems.at[count + k])
        for k, (source, target) in enumerate(zip(sources[1:], (bias, straight, crossed)))
    ]
    part = rows_in[0].shape[0]
    half = part // 2
    size = part + half
    incoming = [
        pltpu.make_async_copy(rows_in[i], rows.at[i * part : (i + 1) * part, :], sems.at[0, i])
        for i in range(parts)
    ]
    outgoing = []

    def send(source, target, *where):
        copy = pltpu.make_async_copy(source, target, sems.at[where])
        copy.start()
        outgoing.append(copy)

    for copy in incoming + loads:
        copy.start()
    for copy in incoming:
        copy.wait()
    if merge:
        before = [
            pltpu.make_async_copy(earlier, held_before, sems.at[0, 3 * parts]),
            pltpu.make_async_copy(earlier_rows, rows_before, sems.at[0, 3 * parts + 1]),
        ]
        for copy in before:
            copy.start()
    for i in range(parts):
        mine = rows_at(owners[i], part) if merge else slice(i * part, (i + 1) * part)
        send(rows.at[i * part : (i + 1) * part, :], rows_out.at[mine, :], 0, 2 * parts + i)
    for copy in loads[count:]:
        copy.wait()
    straight, crossed = (
        jnp.concatenate([table[rows_at(owners[i], part), :] for i in range(parts)], axis=0)
        for table in (straight, crossed)
    )
    projected = []
    for c in range(count):
        loads[c].wait()
        projected.append(
            jnp.dot(rows[...], weight[c], preferred_element_type=WIDE) + bias[c : c + 1, :]
        )
    for step in range(weight.shape[2] // SPAN):
        cols = slice(step * SPAN, (step + 1) * SPAN)
        query, key, value = (item[:, cols] for item in projected)
        for side in range(SPAN // HD):
            lanes = slice(side * HD, (side + 1) * HD)
            head = step * (SPAN // HD) + side
            both = jnp.concatenate([query[:, lanes], key[:, lanes]], axis=1)
            both = turn_packed(both, straight, crossed).astype(NARROW)
            for i in range(parts):
                held[i, head, :part, :] = both[i * part : (i + 1) * part]
                one = value[i * part : (i + 1) * part, lanes]
                held[i, head, part:, :] = jnp.concatenate(
                    [one[:half], one[half:]], axis=1
                ).astype(NARROW)
    if merge:
        for copy in before:
            copy.wait()
        for i in range(parts):
            other = owners[parts + i]
            send(
                rows_before.at[i * part : (i + 1) * part, :],
                rows_out.at[rows_at(other, part), :],
                0,
                parts + i,
            )
            for slot in range(heads):
                send(
                    held_before.at[i, place[0] ^ slot],
                    outs[slot].at[rows_at(other, size), :],
                    1 + i,
                    slot,
                )
                send(
                    held.at[i, place[0] ^ slot],
                    outs[slot].at[rows_at(owners[i], size), :],
                    1 + parts + i,
                    slot,
                )
    else:
        for i in range(parts):
            send(held.at[i], out.at[i], 1, i)
    for copy in outgoing:
        copy.wait()


def pack_heads(place, owners, parts, weight, bias, straight, crossed, heads, earlier=()):
    count = len(parts)
    part, depth = parts[0].shape
    size = part + part // 2
    if earlier:
        outs = [shaped((2 * count * size, 2 * HD), NARROW)] * heads
        outs += [shaped((2 * count * part, depth), NARROW)]
    else:
        outs = [shaped((count, heads, size, 2 * HD), NARROW), shaped((count * part, depth), NARROW)]
    return resident_call(
        functools.partial(pack_kernel, parts=count, heads=heads, merge=bool(earlier)),
        "pack",
        [place, owners],
        [*parts, *earlier, weight, bias, straight, crossed],
        [],
        [],
        outs,
        [pltpu.VMEM(item.shape, NARROW) for item in earlier]
        + [
            pltpu.VMEM(weight.shape, NARROW),
            pltpu.VMEM(bias.shape, WIDE),
            pltpu.VMEM(straight.shape, WIDE),
            pltpu.VMEM(crossed.shape, WIDE),
            pltpu.VMEM((count * part, depth), NARROW),
            pltpu.VMEM((count, heads, size, 2 * HD), NARROW),
            pltpu.SemaphoreType.DMA((1 + 2 * count, max(heads, 3 * count + 2))),
            pltpu.SemaphoreType.DMA((weight.shape[0] + 3,)),
        ],
        54,
    )


def split_chunk(chunk):
    block = chunk.shape[0] * 2 // 3
    both = chunk[:block, :]
    packed = chunk[block:, :]
    value = jnp.concatenate([packed[:, :HD], packed[:, HD:]], axis=0)
    return both[:, :HD], both[:, HD:], value


def allowed_mask(begin, q_begin, starts, shape):
    keys = begin + lax.broadcasted_iota(jnp.int32, shape, 0)
    queries = q_begin + lax.broadcasted_iota(jnp.int32, shape, 1)
    return (keys >= starts) & (keys <= queries)


def key_ranges(info, index, first_block, block):
    here = first_block + index
    low = info[2 + 2 * index] // block
    clear = jnp.minimum((info[3 + 2 * index] + block - 1) // block, here)
    return low, clear, here


def forward_kernel(info, starts, *refs, groups, spread, parts):
    count = groups
    chunks = refs[:count]
    at = count + (1 if spread else 0)
    outs = refs[at : at + count]
    mixed, logs, keys, values, queries = refs[at + count :]
    me = info[0]
    first_block = info[1]
    block = starts.shape[2]
    part = block // parts
    size = part + part // 2
    for slot in range(parts * count):
        side = slot // count
        query, key, value = split_chunk(chunks[slot % count][side * size : (side + 1) * size, :])
        place = me ^ (slot % count)
        rows = slice(side * part, (side + 1) * part)
        queries[place, :, rows] = query.T
        if not spread:
            keys[place, rows, :] = key
            values[place, :, rows] = value.T
    if spread:

        @pl.loop(0, keys.shape[0])
        def _(kb):
            for side in range(parts):
                _, key, value = split_chunk(refs[count][kb, side * size : (side + 1) * size, :])
                rows = slice(side * part, (side + 1) * part)
                keys[kb, rows, :] = key
                values[kb, :, rows] = value.T

    @pl.loop(0, count)
    def _(index):
        low, clear, here = key_ranges(info, index, first_block, block)
        query = queries[index]
        begins = starts[index]

        def step(kb, carry, masked):
            top, total, accum = carry
            cuts = [slice(i * block // 4, (i + 1) * block // 4) for i in range(4)]
            raws = [
                jnp.dot(keys[kb], query[:, cut], preferred_element_type=WIDE) for cut in cuts
            ]
            results = []
            for cut, raw in zip(cuts, raws):
                if masked:
                    mask = allowed_mask(
                        kb * block, here * block + cut.start, begins[:, cut], raw.shape
                    )
                    raw = jnp.where(mask, raw, OUTSIDE)
                fresh = jnp.maximum(
                    top[:, cut], jnp.max(raw, axis=0, keepdims=True) * (SCALE * LOG2E)
                )
                kept = jnp.exp2(raw * (SCALE * LOG2E) - fresh)
                fade = jnp.exp2(top[:, cut] - fresh)
                results.append(
                    (
                        fresh,
                        total[:, cut] * fade + jnp.sum(kept, axis=0, keepdims=True),
                        accum[:, cut] * fade
                        + jnp.dot(values[kb], kept.astype(NARROW), preferred_element_type=WIDE),
                    )
                )
            return tuple(jnp.concatenate(item, axis=1) for item in zip(*results))

        carry = (
            jnp.full((1, block), LOWEST, WIDE),
            jnp.zeros((1, block), WIDE),
            jnp.zeros((HD, block), WIDE),
        )
        carry = lax.fori_loop(low, clear, functools.partial(step, masked=True), carry)
        carry = lax.fori_loop(clear, here, functools.partial(step, masked=False), carry)
        top, total, accum = step(here, carry, True)
        mixed[index] = accum / total
        logs[index] = top + jnp.log2(total)

    for slot in range(count):
        outs[slot][...] = mixed[me ^ slot].astype(NARROW)


def attend_forward(info, starts, chunks, everyone, parts):
    count = len(chunks)
    block = starts.shape[2]
    spread = everyone is not None
    blocks = everyone.shape[0] if spread else count
    return local_call(
        functools.partial(forward_kernel, groups=count, spread=spread, parts=parts),
        "forward",
        [info],
        [starts, *chunks] + ([everyone] if spread else []),
        [],
        [shaped((HD, block), NARROW)] * count
        + [shaped((count, HD, block), WIDE), shaped((count, 1, block), WIDE)],
        [
            pltpu.VMEM((blocks, block, HD), NARROW),
            pltpu.VMEM((blocks, HD, block), NARROW),
            pltpu.VMEM((count, HD, block), NARROW),
        ],
        60,
    )


def backward_kernel(info, starts, logs, mixed, *refs, groups, spread, parts):
    count = groups
    chunks = refs[:count]
    grads = refs[count : 2 * count]
    at = 2 * count
    if spread:
        everyone = refs[at]
        at += 1
    outs = refs[at : at + (1 if spread else count)]
    at += len(outs)
    keys, keys_up, values, queries, queries_up, downs, downs_up, key_sum, value_sum, query_sum = refs[at:]
    me = info[0]
    first_block = info[1]
    block = starts.shape[2]
    blocks = keys.shape[0]
    part = block // parts
    half = block // 2
    size = part + part // 2
    for slot in range(parts * count):
        side = slot // count
        query, key, value = split_chunk(chunks[slot % count][side * size : (side + 1) * size, :])
        place = me ^ (slot % count)
        rows = slice(side * part, (side + 1) * part)
        queries[place, rows, :] = query
        queries_up[place, :, rows] = query.T
        if not spread:
            keys[place, rows, :] = key
            keys_up[place, :, rows] = key.T
            values[place, rows, :] = value
    for slot in range(count):
        down = grads[slot][...]
        downs_up[me ^ slot] = down
        downs[me ^ slot] = down.T
    if spread:

        @pl.loop(0, blocks)
        def _(kb):
            for side in range(parts):
                _, key, value = split_chunk(everyone[kb, side * size : (side + 1) * size, :])
                rows = slice(side * part, (side + 1) * part)
                keys[kb, rows, :] = key
                keys_up[kb, :, rows] = key.T
                values[kb, rows, :] = value

    key_sum[...] = jnp.zeros_like(key_sum)
    value_sum[...] = jnp.zeros_like(value_sum)

    @pl.loop(0, count)
    def _(index):
        low, clear, here = key_ranges(info, index, first_block, block)
        query_up = queries_up[index]
        down_up = downs_up[index]
        begins = starts[index]
        log = logs[index]
        delta = jnp.sum(down_up.astype(WIDE) * mixed[index], axis=0, keepdims=True)

        def step(kb, accum, masked):
            raw = jnp.dot(keys[kb], query_up, preferred_element_type=WIDE)
            probs = jnp.exp2(raw * (SCALE * LOG2E) - log)
            if masked:
                probs = jnp.where(
                    allowed_mask(kb * block, here * block, begins, raw.shape), probs, 0.0
                )
            grad_probs = jnp.dot(values[kb], down_up, preferred_element_type=WIDE)
            grad_scores = (probs * (grad_probs - delta)).astype(NARROW)
            value_sum[kb] += jnp.dot(
                probs.astype(NARROW), downs[index], preferred_element_type=WIDE
            )
            key_sum[kb] += jnp.dot(grad_scores, queries[index], preferred_element_type=WIDE)
            return accum + jnp.dot(keys_up[kb], grad_scores, preferred_element_type=WIDE)

        accum = jnp.zeros((HD, block), WIDE)
        accum = lax.fori_loop(low, clear, functools.partial(step, masked=True), accum)
        accum = lax.fori_loop(clear, here, functools.partial(step, masked=False), accum)
        query_sum[index] = step(here, accum, True)

    def packed(kb, query):
        both = jnp.concatenate([query, key_sum[kb]], axis=1) * SCALE
        one = value_sum[kb]
        return both.astype(NARROW), jnp.concatenate([one[:half], one[half:]], axis=1).astype(NARROW)

    if spread:

        @pl.loop(0, blocks)
        def _(kb):
            inside = (kb >= first_block) & (kb < first_block + count)
            query = query_sum[jnp.clip(kb - first_block, 0, count - 1)]
            both, value = packed(kb, jnp.where(inside, query, 0.0).T)
            outs[0][kb, :block, :] = both
            outs[0][kb, block:, :] = value

    else:
        for slot in range(count):
            place = me ^ slot
            both, value = packed(place, query_sum[place].T)
            outs[slot][:block, :] = both
            outs[slot][block:, :] = value


def attend_backward(info, starts, logs, mixed, chunks, grads, everyone, parts):
    count = len(chunks)
    block = starts.shape[2]
    spread = everyone is not None
    blocks = everyone.shape[0] if spread else count
    rows = block + block // 2
    outs = [shaped((blocks, rows, 2 * HD), NARROW)] if spread else [shaped((rows, 2 * HD), NARROW)] * count
    tall = (block, HD)
    flat = (HD, block)
    return local_call(
        functools.partial(backward_kernel, groups=count, spread=spread, parts=parts),
        "backward",
        [info],
        [starts, logs, mixed, *chunks, *grads] + ([everyone] if spread else []),
        [],
        outs,
        [
            pltpu.VMEM((blocks,) + tall, NARROW),
            pltpu.VMEM((blocks,) + flat, NARROW),
            pltpu.VMEM((blocks,) + tall, NARROW),
            pltpu.VMEM((count,) + tall, NARROW),
            pltpu.VMEM((count,) + flat, NARROW),
            pltpu.VMEM((count,) + tall, NARROW),
            pltpu.VMEM((count,) + flat, NARROW),
            pltpu.VMEM((blocks,) + tall, WIDE),
            pltpu.VMEM((blocks,) + tall, WIDE),
            pltpu.VMEM((count,) + flat, WIDE),
        ],
        60,
    )


def join_kernel(place, *refs):
    count = len(refs) - 3
    chunks, out, sums, held = refs[:count], refs[count], refs[count + 1], refs[count + 2]
    me = place[0]
    total = 0.0
    squares = 0.0
    for slot in range(count):
        held[me ^ slot] = chunks[slot][...]
        wide = chunks[slot][...].astype(WIDE)
        total = total + jnp.sum(wide, axis=0, keepdims=True)
        squares = squares + jnp.sum(wide * wide, axis=0, keepdims=True)
    sums[0:1, :] = total
    sums[1:2, :] = squares
    for pair in range(count // 2):
        both = jnp.concatenate([held[2 * pair], held[2 * pair + 1]], axis=0)
        out[:, pair * 2 * HD : (pair + 1) * 2 * HD] = both.T


def join_heads(place, chunks):
    count = len(chunks)
    block = chunks[0].shape[1]
    return local_call(
        join_kernel,
        "join",
        [place],
        chunks,
        [],
        [shaped((block, count * HD), NARROW), shaped((2, block), WIDE)],
        [pltpu.VMEM((count, HD, block), NARROW)],
        60,
    )


def unpack_kernel(place, straight, crossed, *refs):
    count = len(refs) - 3
    chunks, out, sums, held = refs[:count], refs[count], refs[count + 1], refs[count + 2]
    me = place[0]
    block = straight.shape[0]
    for slot in range(count):
        both = turn_packed(chunks[slot][:block, :].astype(WIDE), straight[...], -crossed[...])
        held[me ^ slot, :block, :] = both.astype(NARROW)
        held[me ^ slot, block:, :] = chunks[slot][block:, :]
    for pair in range(count // 2):
        parts = [split_chunk(held[2 * pair + side]) for side in range(2)]
        cols = slice(pair * 2 * HD, (pair + 1) * 2 * HD)
        for c in range(3):
            joined = jnp.concatenate([parts[0][c], parts[1][c]], axis=1)
            out[c, :, cols] = joined
            sums[c : c + 1, cols] = jnp.sum(joined.astype(WIDE), axis=0, keepdims=True)


def unpack_heads(place, straight, crossed, chunks):
    count = len(chunks)
    block = straight.shape[0]
    return local_call(
        unpack_kernel,
        "unpack",
        [place],
        [straight, crossed, *chunks],
        [],
        [shaped((3, block, count * HD), NARROW), shaped((3, count * HD), WIDE)],
        [pltpu.VMEM((count,) + chunks[0].shape, NARROW)],
        60,
    )


def mixed_out_kernel(mixed, gain, bias, *refs, width):
    sums, weight = refs[:-6], refs[-6]
    out, low, stats, kept, sems = refs[-5:]
    fetch_all(weight, kept, sems, 1)
    total = sums[0][...]
    for other in sums[1:]:
        total = total + other[...]
    center = total[0:1] / width
    spread = total[1:2] / width - center * center
    factor = lax.rsqrt(spread + EPSILON)
    stats[...] = jnp.concatenate([center, factor], axis=0)
    columns = jnp.concatenate([center, factor, total, total, total], axis=0).T
    unit = (mixed[...].astype(WIDE) - columns[:, 0:1]) * columns[:, 1:2]
    low[...] = (unit * gain[...] + bias[...]).astype(NARROW)
    for step in range(weight.shape[1] // SPAN):
        cols = slice(step * SPAN, (step + 1) * SPAN)
        fetch(weight, kept, sems, step, 1).wait()
        out[:, cols] = jnp.dot(low[...], kept[:, cols], preferred_element_type=WIDE).astype(NARROW)


def mixed_out_product(mixed, sums, gain, bias, weight):
    rows = mixed.shape[0]
    return local_call(
        functools.partial(mixed_out_kernel, width=weight.shape[1]),
        "mixed_out",
        [],
        [mixed, gain, bias, *sums],
        [weight],
        [shaped((rows, weight.shape[1]), NARROW), shaped(mixed.shape, NARROW), shaped((2, rows), WIDE)],
        [
            pltpu.VMEM(weight.shape, NARROW),
            pltpu.SemaphoreType.DMA((weight.shape[1] // SPAN,)),
        ],
        24,
    )


def fold_lanes(values):
    total = values[:, :128]
    for begin in range(128, values.shape[1], 128):
        total = total + values[:, begin : begin + 128]
    return total


def up_kernel(owners, *refs, parts, merge):
    rows_in = refs[:parts]
    bias, gain, grad, weight = refs[parts : parts + 4]
    earlier = refs[parts + 4 : parts + 6] if merge else ()
    active_out, slope_out, rows_out, stats, rows, sums, sems = refs[-7:]
    part = rows_in[0].shape[0]
    own = [slice(i * part, (i + 1) * part) for i in range(parts)]
    copies = [
        pltpu.make_async_copy(rows_in[i], rows.at[own[i], :], sems.at[i]) for i in range(parts)
    ]
    for copy in copies:
        copy.start()
    sums[...] = jnp.zeros_like(sums)
    for copy in copies:
        copy.wait()

    @pl.loop(0, weight.shape[1] // SPAN)
    def _(step):
        cols = span_of(step)
        value = jnp.dot(rows[...], weight[:, cols], preferred_element_type=WIDE) + bias[:, cols]
        below = 0.5 + 0.5 * lax.erf(value * math.sqrt(0.5))
        active = value * below
        slope = below + value * (
            jnp.exp(-0.5 * value * value) * (1.0 / math.sqrt(2.0 * math.pi))
        )
        active_out[:, cols] = active.astype(NARROW)
        slope_out[:, cols] = slope.astype(NARROW)
        back = jnp.concatenate([grad[rows_at(owners[i], part), cols] for i in range(parts)], axis=0)
        scaled = back.astype(WIDE) * gain[:, cols]
        sums[0] += fold_lanes(active)
        sums[1] += fold_lanes(active * active)
        sums[2] += fold_lanes(scaled)
        sums[3] += fold_lanes(scaled * active)

    lines = jnp.concatenate([jnp.sum(sums[i].T, axis=0, keepdims=True) for i in range(4)], axis=0)
    if merge:
        for i in range(parts):
            mine = rows_at(owners[i], part)
            other = rows_at(owners[parts + i], part)
            stats[:, mine] = lines[:, own[i]]
            stats[:, other] = earlier[1][:, own[i]]
            rows_out[mine, :] = rows[own[i], :]
            rows_out[other, :] = earlier[0][own[i], :]
    else:
        stats[...] = lines
        rows_out[...] = rows[...]


def up_product(owners, parts, weight, bias, gain, grad, earlier=()):
    count = len(parts)
    rows = count * parts[0].shape[0]
    depth, width = weight.shape
    both = rows * (2 if earlier else 1)
    return resident_call(
        functools.partial(up_kernel, parts=count, merge=bool(earlier)),
        "up",
        [owners],
        parts,
        [bias, gain, grad, weight, *earlier],
        [
            shaped((rows, width), NARROW),
            shaped((rows, width), NARROW),
            shaped((both, depth), NARROW),
            shaped((4, both), WIDE),
        ],
        [],
        [
            pltpu.VMEM((rows, depth), NARROW),
            pltpu.VMEM((4, rows, 128), WIDE),
            pltpu.SemaphoreType.DMA((count,)),
        ],
        20,
    )


def ffn_back_kernel(owners, got, mine, *refs, parts, width):
    halves = refs[:2], refs[2:4]
    grad, gain, shift, weight, hidden_out, grad_out, lines, product = refs[4:12]
    columns, total, sums, low, sems = refs[12:]
    part = grad.shape[0] // parts
    copy = pltpu.make_async_copy(got, sums, sems.at[0])
    copy.start()
    total[...] = jnp.zeros_like(total)
    copy.wait()
    whole = (mine[...] + sums[...]) / width
    center, square, lean, cross = (whole[i : i + 1] for i in range(4))
    factor = lax.rsqrt(square - center * center + EPSILON)
    cross = (cross - center * lean) * factor
    columns[...] = jnp.concatenate([center, factor, lean, cross, whole], axis=0).T

    @pl.loop(0, weight.shape[1] // SPAN)
    def _(step):
        cols = span_of(step)
        line = [0.0, 0.0, 0.0]
        grads = []
        for i in range(parts):
            active, slope = halves[i // (parts // 2)]
            own = i % (parts // 2)
            own = slice(own * part, (own + 1) * part)
            rows = rows_at(owners[i], part)
            center, factor, lean, cross = (columns[rows, k : k + 1] for k in range(4))
            unit = (active[own, cols].astype(WIDE) - center) * factor
            hidden_out[rows, cols] = (unit * gain[:, cols] + shift[:, cols]).astype(NARROW)
            back = grad[rows, cols].astype(WIDE)
            grad_active = (back * gain[:, cols] - lean - unit * cross) * factor
            grad_up = (grad_active * slope[own, cols].astype(WIDE)).astype(NARROW)
            grad_out[rows, cols] = grad_up
            grads.append(grad_up)
            line[0] = line[0] + jnp.sum(grad_up.astype(WIDE), axis=0, keepdims=True)
            line[1] = line[1] + jnp.sum(back * unit, axis=0, keepdims=True)
            line[2] = line[2] + jnp.sum(back, axis=0, keepdims=True)
        lines[:, cols] = jnp.concatenate(line, axis=0)
        total[...] += lax.dot_general(
            jnp.concatenate(grads, axis=0),
            weight[:, cols],
            (((1,), (1,)), ((), ())),
            preferred_element_type=WIDE,
        )

    outgoing = []
    for i in range(parts):
        low[i * part : (i + 1) * part, :] = total[i * part : (i + 1) * part, :].astype(NARROW)
        copy = pltpu.make_async_copy(
            low.at[i * part : (i + 1) * part, :],
            product.at[rows_at(owners[i], part), :],
            sems.at[1 + i],
        )
        copy.start()
        outgoing.append(copy)
    for copy in outgoing:
        copy.wait()


def ffn_back_product(owners, sums, near, far, grad, gain, shift, weight, width):
    rows, local = grad.shape
    depth = weight.shape[0]
    both = shaped((rows, local), NARROW)
    parts = owners.shape[0]
    mine, got = sums
    hidden, grad_up, lines, product = resident_call(
        functools.partial(ffn_back_kernel, parts=parts, width=width),
        "ffn_back",
        [owners],
        [got],
        [mine, *near, *far, grad, gain, shift, weight],
        [both, both, shaped((3, local), WIDE)],
        [shaped((rows, depth), NARROW)],
        [
            pltpu.VMEM((rows, 8), WIDE),
            pltpu.VMEM((rows, depth), WIDE),
            pltpu.VMEM(mine.shape, WIDE),
            pltpu.VMEM((rows, depth), NARROW),
            pltpu.SemaphoreType.DMA((1 + parts,)),
        ],
        24,
    )
    return hidden, grad_up, product, lines


def mixed_back_kernel(seat, *refs, parts):
    mixed, stats, gain, weight, grad, rows, sums, lines, kept, sem = refs[parts:]
    copy = pltpu.make_async_copy(weight, kept, sem)
    copy.start()
    part = refs[0].shape[0]
    for i in range(parts):
        rows[rows_at(seat[i], part), :] = refs[i][...]
    columns = jnp.concatenate([stats[...]] * 4, axis=0).T
    unit = (mixed[...].astype(WIDE) - columns[:, 0:1]) * columns[:, 1:2]
    copy.wait()
    back = lax.dot_general(
        rows[...], kept[...], (((1,), (1,)), ((), ())), preferred_element_type=WIDE
    )
    grad[...] = back
    lines[0:1, :] = jnp.sum(back * unit, axis=0, keepdims=True)
    lines[1:2, :] = jnp.sum(back, axis=0, keepdims=True)
    scaled = back * gain[...]
    sums[0:1, :] = jnp.sum(fold_lanes(scaled).T, axis=0, keepdims=True)
    sums[1:2, :] = jnp.sum(fold_lanes(scaled * unit).T, axis=0, keepdims=True)


def mixed_back_product(seat, parts, mixed, stats, gain, weight):
    rows, local = mixed.shape
    return local_call(
        functools.partial(mixed_back_kernel, parts=len(parts)),
        "mixed_back",
        [seat],
        [*parts, mixed, stats, gain],
        [weight],
        [
            shaped((rows, local), WIDE),
            shaped((rows, weight.shape[1]), NARROW),
            shaped((2, rows), WIDE),
            shaped((2, local), WIDE),
        ],
        [pltpu.VMEM(weight.shape, NARROW), pltpu.SemaphoreType.DMA],
        24,
    )


def cut_kernel(seat, grad, mixed, stats, gain, *refs, count, width):
    sums = refs[:count]
    outs, held = refs[count:-1], refs[-1]
    total = sums[0][...]
    for other in sums[1:]:
        total = total + other[...]
    total = total / width
    columns = jnp.concatenate([stats[...], total] * 2, axis=0).T
    factor = columns[:, 1:2]
    unit = (mixed[...].astype(WIDE) - columns[:, 0:1]) * factor
    result = (grad[...] * gain[...] - columns[:, 2:3] - unit * columns[:, 3:4]) * factor
    result = result.astype(NARROW)
    heads = len(outs)
    for pair in range(heads // 2):
        both = result[:, pair * 2 * HD : (pair + 1) * 2 * HD].T
        held[2 * pair] = both[:HD]
        held[2 * pair + 1] = both[HD:]
    for slot in range(heads):
        outs[slot][...] = held[seat[0] ^ slot]


def cut_heads(seat, grad, mixed, stats, gain, sums, heads, width):
    block = grad.shape[0]
    return local_call(
        functools.partial(cut_kernel, count=len(sums), width=width),
        "cut",
        [seat],
        [grad, mixed, stats, gain, *sums],
        [],
        [shaped((HD, block), NARROW)] * heads,
        [pltpu.VMEM((heads, HD, block), NARROW)],
        60,
    )


def attn_back_kernel(grads, rows, gain, bias, weight, product, lines, kept, sems):
    fetch_all(weight, kept, sems, 1)

    @pl.loop(0, product.shape[1] // SPAN)
    def _(step):
        cols = span_of(step)
        fetch(weight, kept, sems, step, 1).wait()
        total = 0.0
        for c in range(grads.shape[0]):
            total = total + lax.dot_general(
                grads[c], kept[c, cols, :], (((1,), (1,)), ((), ())), preferred_element_type=WIDE
            )
        product[:, cols] = total.astype(NARROW)
        unit = (rows[:, cols].astype(WIDE) - bias[:, cols]) / gain[:, cols]
        lines[0:1, cols] = jnp.sum(total * unit, axis=0, keepdims=True)
        lines[1:2, cols] = jnp.sum(total, axis=0, keepdims=True)


def attn_back_product(grads, rows, gain, bias, weight):
    count, depth = rows.shape
    return local_call(
        attn_back_kernel,
        "attn_back",
        [],
        [grads, rows, gain, bias],
        [weight],
        [shaped((count, depth), NARROW), shaped((2, depth), WIDE)],
        [
            pltpu.VMEM(weight.shape, NARROW),
            pltpu.SemaphoreType.DMA((depth // SPAN,)),
        ],
        60,
    )


def shards(
    inputs,
    segment_ids,
    cotangent,
    qkv_weight,
    qkv_bias,
    out_weight,
    out_bias,
    up_weight,
    up_bias,
    down_weight,
    down_bias,
    input_gain,
    input_bias,
    mixed_gain,
    mixed_bias,
    middle_gain,
    middle_bias,
    hidden_gain,
    hidden_bias,
    qkv_average,
    out_average,
    up_average,
    down_average,
    decay_rate,
):
    seq_count = lax.axis_size("seq")
    seq_rank = lax.axis_index("seq")
    local_rows = segment_ids.shape[0]
    model_width = inputs.shape[1]
    local_width = qkv_weight.shape[2]
    heads_here = local_width // HD
    team = heads_here
    teams = seq_count // team
    place = seq_rank % team
    home = seq_rank - place

    def trade(chunks):
        got = {m: hop(chunks[m], "seq", m, seq_count) for m in range(2, team)}
        got[1] = hop(after(chunks[1], got[2]), "seq", 1, seq_count)
        return [chunks[0]] + [got[m] for m in range(1, team)]

    row_index = seq_rank * local_rows + jnp.arange(local_rows, dtype=jnp.int32)
    documents = jnp.arange(COUNT, dtype=jnp.int32)
    member = segment_ids[:, None] == documents[None, :]
    first_all = jnp.min(jnp.where(member, row_index[:, None], LARGEST), axis=0)
    bit = 1
    while bit < seq_count:
        first_all = jnp.minimum(first_all, hop(first_all, "seq", bit, seq_count))
        bit *= 2

    def starts_of(rows):
        earlier = first_all[None, :] <= rows[:, None]
        return jnp.max(jnp.where(earlier, first_all[None, :], 0), axis=1)

    cosine, sine, growth = xpos_tables(row_index - starts_of(row_index), HD)
    shrink = 1.0 / growth
    straight = jnp.concatenate([cosine * growth] * 2 + [cosine * shrink] * 2, axis=1)
    crossed = jnp.concatenate(
        [-sine * growth, sine * growth, -sine * shrink, sine * shrink], axis=1
    )
    team_rows = home * local_rows + jnp.arange(team * local_rows, dtype=jnp.int32)
    team_starts = starts_of(team_rows).reshape(team, local_rows)
    spans = jnp.stack([jnp.min(team_starts, axis=1), jnp.max(team_starts, axis=1)], axis=1)
    info = jnp.concatenate(
        [jnp.stack([place, home]).astype(jnp.int32), spans.reshape(-1)]
    )
    team_starts = team_starts.reshape(team, 1, local_rows)
    seat = jnp.reshape(place, (1,)).astype(jnp.int32)

    tp_count = lax.axis_size("tp")
    tp_rank = lax.axis_index("tp")
    inner = tp_count // 2
    near_first = part_owners(0)
    far_first = part_owners(inner)

    def line(vector):
        return vector.astype(WIDE).reshape(1, -1)

    def exchange(values):
        mask = 1
        while 2 * mask < tp_count:
            values = values + hop(values, "tp", mask, tp_count)
            mask *= 2
        return [values, hop(values, "tp", mask, tp_count)]

    inputs_wide = inputs.astype(WIDE)
    input_normed, input_back = jax.vjp(
        norm_rows, inputs_wide, input_gain.astype(WIDE), input_bias.astype(WIDE)
    )
    attn_parts = gather_parts(input_normed.astype(NARROW))
    rate = decay_rate[0]
    seq_part = model_width // seq_count
    offset = seq_rank * seq_part

    def average(old, weight, axis):
        piece = lax.dynamic_slice_in_dim(weight, offset, seq_part, axis).astype(WIDE)
        return rate * old + (1.0 - rate) * piece

    qkv_new = average(qkv_average, qkv_weight, 1)
    out_new = average(out_average, out_weight, 1)
    up_new = average(up_average, up_weight, 0)
    down_new = average(down_average, down_weight, 1)
    attn_parts[0] = after(attn_parts[0], straight, crossed)

    def pack(parts, chairs, earlier=()):
        return pack_heads(
            seat, chairs, parts, qkv_weight, qkv_bias.astype(WIDE), straight, crossed, team, earlier
        )

    packed = pack(attn_parts[:inner], near_first)
    attn_parts[inner] = after(attn_parts[inner], *packed)
    *packs, attn_in = pack(attn_parts[inner:], far_first, packed)
    grad_rows = gather_rows(after(cotangent, packs[0]))
    chunks = trade(packs)
    everyone = None
    if teams > 1:
        rings = [[j + team * t for t in range(teams)] for j in range(team)]
        natural = jnp.stack(chunks)[jnp.arange(team) ^ place]
        everyone = lax.all_gather(
            natural, "seq", axis=0, tiled=True, axis_index_groups=rings
        )
    *mixed_out, mixed_wide, logs = attend_forward(info, team_starts, chunks, everyone, tp_count)
    mixed_got = trade(mixed_out)

    mixed_got[0] = after(mixed_got[0], grad_rows)
    mixed, mixed_sums = join_heads(seat, mixed_got)
    out_product, mixed_low, mixed_stats = mixed_out_product(
        mixed, exchange(mixed_sums), line(mixed_gain), line(mixed_bias), out_weight
    )
    grad_hidden = jnp.einsum(
        "rd,fd->rf", grad_rows, down_weight, preferred_element_type=WIDE
    ).astype(NARROW)
    summed = after(scatter_rows(out_product), grad_hidden, qkv_new, out_new, up_new, down_new)
    middle = inputs_wide + summed + out_bias.astype(WIDE)
    normed, middle_back = jax.vjp(
        norm_rows, middle, middle_gain.astype(WIDE), middle_bias.astype(WIDE)
    )
    ffn_parts = gather_parts(normed.astype(NARROW))
    gain_line = line(hidden_gain)

    def up(parts, chairs, earlier=()):
        return up_product(
            chairs, parts, up_weight, line(up_bias), gain_line, grad_hidden, earlier
        )

    *up_near, ffn_near, sums_near = up(ffn_parts[:inner], near_first)
    ffn_parts[inner] = after(ffn_parts[inner], sums_near)
    *up_far, ffn_in, sums = up(ffn_parts[inner:], far_first, (ffn_near, sums_near))
    hidden_low, grad_up, ffn_back, hidden_lines = ffn_back_product(
        near_first,
        exchange(sums),
        up_near,
        up_far,
        grad_hidden,
        gain_line,
        line(hidden_bias),
        up_weight,
        FF,
    )
    upbias_part, hiddengain_part, hiddenbias_part = hidden_lines
    down_product = jnp.dot(hidden_low, down_weight, preferred_element_type=WIDE).astype(NARROW)
    late_rows = after(grad_rows, down_product)
    down_sent = send_gradient(hidden_low, late_rows, seq_rank, seq_count, True)
    up_sent = send_gradient(after(grad_up, down_product)[None], ffn_in, seq_rank, seq_count, False)
    summed = after(scatter_rows(ffn_back), down_sent, up_sent)
    norm_grad, middlegain_part, middlebias_part = middle_back(summed)
    grad_middle = cotangent.astype(WIDE) + norm_grad
    grad_low = grad_middle.astype(NARROW)
    middle_parts = gather_parts(grad_low)
    down_got = after(hop(down_sent, "seq", 1, seq_count), grad_low)
    up_got = hop(up_sent, "seq", 1, seq_count)
    down_pieces = keep_gradient(hidden_low, grad_rows, down_got, seq_rank, seq_count, True, True)
    up_pieces = keep_gradient(
        grad_up[None], ffn_in, up_got, seq_rank, seq_count, False, True
    )
    down_pieces = start_gradient(down_pieces, seq_count)
    middle_parts[-1] = after(middle_parts[-1], *up_pieces, *down_pieces)
    outbias_part = jnp.sum(grad_low, axis=0, dtype=WIDE)
    downbias_part = jnp.sum(cotangent, axis=0, dtype=WIDE)
    grad_mixed_norm, grad_mixed_rows, back_sums, mixed_lines = mixed_back_product(
        near_first,
        middle_parts,
        mixed,
        mixed_stats,
        line(mixed_gain),
        out_weight,
    )
    mixedgain_part, mixedbias_part = mixed_lines
    grad_cuts = cut_heads(
        seat,
        grad_mixed_norm,
        mixed,
        mixed_stats,
        line(mixed_gain),
        exchange(back_sums),
        team,
        model_width,
    )
    down_pieces = list(down_pieces)
    for slot in range(1, len(down_pieces)):
        down_pieces[slot] = after(down_pieces[slot], grad_mixed_norm)
    down_rest = finish_gradient(down_pieces, seq_count)
    grad_chunks = trade(grad_cuts)
    up_pieces = list(up_pieces)
    for slot in range(1, len(up_pieces)):
        up_pieces[slot] = after(up_pieces[slot], *grad_chunks)
    up_pieces = list(start_gradient(up_pieces, seq_count))
    layer_out = (
        middle
        + scatter_rows(after(down_product, grad_mixed_norm))
        + down_bias.astype(WIDE)
    ).astype(NARROW)
    pieces = attend_backward(
        info,
        team_starts,
        logs,
        mixed_wide,
        chunks,
        grad_chunks,
        everyone,
        tp_count,
    )
    pieces = list(pieces)
    down_grad = add_gradient(down_rest, pieces[0])
    arrived = list(down_rest[1:4:2]) + up_pieces[1:3]
    pieces = [after(piece, *arrived) for piece in pieces]
    out_sent = send_gradient(mixed_low, after(grad_mixed_rows, pieces[0]), seq_rank, seq_count, True)
    out_got = hop(out_sent, "seq", 1, seq_count)
    out_pieces = keep_gradient(mixed_low, grad_mixed_rows, out_got, seq_rank, seq_count, True)
    pieces[0] = after(pieces[0], layer_out)
    if teams > 1:
        natural = lax.psum_scatter(
            pieces[0], "seq", scatter_dimension=0, tiled=True, axis_index_groups=rings
        )
        pieces = [
            lax.dynamic_index_in_dim(natural, place ^ m, 0, keepdims=False) for m in range(team)
        ]
    parts_got = trade(pieces)
    parts_got[0] = after(parts_got[0], down_grad, *out_pieces)
    for slot in range(1, len(up_pieces)):
        up_pieces[slot] = after(up_pieces[slot], *parts_got)
    up_rest = finish_gradient(up_pieces, seq_count)
    out_pieces = list(out_pieces)
    for slot in range(1, len(out_pieces)):
        out_pieces[slot] = after(out_pieces[slot], *parts_got)
    out_grad = add_gradient(finish_gradient(out_pieces, seq_count))
    stacked, qkvbias_part = unpack_heads(seat, straight, crossed, parts_got)
    qkv_got = hop(send_gradient(stacked, attn_in, seq_rank, seq_count, False), "seq", 1, seq_count)
    attn_back, attn_lines = attn_back_product(
        stacked, attn_in, line(input_gain), line(input_bias), qkv_weight
    )
    inputgain_part, inputbias_part = attn_lines
    grad_attn_in = scatter_rows(attn_back)
    qkv_got = after(qkv_got, out_grad, attn_back, *(up_rest[1:4:2] if isinstance(up_rest, tuple) else ()))
    qkv_pieces = keep_gradient(stacked, attn_in, qkv_got, seq_rank, seq_count, False, True)
    qkv_pieces = start_gradient(qkv_pieces, seq_count)
    qkv_sent = []
    qkv_grad = add_gradient(finish_gradient(qkv_pieces, seq_count, qkv_sent))

    def spread_norms(parts):
        both = jnp.stack(parts).reshape(len(parts), seq_count, tp_count, -1)
        mine = tp_scatter(both.transpose(2, 1, 0, 3))
        return mine.reshape(seq_count, -1)

    inputgain_part = after(inputgain_part, qkv_pieces[0])
    vectors = jnp.concatenate(
        [
            item.reshape(seq_count, -1)
            for item in (
                upbias_part,
                hiddengain_part,
                hiddenbias_part,
                mixedgain_part,
                mixedbias_part,
                qkvbias_part[0],
                qkvbias_part[1],
                qkvbias_part[2],
            )
        ]
        + [
            spread_norms(
                [
                    middlegain_part,
                    middlebias_part,
                    outbias_part,
                    downbias_part,
                    inputgain_part,
                    inputbias_part,
                ]
            )
        ],
        axis=1,
    )
    vector_sums = vector_scatter(after(vectors, *qkv_sent), seq_rank, seq_count)
    up_grad = add_gradient(up_rest, vector_sums)[0]
    grad_attn_in = after(grad_attn_in, vector_sums)
    grad_input_norm, _, _ = input_back(grad_attn_in)
    input_grad = (grad_middle + grad_input_norm).astype(NARROW)
    narrow_part = local_width // seq_count
    wide_part = up_bias.shape[0] // seq_count
    norm_part = model_width // (seq_count * lax.axis_size("tp"))

    def cuts(vector, widths):
        begin = 0
        pieces = []
        for width in widths:
            pieces.append(vector[begin : begin + width])
            begin += width
        return pieces

    (
        upbias_grad,
        hiddengain_grad,
        hiddenbias_grad,
        mixedgain_grad,
        mixedbias_grad,
        q_bias,
        k_bias,
        v_bias,
        middlegain_grad,
        middlebias_grad,
        outbias_grad,
        downbias_grad,
        inputgain_grad,
        inputbias_grad,
    ) = cuts(vector_sums, (wide_part,) * 3 + (narrow_part,) * 5 + (norm_part,) * 6)
    return (
        layer_out,
        input_grad,
        qkv_grad,
        jnp.stack([q_bias, k_bias, v_bias]),
        out_grad,
        outbias_grad,
        up_grad,
        upbias_grad,
        down_grad,
        downbias_grad,
        inputgain_grad,
        inputbias_grad,
        mixedgain_grad,
        mixedbias_grad,
        middlegain_grad,
        middlebias_grad,
        hiddengain_grad,
        hiddenbias_grad,
        qkv_new,
        out_new,
        up_new,
        down_new,
    )


def solution(mesh):
    in_specs = (
        P(("seq", "tp"), None),
        P("seq"),
        P(("seq", "tp"), None),
        P(None, None, "tp"),
        P(None, "tp"),
        P("tp", None),
        P(),
        P(None, "tp"),
        P("tp"),
        P("tp", None),
        P(),
        P(),
        P(),
        P("tp"),
        P("tp"),
        P(),
        P(),
        P("tp"),
        P("tp"),
        P(None, "seq", "tp"),
        P("tp", "seq"),
        P("seq", "tp"),
        P("tp", "seq"),
        P(),
    )
    out_specs = (
        P(("seq", "tp"), None),
        P(("seq", "tp"), None),
        P(None, "seq", "tp"),
        P(None, ("tp", "seq")),
        P("tp", "seq"),
        P(("seq", "tp")),
        P("seq", "tp"),
        P(("tp", "seq")),
        P("tp", "seq"),
        P(("seq", "tp")),
        P(("seq", "tp")),
        P(("seq", "tp")),
        P(("tp", "seq")),
        P(("tp", "seq")),
        P(("seq", "tp")),
        P(("seq", "tp")),
        P(("tp", "seq")),
        P(("tp", "seq")),
        P(None, "seq", "tp"),
        P("tp", "seq"),
        P("seq", "tp"),
        P("tp", "seq"),
    )
    return jax.shard_map(shards, mesh=mesh, in_specs=in_specs, out_specs=out_specs, check_vma=False)
```

```python
import functools
import math

import jax
import jax.numpy as jnp
from jax import lax
from jax.experimental import pallas as pl
from jax.experimental.pallas import tpu as pltpu
from jax.sharding import PartitionSpec as P

FF = 8192
COUNT = 16
HD = 64

SCALE = 0.125
LOG2E = 1.4426950408889634
EPSILON = 1e-05
OUTSIDE = -2e30
LOWEST = -1e30
LARGEST = 1 << 30
WIDE = jnp.float32
NARROW = jnp.bfloat16
MIB = 1 << 20
SMALL = pl.CostEstimate(flops=1 << 20, bytes_accessed=1 << 16, transcendentals=0)


def xpos_tables(positions, head_size):
    half = head_size // 2
    index = jnp.arange(half, dtype=jnp.float32)
    frequency = jnp.exp(index * (-2.0 * math.log(10000.0) / head_size))
    zeta = (index * (2.0 / head_size) + 0.4) / 1.4
    places = positions.astype(jnp.float32)[:, None]
    angle = places * frequency[None, :]
    growth = jnp.exp(places * (jnp.log(zeta)[None, :] / 512.0))
    return (jnp.cos(angle), jnp.sin(angle), growth)


def norm_rows(values, gain, shift):
    center = jnp.mean(values, axis=-1, keepdims=True)
    spread = jnp.mean(values * values, axis=-1, keepdims=True) - center * center
    return (values - center) * lax.rsqrt(spread + EPSILON) * gain + shift


def exact_gelu(values):
    return jax.nn.gelu(values, approximate=False)


def gather_rows(values):
    return lax.all_gather(values, "tp", axis=0, tiled=True)


def ring_order(count):
    return [0] + list(range(1, count, 2)) + list(range(2, count, 2))[::-1]


def gather_parts(values):
    order = ring_order(lax.axis_size("tp"))
    parts = [values]
    for _ in order[1:]:
        pairs = [(a, b) for a, b in zip(order, order[1:] + order[:1])]
        parts.append(lax.ppermute(parts[-1], "tp", pairs))
    return parts


def part_owners(first):
    order = ring_order(lax.axis_size("tp"))
    count = len(order)
    rows = [
        [order[(order.index(rank) - first - slot) % count] for slot in range(count)]
        for rank in range(count)
    ]
    table = jnp.array(rows, jnp.int32)
    return lax.dynamic_index_in_dim(table, lax.axis_index("tp"), 0, keepdims=False)


def scatter_rows(values):
    return lax.psum_scatter(values.astype(NARROW), "tp", scatter_dimension=0, tiled=True).astype(WIDE)


def hop(values, axis, mask, count):
    return lax.ppermute(values, axis, [(i, i ^ mask) for i in range(count)])


def tp_total(values):
    count = lax.axis_size("tp")
    if count & (count - 1):
        return lax.psum(values, "tp")
    total = values
    for mask in range(1, count):
        total = total + hop(values, "tp", mask, count)
    return total


def after(value, *others):
    return lax.optimization_barrier((value,) + others)[0]


def vector_scatter(values, rank, count):
    bit = count // 2
    while bit:
        pair = values.reshape(2, bit, -1)
        mine = (rank & bit) // bit
        send = lax.dynamic_index_in_dim(pair, 1 - mine, 0, keepdims=False)
        keep = lax.dynamic_index_in_dim(pair, mine, 0, keepdims=False)
        values = keep + hop(send, "seq", bit, count)
        bit //= 2
    return values.reshape(-1)


def tp_scatter(values):
    count = lax.axis_size("tp")
    rank = lax.axis_index("tp")
    if count & (count - 1):
        return lax.psum_scatter(values, "tp", scatter_dimension=0)
    total = lax.dynamic_index_in_dim(values, rank, 0, keepdims=False)
    for mask in range(1, count):
        part = lax.dynamic_index_in_dim(values, rank ^ mask, 0, keepdims=False)
        total = total + hop(part, "tp", mask, count)
    return total


def sent_kernel(place, left, right, out, *, tall):
    if tall:
        out[0] = lax.dot_general(
            left[...], right[...], (((0,), (0,)), ((), ())), preferred_element_type=WIDE
        ).astype(NARROW)
    else:
        turned = right[...].T
        for c in range(left.shape[0]):
            out[0, c] = jnp.dot(turned, left[c], preferred_element_type=WIDE).astype(NARROW)


def kept_kernel(seat, left, right, got, *outs, tall, crossing):
    slots = pl.num_programs(0)
    step = pl.program_id(0)
    if tall:
        total = lax.dot_general(
            left[...], right[...], (((0,), (0,)), ((), ())), preferred_element_type=WIDE
        ) + got[0].astype(WIDE)
        rows = total.shape[0]
    else:
        turned = right[...].T
        total = jnp.stack(
            [
                jnp.dot(turned, left[c], preferred_element_type=WIDE) + got[0, c].astype(WIDE)
                for c in range(left.shape[0])
            ]
        )
        rows = total.shape[1]

    def at(slot):
        return pl.when(step == (slot - 1) % slots)

    @at(0)
    def _():
        outs[0][...] = total

    if crossing:
        cut = rows // 2
        low = total.astype(NARROW)
        first, second = (low[:cut], low[cut:]) if tall else (low[:, :cut], low[:, cut:])
        across, along, keep_first, keep_second = outs[1:]

        @at(1)
        def _():
            across[0] = first
            keep_second[...] = second

        @at(2)
        def _():
            keep_first[...] = first
            along[0] = second

        @at(3)
        def _():
            across[1] = first
            along[1] = second

    else:
        for slot in range(1, len(outs)):

            @at(slot)
            def _():
                outs[slot][...] = total.astype(NARROW)


def gradient_blocks(seat, left, right, count, tall, got=None, crossing=False):
    rows = right.shape[0]
    part = right.shape[1] // count
    slots = count // 2
    if tall:
        block = (left.shape[1], part)
        half = (left.shape[1] // 2, part)
    else:
        block = (left.shape[0], part, left.shape[2])
        half = (left.shape[0], part // 2, left.shape[2])
    first = 0 if got is None else 1
    slot_of = lambda k: (k + first) & (slots - 1)
    left_spec = pl.BlockSpec(left.shape, lambda k, seat: (0,) * left.ndim)
    if part % 128:
        order = 2 * (jnp.arange(slots, dtype=jnp.int32) ^ seat[0]) + seat[1]
        right = right.reshape(rows, count, part)[:, order].transpose(1, 0, 2)
        right_spec = pl.BlockSpec((None, rows, part), lambda k, seat: (slot_of(k), 0, 0))
    else:
        right_spec = pl.BlockSpec(
            (rows, part), lambda k, seat: (0, 2 * (slot_of(k) ^ seat[0]) + seat[1])
        )

    def fixed(shape):
        return pl.BlockSpec(shape, lambda k, seat: (0,) * len(shape))

    block_spec = pl.BlockSpec((1,) + block, lambda k, seat: (slot_of(k),) + (0,) * len(block))
    if got is None:
        shapes = [jax.ShapeDtypeStruct((slots,) + block, NARROW)]
        specs = [block_spec]
    else:
        rest = [(2,) + half, (2,) + half, half, half] if crossing else [block] * (slots - 1)
        shapes = [jax.ShapeDtypeStruct(block, WIDE)]
        shapes += [jax.ShapeDtypeStruct(shape, NARROW) for shape in rest]
        specs = [fixed(shape.shape) for shape in shapes]
    kernel = (
        functools.partial(sent_kernel, tall=tall)
        if got is None
        else functools.partial(kept_kernel, tall=tall, crossing=crossing)
    )
    return pl.pallas_call(
        kernel,
        name="sent" if got is None else "kept",
        grid_spec=pltpu.PrefetchScalarGridSpec(
            num_scalar_prefetch=1,
            grid=(slots,),
            in_specs=[left_spec, right_spec] + ([] if got is None else [block_spec]),
            out_specs=tuple(specs),
        ),
        out_shape=tuple(shapes),
        compiler_params=params(40),
        cost_estimate=SMALL,
    )(seat, left, right, *([] if got is None else [got]))


def send_gradient(left, right, rank, count, tall):
    seat = jnp.stack([rank >> 1, 1 - (rank & 1)])
    return gradient_blocks(seat, left, right, count, tall)[0]


def keep_gradient(left, right, got, rank, count, tall, crossing=False):
    seat = jnp.stack([rank >> 1, rank & 1])
    return gradient_blocks(
        seat, left, right, count, tall, got, crossing=crossing and count == 8
    )


def add_gradient(rest, *earlier):
    if isinstance(rest, list):
        total = after(rest[0], *earlier) if earlier else rest[0]
        for got in rest[1:]:
            total = total + got.astype(WIDE)
        return total
    total, first, first_own, second, second_own, axis = rest
    if earlier:
        total = after(total, *earlier)
    first = first.astype(WIDE) + first_own.astype(WIDE)
    second = second.astype(WIDE) + second_own.astype(WIDE)
    return total + jnp.concatenate([first, second], axis=axis)


def start_gradient(pieces, count):
    if count != 8:
        return pieces
    total, across, along, keep_first, keep_second = pieces
    return total, hop(across, "seq", 2, count), hop(along, "seq", 4, count), keep_first, keep_second


def finish_gradient(pieces, count, sent=None):
    total = pieces[0]
    if count == 8 and pieces[1].ndim > total.ndim:
        _, across, along, keep_first, keep_second = pieces
        axis = total.ndim - 2
        first = (keep_first.astype(WIDE) + across[1].astype(WIDE)).astype(NARROW)
        second = (keep_second.astype(WIDE) + along[1].astype(WIDE)).astype(NARROW)
        if sent is not None:
            sent += [first, second]
        first = hop(first, "seq", 4, count)
        second = hop(second, "seq", 2, count)
        return total, first, across[0], second, along[0], axis
    return [total] + [hop(pieces[slot], "seq", 2 * slot, count) for slot in range(1, len(pieces))]


def scalar_spec():
    return pl.BlockSpec(memory_space=pltpu.SMEM)


def full_spec(array):
    return pl.BlockSpec(array.shape, lambda i: (0,) * len(array.shape))


def local_call(kernel, name, scalars, inputs, heavy, outs, scratch, mib):
    return pl.pallas_call(
        kernel,
        name=name,
        grid=(1,),
        out_shape=tuple(outs),
        in_specs=[scalar_spec()] * len(scalars)
        + [full_spec(item) for item in inputs]
        + [pl.BlockSpec(memory_space=pl.ANY)] * len(heavy),
        out_specs=tuple(full_spec(item) for item in outs),
        scratch_shapes=list(scratch),
        compiler_params=params(mib),
        cost_estimate=SMALL,
    )(*scalars, *inputs, *heavy)


def resident_call(kernel, name, scalars, remote, inputs, outs, remote_outs, scratch, mib):
    return pl.pallas_call(
        kernel,
        name=name,
        out_shape=tuple(outs) + tuple(remote_outs),
        in_specs=[scalar_spec()] * len(scalars)
        + [pl.BlockSpec(memory_space=pl.ANY)] * len(remote)
        + [pl.BlockSpec(memory_space=pltpu.VMEM)] * len(inputs),
        out_specs=(pl.BlockSpec(memory_space=pltpu.VMEM),) * len(outs)
        + (pl.BlockSpec(memory_space=pl.ANY),) * len(remote_outs),
        scratch_shapes=list(scratch),
        compiler_params=params(mib),
        cost_estimate=SMALL,
    )(*scalars, *remote, *inputs)


def shaped(shape, dtype):
    return jax.ShapeDtypeStruct(tuple(shape), dtype)


SPAN = 256


def span_of(step):
    return pl.ds(pl.multiple_of(step * SPAN, SPAN), SPAN)


def fetch(source, held, sems, step, axis):
    where = (slice(None),) * axis + (span_of(step),)
    return pltpu.make_async_copy(source.at[where], held.at[where], sems.at[step])


def fetch_all(source, held, sems, axis):
    for step in range(source.shape[axis] // SPAN):
        fetch(source, held, sems, step, axis).start()


def params(mib):
    return pltpu.CompilerParams(vmem_limit_bytes=mib * MIB)


def turn_packed(values, straight, crossed):
    lane = lax.broadcasted_iota(jnp.int32, values.shape, 1)
    ahead = pltpu.roll(values, 2 * HD - HD // 2, 1)
    behind = pltpu.roll(values, HD // 2, 1)
    partner = jnp.where((lane & (HD // 2)) == 0, ahead, behind)
    return values * straight + partner * crossed


def rows_at(owner, rows):
    return pl.ds(pl.multiple_of(owner * rows, rows), rows)


def pack_kernel(place, owners, *refs, parts, heads, merge):
    rows_in = refs[:parts]
    at = parts
    if merge:
        earlier, earlier_rows = refs[at : at + 2]
        at += 2
    sources = refs[at : at + 4]
    at += 4
    if merge:
        outs, rows_out = refs[at : at + heads], refs[at + heads]
    else:
        out, rows_out = refs[at], refs[at + 1]
    if merge:
        held_before, rows_before, *rest = refs[-10:]
    else:
        rest = refs[-8:]
    weight, bias, straight, crossed, rows, held, sems, more_sems = rest
    count = weight.shape[0]
    loads = [
        pltpu.make_async_copy(sources[0].at[c], weight.at[c], more_sems.at[c]) for c in range(count)
    ] + [
        pltpu.make_async_copy(source, target, more_sems.at[count + k])
        for k, (source, target) in enumerate(zip(sources[1:], (bias, straight, crossed)))
    ]
    part = rows_in[0].shape[0]
    half = part // 2
    size = part + half
    incoming = [
        pltpu.make_async_copy(rows_in[i], rows.at[i * part : (i + 1) * part, :], sems.at[0, i])
        for i in range(parts)
    ]
    outgoing = []

    def send(source, target, *where):
        copy = pltpu.make_async_copy(source, target, sems.at[where])
        copy.start()
        outgoing.append(copy)

    for copy in incoming + loads:
        copy.start()
    for copy in incoming:
        copy.wait()
    if merge:
        before = [
            pltpu.make_async_copy(earlier, held_before, sems.at[0, 3 * parts]),
            pltpu.make_async_copy(earlier_rows, rows_before, sems.at[0, 3 * parts + 1]),
        ]
        for copy in before:
            copy.start()
    for i in range(parts):
        mine = rows_at(owners[i], part) if merge else slice(i * part, (i + 1) * part)
        send(rows.at[i * part : (i + 1) * part, :], rows_out.at[mine, :], 0, 2 * parts + i)
    for copy in loads[count:]:
        copy.wait()
    straight, crossed = (
        jnp.concatenate([table[rows_at(owners[i], part), :] for i in range(parts)], axis=0)
        for table in (straight, crossed)
    )
    projected = []
    for c in range(count):
        loads[c].wait()
        projected.append(
            jnp.dot(rows[...], weight[c], preferred_element_type=WIDE) + bias[c : c + 1, :]
        )
    for step in range(weight.shape[2] // SPAN):
        cols = slice(step * SPAN, (step + 1) * SPAN)
        query, key, value = (item[:, cols] for item in projected)
        for side in range(SPAN // HD):
            lanes = slice(side * HD, (side + 1) * HD)
            head = step * (SPAN // HD) + side
            both = jnp.concatenate([query[:, lanes], key[:, lanes]], axis=1)
            both = turn_packed(both, straight, crossed).astype(NARROW)
            for i in range(parts):
                held[i, head, :part, :] = both[i * part : (i + 1) * part]
                one = value[i * part : (i + 1) * part, lanes]
                held[i, head, part:, :] = jnp.concatenate(
                    [one[:half], one[half:]], axis=1
                ).astype(NARROW)
    if merge:
        for copy in before:
            copy.wait()
        for i in range(parts):
            other = owners[parts + i]
            send(
                rows_before.at[i * part : (i + 1) * part, :],
                rows_out.at[rows_at(other, part), :],
                0,
                parts + i,
            )
            for slot in range(heads):
                send(
                    held_before.at[i, place[0] ^ slot],
                    outs[slot].at[rows_at(other, size), :],
                    1 + i,
                    slot,
                )
                send(
                    held.at[i, place[0] ^ slot],
                    outs[slot].at[rows_at(owners[i], size), :],
                    1 + parts + i,
                    slot,
                )
    else:
        for i in range(parts):
            send(held.at[i], out.at[i], 1, i)
    for copy in outgoing:
        copy.wait()


def pack_heads(place, owners, parts, weight, bias, straight, crossed, heads, earlier=()):
    count = len(parts)
    part, depth = parts[0].shape
    size = part + part // 2
    if earlier:
        outs = [shaped((2 * count * size, 2 * HD), NARROW)] * heads
        outs += [shaped((2 * count * part, depth), NARROW)]
    else:
        outs = [shaped((count, heads, size, 2 * HD), NARROW), shaped((count * part, depth), NARROW)]
    return resident_call(
        functools.partial(pack_kernel, parts=count, heads=heads, merge=bool(earlier)),
        "pack",
        [place, owners],
        [*parts, *earlier, weight, bias, straight, crossed],
        [],
        [],
        outs,
        [pltpu.VMEM(item.shape, NARROW) for item in earlier]
        + [
            pltpu.VMEM(weight.shape, NARROW),
            pltpu.VMEM(bias.shape, WIDE),
            pltpu.VMEM(straight.shape, WIDE),
            pltpu.VMEM(crossed.shape, WIDE),
            pltpu.VMEM((count * part, depth), NARROW),
            pltpu.VMEM((count, heads, size, 2 * HD), NARROW),
            pltpu.SemaphoreType.DMA((1 + 2 * count, max(heads, 3 * count + 2))),
            pltpu.SemaphoreType.DMA((weight.shape[0] + 3,)),
        ],
        54,
    )


def split_chunk(chunk):
    block = chunk.shape[0] * 2 // 3
    both = chunk[:block, :]
    packed = chunk[block:, :]
    value = jnp.concatenate([packed[:, :HD], packed[:, HD:]], axis=0)
    return both[:, :HD], both[:, HD:], value


def allowed_mask(begin, q_begin, starts, shape):
    keys = begin + lax.broadcasted_iota(jnp.int32, shape, 0)
    queries = q_begin + lax.broadcasted_iota(jnp.int32, shape, 1)
    return (keys >= starts) & (keys <= queries)


def key_ranges(info, index, first_block, block):
    here = first_block + index
    low = info[2 + 2 * index] // block
    clear = jnp.minimum((info[3 + 2 * index] + block - 1) // block, here)
    return low, clear, here


def forward_kernel(info, starts, *refs, groups, spread, parts):
    count = groups
    chunks = refs[:count]
    at = count + (1 if spread else 0)
    outs = refs[at : at + count]
    mixed, logs, keys, values, queries = refs[at + count :]
    me = info[0]
    first_block = info[1]
    block = starts.shape[2]
    part = block // parts
    size = part + part // 2
    for slot in range(parts * count):
        side = slot // count
        query, key, value = split_chunk(chunks[slot % count][side * size : (side + 1) * size, :])
        place = me ^ (slot % count)
        rows = slice(side * part, (side + 1) * part)
        queries[place, :, rows] = query.T
        if not spread:
            keys[place, rows, :] = key
            values[place, :, rows] = value.T
    if spread:

        @pl.loop(0, keys.shape[0])
        def _(kb):
            for side in range(parts):
                _, key, value = split_chunk(refs[count][kb, side * size : (side + 1) * size, :])
                rows = slice(side * part, (side + 1) * part)
                keys[kb, rows, :] = key
                values[kb, :, rows] = value.T

    @pl.loop(0, count)
    def _(index):
        low, clear, here = key_ranges(info, index, first_block, block)
        query = queries[index]
        begins = starts[index]

        def step(kb, carry, masked):
            top, total, accum = carry
            cuts = [slice(i * block // 4, (i + 1) * block // 4) for i in range(4)]
            raws = [
                jnp.dot(keys[kb], query[:, cut], preferred_element_type=WIDE) for cut in cuts
            ]
            results = []
            for cut, raw in zip(cuts, raws):
                if masked:
                    mask = allowed_mask(
                        kb * block, here * block + cut.start, begins[:, cut], raw.shape
                    )
                    raw = jnp.where(mask, raw, OUTSIDE)
                fresh = jnp.maximum(
                    top[:, cut], jnp.max(raw, axis=0, keepdims=True) * (SCALE * LOG2E)
                )
                kept = jnp.exp2(raw * (SCALE * LOG2E) - fresh)
                fade = jnp.exp2(top[:, cut] - fresh)
                results.append(
                    (
                        fresh,
                        total[:, cut] * fade + jnp.sum(kept, axis=0, keepdims=True),
                        accum[:, cut] * fade
                        + jnp.dot(values[kb], kept.astype(NARROW), preferred_element_type=WIDE),
                    )
                )
            return tuple(jnp.concatenate(item, axis=1) for item in zip(*results))

        carry = (
            jnp.full((1, block), LOWEST, WIDE),
            jnp.zeros((1, block), WIDE),
            jnp.zeros((HD, block), WIDE),
        )
        carry = lax.fori_loop(low, clear, functools.partial(step, masked=True), carry)
        carry = lax.fori_loop(clear, here, functools.partial(step, masked=False), carry)
        top, total, accum = step(here, carry, True)
        mixed[index] = accum / total
        logs[index] = top + jnp.log2(total)

    for slot in range(count):
        outs[slot][...] = mixed[me ^ slot].astype(NARROW)


def attend_forward(info, starts, chunks, everyone, parts):
    count = len(chunks)
    block = starts.shape[2]
    spread = everyone is not None
    blocks = everyone.shape[0] if spread else count
    return local_call(
        functools.partial(forward_kernel, groups=count, spread=spread, parts=parts),
        "forward",
        [info],
        [starts, *chunks] + ([everyone] if spread else []),
        [],
        [shaped((HD, block), NARROW)] * count
        + [shaped((count, HD, block), WIDE), shaped((count, 1, block), WIDE)],
        [
            pltpu.VMEM((blocks, block, HD), NARROW),
            pltpu.VMEM((blocks, HD, block), NARROW),
            pltpu.VMEM((count, HD, block), NARROW),
        ],
        60,
    )


def backward_kernel(info, starts, logs, mixed, *refs, groups, spread, parts):
    count = groups
    chunks = refs[:count]
    grads = refs[count : 2 * count]
    at = 2 * count
    if spread:
        everyone = refs[at]
        at += 1
    outs = refs[at : at + (1 if spread else count)]
    at += len(outs)
    keys, keys_up, values, queries, queries_up, downs, downs_up, key_sum, value_sum, query_sum = refs[at:]
    me = info[0]
    first_block = info[1]
    block = starts.shape[2]
    blocks = keys.shape[0]
    part = block // parts
    half = block // 2
    size = part + part // 2
    for slot in range(parts * count):
        side = slot // count
        query, key, value = split_chunk(chunks[slot % count][side * size : (side + 1) * size, :])
        place = me ^ (slot % count)
        rows = slice(side * part, (side + 1) * part)
        queries[place, rows, :] = query
        queries_up[place, :, rows] = query.T
        if not spread:
            keys[place, rows, :] = key
            keys_up[place, :, rows] = key.T
            values[place, rows, :] = value
    for slot in range(count):
        down = grads[slot][...]
        downs_up[me ^ slot] = down
        downs[me ^ slot] = down.T
    if spread:

        @pl.loop(0, blocks)
        def _(kb):
            for side in range(parts):
                _, key, value = split_chunk(everyone[kb, side * size : (side + 1) * size, :])
                rows = slice(side * part, (side + 1) * part)
                keys[kb, rows, :] = key
                keys_up[kb, :, rows] = key.T
                values[kb, rows, :] = value

    key_sum[...] = jnp.zeros_like(key_sum)
    value_sum[...] = jnp.zeros_like(value_sum)

    @pl.loop(0, count)
    def _(index):
        low, clear, here = key_ranges(info, index, first_block, block)
        query_up = queries_up[index]
        down_up = downs_up[index]
        begins = starts[index]
        log = logs[index]
        delta = jnp.sum(down_up.astype(WIDE) * mixed[index], axis=0, keepdims=True)

        def step(kb, accum, masked):
            raw = jnp.dot(keys[kb], query_up, preferred_element_type=WIDE)
            probs = jnp.exp2(raw * (SCALE * LOG2E) - log)
            if masked:
                probs = jnp.where(
                    allowed_mask(kb * block, here * block, begins, raw.shape), probs, 0.0
                )
            grad_probs = jnp.dot(values[kb], down_up, preferred_element_type=WIDE)
            grad_scores = (probs * (grad_probs - delta)).astype(NARROW)
            value_sum[kb] += jnp.dot(
                probs.astype(NARROW), downs[index], preferred_element_type=WIDE
            )
            key_sum[kb] += jnp.dot(grad_scores, queries[index], preferred_element_type=WIDE)
            return accum + jnp.dot(keys_up[kb], grad_scores, preferred_element_type=WIDE)

        accum = jnp.zeros((HD, block), WIDE)
        accum = lax.fori_loop(low, clear, functools.partial(step, masked=True), accum)
        accum = lax.fori_loop(clear, here, functools.partial(step, masked=False), accum)
        query_sum[index] = step(here, accum, True)

    def packed(kb, query):
        both = jnp.concatenate([query, key_sum[kb]], axis=1) * SCALE
        one = value_sum[kb]
        return both.astype(NARROW), jnp.concatenate([one[:half], one[half:]], axis=1).astype(NARROW)

    if spread:

        @pl.loop(0, blocks)
        def _(kb):
            inside = (kb >= first_block) & (kb < first_block + count)
            query = query_sum[jnp.clip(kb - first_block, 0, count - 1)]
            both, value = packed(kb, jnp.where(inside, query, 0.0).T)
            outs[0][kb, :block, :] = both
            outs[0][kb, block:, :] = value

    else:
        for slot in range(count):
            place = me ^ slot
            both, value = packed(place, query_sum[place].T)
            outs[slot][:block, :] = both
            outs[slot][block:, :] = value


def attend_backward(info, starts, logs, mixed, chunks, grads, everyone, parts):
    count = len(chunks)
    block = starts.shape[2]
    spread = everyone is not None
    blocks = everyone.shape[0] if spread else count
    rows = block + block // 2
    outs = [shaped((blocks, rows, 2 * HD), NARROW)] if spread else [shaped((rows, 2 * HD), NARROW)] * count
    tall = (block, HD)
    flat = (HD, block)
    return local_call(
        functools.partial(backward_kernel, groups=count, spread=spread, parts=parts),
        "backward",
        [info],
        [starts, logs, mixed, *chunks, *grads] + ([everyone] if spread else []),
        [],
        outs,
        [
            pltpu.VMEM((blocks,) + tall, NARROW),
            pltpu.VMEM((blocks,) + flat, NARROW),
            pltpu.VMEM((blocks,) + tall, NARROW),
            pltpu.VMEM((count,) + tall, NARROW),
            pltpu.VMEM((count,) + flat, NARROW),
            pltpu.VMEM((count,) + tall, NARROW),
            pltpu.VMEM((count,) + flat, NARROW),
            pltpu.VMEM((blocks,) + tall, WIDE),
            pltpu.VMEM((blocks,) + tall, WIDE),
            pltpu.VMEM((count,) + flat, WIDE),
        ],
        60,
    )


def join_kernel(place, *refs):
    count = len(refs) - 3
    chunks, out, sums, held = refs[:count], refs[count], refs[count + 1], refs[count + 2]
    me = place[0]
    total = 0.0
    squares = 0.0
    for slot in range(count):
        held[me ^ slot] = chunks[slot][...]
        wide = chunks[slot][...].astype(WIDE)
        total = total + jnp.sum(wide, axis=0, keepdims=True)
        squares = squares + jnp.sum(wide * wide, axis=0, keepdims=True)
    sums[0:1, :] = total
    sums[1:2, :] = squares
    for pair in range(count // 2):
        both = jnp.concatenate([held[2 * pair], held[2 * pair + 1]], axis=0)
        out[:, pair * 2 * HD : (pair + 1) * 2 * HD] = both.T


def join_heads(place, chunks):
    count = len(chunks)
    block = chunks[0].shape[1]
    return local_call(
        join_kernel,
        "join",
        [place],
        chunks,
        [],
        [shaped((block, count * HD), NARROW), shaped((2, block), WIDE)],
        [pltpu.VMEM((count, HD, block), NARROW)],
        60,
    )


def unpack_kernel(place, straight, crossed, *refs):
    count = len(refs) - 3
    chunks, out, sums, held = refs[:count], refs[count], refs[count + 1], refs[count + 2]
    me = place[0]
    block = straight.shape[0]
    for slot in range(count):
        both = turn_packed(chunks[slot][:block, :].astype(WIDE), straight[...], -crossed[...])
        held[me ^ slot, :block, :] = both.astype(NARROW)
        held[me ^ slot, block:, :] = chunks[slot][block:, :]
    for pair in range(count // 2):
        parts = [split_chunk(held[2 * pair + side]) for side in range(2)]
        cols = slice(pair * 2 * HD, (pair + 1) * 2 * HD)
        for c in range(3):
            joined = jnp.concatenate([parts[0][c], parts[1][c]], axis=1)
            out[c, :, cols] = joined
            sums[c : c + 1, cols] = jnp.sum(joined.astype(WIDE), axis=0, keepdims=True)


def unpack_heads(place, straight, crossed, chunks):
    count = len(chunks)
    block = straight.shape[0]
    return local_call(
        unpack_kernel,
        "unpack",
        [place],
        [straight, crossed, *chunks],
        [],
        [shaped((3, block, count * HD), NARROW), shaped((3, count * HD), WIDE)],
        [pltpu.VMEM((count,) + chunks[0].shape, NARROW)],
        60,
    )


def mixed_out_kernel(mixed, gain, bias, *refs, width):
    sums, weight = refs[:-6], refs[-6]
    out, low, stats, kept, sems = refs[-5:]
    fetch_all(weight, kept, sems, 1)
    total = sums[0][...]
    for other in sums[1:]:
        total = total + other[...]
    center = total[0:1] / width
    spread = total[1:2] / width - center * center
    factor = lax.rsqrt(spread + EPSILON)
    stats[...] = jnp.concatenate([center, factor], axis=0)
    columns = jnp.concatenate([center, factor, total, total, total], axis=0).T
    unit = (mixed[...].astype(WIDE) - columns[:, 0:1]) * columns[:, 1:2]
    low[...] = (unit * gain[...] + bias[...]).astype(NARROW)
    for step in range(weight.shape[1] // SPAN):
        cols = slice(step * SPAN, (step + 1) * SPAN)
        fetch(weight, kept, sems, step, 1).wait()
        out[:, cols] = jnp.dot(low[...], kept[:, cols], preferred_element_type=WIDE).astype(NARROW)


def mixed_out_product(mixed, sums, gain, bias, weight):
    rows = mixed.shape[0]
    return local_call(
        functools.partial(mixed_out_kernel, width=weight.shape[1]),
        "mixed_out",
        [],
        [mixed, gain, bias, *sums],
        [weight],
        [shaped((rows, weight.shape[1]), NARROW), shaped(mixed.shape, NARROW), shaped((2, rows), WIDE)],
        [
            pltpu.VMEM(weight.shape, NARROW),
            pltpu.SemaphoreType.DMA((weight.shape[1] // SPAN,)),
        ],
        24,
    )


def fold_lanes(values):
    total = values[:, :128]
    for begin in range(128, values.shape[1], 128):
        total = total + values[:, begin : begin + 128]
    return total


def up_kernel(owners, *refs, parts, merge):
    rows_in = refs[:parts]
    bias, gain, grad, weight = refs[parts : parts + 4]
    earlier = refs[parts + 4 : parts + 6] if merge else ()
    active_out, slope_out, rows_out, stats, rows, sums, sems = refs[-7:]
    part = rows_in[0].shape[0]
    own = [slice(i * part, (i + 1) * part) for i in range(parts)]
    copies = [
        pltpu.make_async_copy(rows_in[i], rows.at[own[i], :], sems.at[i]) for i in range(parts)
    ]
    for copy in copies:
        copy.start()
    sums[...] = jnp.zeros_like(sums)
    for copy in copies:
        copy.wait()

    @pl.loop(0, weight.shape[1] // SPAN)
    def _(step):
        cols = span_of(step)
        value = jnp.dot(rows[...], weight[:, cols], preferred_element_type=WIDE) + bias[:, cols]
        below = 0.5 + 0.5 * lax.erf(value * math.sqrt(0.5))
        active = value * below
        slope = below + value * (
            jnp.exp(-0.5 * value * value) * (1.0 / math.sqrt(2.0 * math.pi))
        )
        active_out[:, cols] = active.astype(NARROW)
        slope_out[:, cols] = slope.astype(NARROW)
        back = jnp.concatenate([grad[rows_at(owners[i], part), cols] for i in range(parts)], axis=0)
        scaled = back.astype(WIDE) * gain[:, cols]
        sums[0] += fold_lanes(active)
        sums[1] += fold_lanes(active * active)
        sums[2] += fold_lanes(scaled)
        sums[3] += fold_lanes(scaled * active)

    lines = jnp.concatenate([jnp.sum(sums[i].T, axis=0, keepdims=True) for i in range(4)], axis=0)
    if merge:
        for i in range(parts):
            mine = rows_at(owners[i], part)
            other = rows_at(owners[parts + i], part)
            stats[:, mine] = lines[:, own[i]]
            stats[:, other] = earlier[1][:, own[i]]
            rows_out[mine, :] = rows[own[i], :]
            rows_out[other, :] = earlier[0][own[i], :]
    else:
        stats[...] = lines
        rows_out[...] = rows[...]


def up_product(owners, parts, weight, bias, gain, grad, earlier=()):
    count = len(parts)
    rows = count * parts[0].shape[0]
    depth, width = weight.shape
    both = rows * (2 if earlier else 1)
    return resident_call(
        functools.partial(up_kernel, parts=count, merge=bool(earlier)),
        "up",
        [owners],
        parts,
        [bias, gain, grad, weight, *earlier],
        [
            shaped((rows, width), NARROW),
            shaped((rows, width), NARROW),
            shaped((both, depth), NARROW),
            shaped((4, both), WIDE),
        ],
        [],
        [
            pltpu.VMEM((rows, depth), NARROW),
            pltpu.VMEM((4, rows, 128), WIDE),
            pltpu.SemaphoreType.DMA((count,)),
        ],
        20,
    )


def ffn_back_kernel(owners, got, mine, *refs, parts, width):
    halves = refs[:2], refs[2:4]
    grad, gain, shift, weight, hidden_out, grad_out, lines, product = refs[4:12]
    columns, total, sums, low, sems = refs[12:]
    part = grad.shape[0] // parts
    copy = pltpu.make_async_copy(got, sums, sems.at[0])
    copy.start()
    total[...] = jnp.zeros_like(total)
    copy.wait()
    whole = (mine[...] + sums[...]) / width
    center, square, lean, cross = (whole[i : i + 1] for i in range(4))
    factor = lax.rsqrt(square - center * center + EPSILON)
    cross = (cross - center * lean) * factor
    columns[...] = jnp.concatenate([center, factor, lean, cross, whole], axis=0).T

    @pl.loop(0, weight.shape[1] // SPAN)
    def _(step):
        cols = span_of(step)
        line = [0.0, 0.0, 0.0]
        grads = []
        for i in range(parts):
            active, slope = halves[i // (parts // 2)]
            own = i % (parts // 2)
            own = slice(own * part, (own + 1) * part)
            rows = rows_at(owners[i], part)
            center, factor, lean, cross = (columns[rows, k : k + 1] for k in range(4))
            unit = (active[own, cols].astype(WIDE) - center) * factor
            hidden_out[rows, cols] = (unit * gain[:, cols] + shift[:, cols]).astype(NARROW)
            back = grad[rows, cols].astype(WIDE)
            grad_active = (back * gain[:, cols] - lean - unit * cross) * factor
            grad_up = (grad_active * slope[own, cols].astype(WIDE)).astype(NARROW)
            grad_out[rows, cols] = grad_up
            grads.append(grad_up)
            line[0] = line[0] + jnp.sum(grad_up.astype(WIDE), axis=0, keepdims=True)
            line[1] = line[1] + jnp.sum(back * unit, axis=0, keepdims=True)
            line[2] = line[2] + jnp.sum(back, axis=0, keepdims=True)
        lines[:, cols] = jnp.concatenate(line, axis=0)
        total[...] += lax.dot_general(
            jnp.concatenate(grads, axis=0),
            weight[:, cols],
            (((1,), (1,)), ((), ())),
            preferred_element_type=WIDE,
        )

    outgoing = []
    for i in range(parts):
        low[i * part : (i + 1) * part, :] = total[i * part : (i + 1) * part, :].astype(NARROW)
        copy = pltpu.make_async_copy(
            low.at[i * part : (i + 1) * part, :],
            product.at[rows_at(owners[i], part), :],
            sems.at[1 + i],
        )
        copy.start()
        outgoing.append(copy)
    for copy in outgoing:
        copy.wait()


def ffn_back_product(owners, sums, near, far, grad, gain, shift, weight, width):
    rows, local = grad.shape
    depth = weight.shape[0]
    both = shaped((rows, local), NARROW)
    parts = owners.shape[0]
    mine, got = sums
    hidden, grad_up, lines, product = resident_call(
        functools.partial(ffn_back_kernel, parts=parts, width=width),
        "ffn_back",
        [owners],
        [got],
        [mine, *near, *far, grad, gain, shift, weight],
        [both, both, shaped((3, local), WIDE)],
        [shaped((rows, depth), NARROW)],
        [
            pltpu.VMEM((rows, 8), WIDE),
            pltpu.VMEM((rows, depth), WIDE),
            pltpu.VMEM(mine.shape, WIDE),
            pltpu.VMEM((rows, depth), NARROW),
            pltpu.SemaphoreType.DMA((1 + parts,)),
        ],
        24,
    )
    return hidden, grad_up, product, lines


def mixed_back_kernel(seat, *refs, parts):
    mixed, stats, gain, weight, grad, rows, sums, lines, kept, sem = refs[parts:]
    copy = pltpu.make_async_copy(weight, kept, sem)
    copy.start()
    part = refs[0].shape[0]
    for i in range(parts):
        rows[rows_at(seat[i], part), :] = refs[i][...]
    columns = jnp.concatenate([stats[...]] * 4, axis=0).T
    unit = (mixed[...].astype(WIDE) - columns[:, 0:1]) * columns[:, 1:2]
    copy.wait()
    back = lax.dot_general(
        rows[...], kept[...], (((1,), (1,)), ((), ())), preferred_element_type=WIDE
    )
    grad[...] = back
    lines[0:1, :] = jnp.sum(back * unit, axis=0, keepdims=True)
    lines[1:2, :] = jnp.sum(back, axis=0, keepdims=True)
    scaled = back * gain[...]
    sums[0:1, :] = jnp.sum(fold_lanes(scaled).T, axis=0, keepdims=True)
    sums[1:2, :] = jnp.sum(fold_lanes(scaled * unit).T, axis=0, keepdims=True)


def mixed_back_product(seat, parts, mixed, stats, gain, weight):
    rows, local = mixed.shape
    return local_call(
        functools.partial(mixed_back_kernel, parts=len(parts)),
        "mixed_back",
        [seat],
        [*parts, mixed, stats, gain],
        [weight],
        [
            shaped((rows, local), WIDE),
            shaped((rows, weight.shape[1]), NARROW),
            shaped((2, rows), WIDE),
            shaped((2, local), WIDE),
        ],
        [pltpu.VMEM(weight.shape, NARROW), pltpu.SemaphoreType.DMA],
        24,
    )


def cut_kernel(seat, grad, mixed, stats, gain, *refs, count, width):
    sums = refs[:count]
    outs, held = refs[count:-1], refs[-1]
    total = sums[0][...]
    for other in sums[1:]:
        total = total + other[...]
    total = total / width
    columns = jnp.concatenate([stats[...], total] * 2, axis=0).T
    factor = columns[:, 1:2]
    unit = (mixed[...].astype(WIDE) - columns[:, 0:1]) * factor
    result = (grad[...] * gain[...] - columns[:, 2:3] - unit * columns[:, 3:4]) * factor
    result = result.astype(NARROW)
    heads = len(outs)
    for pair in range(heads // 2):
        both = result[:, pair * 2 * HD : (pair + 1) * 2 * HD].T
        held[2 * pair] = both[:HD]
        held[2 * pair + 1] = both[HD:]
    for slot in range(heads):
        outs[slot][...] = held[seat[0] ^ slot]


def cut_heads(seat, grad, mixed, stats, gain, sums, heads, width):
    block = grad.shape[0]
    return local_call(
        functools.partial(cut_kernel, count=len(sums), width=width),
        "cut",
        [seat],
        [grad, mixed, stats, gain, *sums],
        [],
        [shaped((HD, block), NARROW)] * heads,
        [pltpu.VMEM((heads, HD, block), NARROW)],
        60,
    )


def attn_back_kernel(grads, rows, gain, bias, weight, product, lines, kept, sems):
    fetch_all(weight, kept, sems, 1)

    @pl.loop(0, product.shape[1] // SPAN)
    def _(step):
        cols = span_of(step)
        fetch(weight, kept, sems, step, 1).wait()
        total = 0.0
        for c in range(grads.shape[0]):
            total = total + lax.dot_general(
                grads[c], kept[c, cols, :], (((1,), (1,)), ((), ())), preferred_element_type=WIDE
            )
        product[:, cols] = total.astype(NARROW)
        unit = (rows[:, cols].astype(WIDE) - bias[:, cols]) / gain[:, cols]
        lines[0:1, cols] = jnp.sum(total * unit, axis=0, keepdims=True)
        lines[1:2, cols] = jnp.sum(total, axis=0, keepdims=True)


def attn_back_product(grads, rows, gain, bias, weight):
    count, depth = rows.shape
    return local_call(
        attn_back_kernel,
        "attn_back",
        [],
        [grads, rows, gain, bias],
        [weight],
        [shaped((count, depth), NARROW), shaped((2, depth), WIDE)],
        [
            pltpu.VMEM(weight.shape, NARROW),
            pltpu.SemaphoreType.DMA((depth // SPAN,)),
        ],
        60,
    )


def shards(
    inputs,
    segment_ids,
    cotangent,
    qkv_weight,
    qkv_bias,
    out_weight,
    out_bias,
    up_weight,
    up_bias,
    down_weight,
    down_bias,
    input_gain,
    input_bias,
    mixed_gain,
    mixed_bias,
    middle_gain,
    middle_bias,
    hidden_gain,
    hidden_bias,
    qkv_average,
    out_average,
    up_average,
    down_average,
    decay_rate,
):
    seq_count = lax.axis_size("seq")
    seq_rank = lax.axis_index("seq")
    local_rows = segment_ids.shape[0]
    model_width = inputs.shape[1]
    local_width = qkv_weight.shape[2]
    heads_here = local_width // HD
    team = heads_here
    teams = seq_count // team
    place = seq_rank % team
    home = seq_rank - place

    def trade(chunks):
        got = {m: hop(chunks[m], "seq", m, seq_count) for m in range(2, team)}
        got[1] = hop(after(chunks[1], got[2]), "seq", 1, seq_count)
        return [chunks[0]] + [got[m] for m in range(1, team)]

    row_index = seq_rank * local_rows + jnp.arange(local_rows, dtype=jnp.int32)
    documents = jnp.arange(COUNT, dtype=jnp.int32)
    member = segment_ids[:, None] == documents[None, :]
    first_all = jnp.min(jnp.where(member, row_index[:, None], LARGEST), axis=0)
    bit = 1
    while bit < seq_count:
        first_all = jnp.minimum(first_all, hop(first_all, "seq", bit, seq_count))
        bit *= 2

    def starts_of(rows):
        earlier = first_all[None, :] <= rows[:, None]
        return jnp.max(jnp.where(earlier, first_all[None, :], 0), axis=1)

    cosine, sine, growth = xpos_tables(row_index - starts_of(row_index), HD)
    shrink = 1.0 / growth
    straight = jnp.concatenate([cosine * growth] * 2 + [cosine * shrink] * 2, axis=1)
    crossed = jnp.concatenate(
        [-sine * growth, sine * growth, -sine * shrink, sine * shrink], axis=1
    )
    team_rows = home * local_rows + jnp.arange(team * local_rows, dtype=jnp.int32)
    team_starts = starts_of(team_rows).reshape(team, local_rows)
    spans = jnp.stack([jnp.min(team_starts, axis=1), jnp.max(team_starts, axis=1)], axis=1)
    info = jnp.concatenate(
        [jnp.stack([place, home]).astype(jnp.int32), spans.reshape(-1)]
    )
    team_starts = team_starts.reshape(team, 1, local_rows)
    seat = jnp.reshape(place, (1,)).astype(jnp.int32)

    tp_count = lax.axis_size("tp")
    tp_rank = lax.axis_index("tp")
    inner = tp_count // 2
    near_first = part_owners(0)
    far_first = part_owners(inner)

    def line(vector):
        return vector.astype(WIDE).reshape(1, -1)

    def exchange(values):
        mask = 1
        while 2 * mask < tp_count:
            values = values + hop(values, "tp", mask, tp_count)
            mask *= 2
        return [values, hop(values, "tp", mask, tp_count)]

    inputs_wide = inputs.astype(WIDE)
    input_normed, input_back = jax.vjp(
        norm_rows, inputs_wide, input_gain.astype(WIDE), input_bias.astype(WIDE)
    )
    attn_parts = gather_parts(input_normed.astype(NARROW))
    rate = decay_rate[0]
    seq_part = model_width // seq_count
    offset = seq_rank * seq_part

    def average(old, weight, axis):
        piece = lax.dynamic_slice_in_dim(weight, offset, seq_part, axis).astype(WIDE)
        return rate * old + (1.0 - rate) * piece

    qkv_new = average(qkv_average, qkv_weight, 1)
    out_new = average(out_average, out_weight, 1)
    up_new = average(up_average, up_weight, 0)
    down_new = average(down_average, down_weight, 1)
    attn_parts[0] = after(attn_parts[0], straight, crossed)

    def pack(parts, chairs, earlier=()):
        return pack_heads(
            seat, chairs, parts, qkv_weight, qkv_bias.astype(WIDE), straight, crossed, team, earlier
        )

    packed = pack(attn_parts[:inner], near_first)
    attn_parts[inner] = after(attn_parts[inner], *packed)
    *packs, attn_in = pack(attn_parts[inner:], far_first, packed)
    grad_rows = gather_rows(after(cotangent, packs[0]))
    chunks = trade(packs)
    everyone = None
    if teams > 1:
        rings = [[j + team * t for t in range(teams)] for j in range(team)]
        natural = jnp.stack(chunks)[jnp.arange(team) ^ place]
        everyone = lax.all_gather(
            natural, "seq", axis=0, tiled=True, axis_index_groups=rings
        )
    *mixed_out, mixed_wide, logs = attend_forward(info, team_starts, chunks, everyone, tp_count)
    mixed_got = trade(mixed_out)

    mixed_got[0] = after(mixed_got[0], grad_rows)
    mixed, mixed_sums = join_heads(seat, mixed_got)
    out_product, mixed_low, mixed_stats = mixed_out_product(
        mixed, exchange(mixed_sums), line(mixed_gain), line(mixed_bias), out_weight
    )
    grad_hidden = jnp.einsum(
        "rd,fd->rf", grad_rows, down_weight, preferred_element_type=WIDE
    ).astype(NARROW)
    summed = after(scatter_rows(out_product), grad_hidden, qkv_new, out_new, up_new, down_new)
    middle = inputs_wide + summed + out_bias.astype(WIDE)
    normed, middle_back = jax.vjp(
        norm_rows, middle, middle_gain.astype(WIDE), middle_bias.astype(WIDE)
    )
    ffn_parts = gather_parts(normed.astype(NARROW))
    gain_line = line(hidden_gain)

    def up(parts, chairs, earlier=()):
        return up_product(
            chairs, parts, up_weight, line(up_bias), gain_line, grad_hidden, earlier
        )

    *up_near, ffn_near, sums_near = up(ffn_parts[:inner], near_first)
    ffn_parts[inner] = after(ffn_parts[inner], sums_near)
    *up_far, ffn_in, sums = up(ffn_parts[inner:], far_first, (ffn_near, sums_near))
    hidden_low, grad_up, ffn_back, hidden_lines = ffn_back_product(
        near_first,
        exchange(sums),
        up_near,
        up_far,
        grad_hidden,
        gain_line,
        line(hidden_bias),
        up_weight,
        FF,
    )
    upbias_part, hiddengain_part, hiddenbias_part = hidden_lines
    down_product = jnp.dot(hidden_low, down_weight, preferred_element_type=WIDE).astype(NARROW)
    late_rows = after(grad_rows, down_product)
    down_sent = send_gradient(hidden_low, late_rows, seq_rank, seq_count, True)
    up_sent = send_gradient(after(grad_up, down_product)[None], ffn_in, seq_rank, seq_count, False)
    summed = after(scatter_rows(ffn_back), down_sent, up_sent)
    norm_grad, middlegain_part, middlebias_part = middle_back(summed)
    grad_middle = cotangent.astype(WIDE) + norm_grad
    grad_low = grad_middle.astype(NARROW)
    middle_parts = gather_parts(grad_low)
    down_got = after(hop(down_sent, "seq", 1, seq_count), grad_low)
    up_got = hop(up_sent, "seq", 1, seq_count)
    down_pieces = keep_gradient(hidden_low, grad_rows, down_got, seq_rank, seq_count, True, True)
    up_pieces = keep_gradient(
        grad_up[None], ffn_in, up_got, seq_rank, seq_count, False, True
    )
    down_pieces = start_gradient(down_pieces, seq_count)
    middle_parts[-1] = after(middle_parts[-1], *up_pieces, *down_pieces)
    outbias_part = jnp.sum(grad_low, axis=0, dtype=WIDE)
    downbias_part = jnp.sum(cotangent, axis=0, dtype=WIDE)
    grad_mixed_norm, grad_mixed_rows, back_sums, mixed_lines = mixed_back_product(
        near_first,
        middle_parts,
        mixed,
        mixed_stats,
        line(mixed_gain),
        out_weight,
    )
    mixedgain_part, mixedbias_part = mixed_lines
    grad_cuts = cut_heads(
        seat,
        grad_mixed_norm,
        mixed,
        mixed_stats,
        line(mixed_gain),
        exchange(back_sums),
        team,
        model_width,
    )
    down_pieces = list(down_pieces)
    for slot in range(1, len(down_pieces)):
        down_pieces[slot] = after(down_pieces[slot], grad_mixed_norm)
    down_rest = finish_gradient(down_pieces, seq_count)
    grad_chunks = trade(grad_cuts)
    up_pieces = list(up_pieces)
    for slot in range(1, len(up_pieces)):
        up_pieces[slot] = after(up_pieces[slot], *grad_chunks)
    up_pieces = list(start_gradient(up_pieces, seq_count))
    layer_out = (
        middle
        + scatter_rows(after(down_product, grad_mixed_norm))
        + down_bias.astype(WIDE)
    ).astype(NARROW)
    pieces = attend_backward(
        info,
        team_starts,
        logs,
        mixed_wide,
        chunks,
        grad_chunks,
        everyone,
        tp_count,
    )
    pieces = list(pieces)
    down_grad = add_gradient(down_rest, pieces[0])
    arrived = list(down_rest[1:4:2]) + up_pieces[1:3]
    pieces = [after(piece, *arrived) for piece in pieces]
    out_sent = send_gradient(mixed_low, after(grad_mixed_rows, pieces[0]), seq_rank, seq_count, True)
    out_got = hop(out_sent, "seq", 1, seq_count)
    out_pieces = keep_gradient(mixed_low, grad_mixed_rows, out_got, seq_rank, seq_count, True)
    pieces[0] = after(pieces[0], layer_out)
    if teams > 1:
        natural = lax.psum_scatter(
            pieces[0], "seq", scatter_dimension=0, tiled=True, axis_index_groups=rings
        )
        pieces = [
            lax.dynamic_index_in_dim(natural, place ^ m, 0, keepdims=False) for m in range(team)
        ]
    parts_got = trade(pieces)
    parts_got[0] = after(parts_got[0], down_grad, *out_pieces)
    for slot in range(1, len(up_pieces)):
        up_pieces[slot] = after(up_pieces[slot], *parts_got)
    up_rest = finish_gradient(up_pieces, seq_count)
    out_pieces = list(out_pieces)
    for slot in range(1, len(out_pieces)):
        out_pieces[slot] = after(out_pieces[slot], *parts_got)
    out_grad = add_gradient(finish_gradient(out_pieces, seq_count))
    stacked, qkvbias_part = unpack_heads(seat, straight, crossed, parts_got)
    qkv_got = hop(send_gradient(stacked, attn_in, seq_rank, seq_count, False), "seq", 1, seq_count)
    attn_back, attn_lines = attn_back_product(
        stacked, attn_in, line(input_gain), line(input_bias), qkv_weight
    )
    inputgain_part, inputbias_part = attn_lines
    grad_attn_in = scatter_rows(attn_back)
    qkv_got = after(qkv_got, out_grad, attn_back, *(up_rest[1:4:2] if isinstance(up_rest, tuple) else ()))
    qkv_pieces = keep_gradient(stacked, attn_in, qkv_got, seq_rank, seq_count, False, True)
    qkv_pieces = start_gradient(qkv_pieces, seq_count)
    qkv_sent = []
    qkv_grad = add_gradient(finish_gradient(qkv_pieces, seq_count, qkv_sent))

    def spread_norms(parts):
        both = jnp.stack(parts).reshape(len(parts), seq_count, tp_count, -1)
        mine = tp_scatter(both.transpose(2, 1, 0, 3))
        return mine.reshape(seq_count, -1)

    inputgain_part = after(inputgain_part, qkv_pieces[0])
    vectors = jnp.concatenate(
        [
            item.reshape(seq_count, -1)
            for item in (
                upbias_part,
                hiddengain_part,
                hiddenbias_part,
                mixedgain_part,
                mixedbias_part,
                qkvbias_part[0],
                qkvbias_part[1],
                qkvbias_part[2],
            )
        ]
        + [
            spread_norms(
                [
                    middlegain_part,
                    middlebias_part,
                    outbias_part,
                    downbias_part,
                    inputgain_part,
                    inputbias_part,
                ]
            )
        ],
        axis=1,
    )
    vector_sums = vector_scatter(after(vectors, *qkv_sent), seq_rank, seq_count)
    up_grad = add_gradient(up_rest, vector_sums)[0]

    grad_input_norm, _, _ = input_back(grad_attn_in)
    input_grad = (grad_middle + grad_input_norm).astype(NARROW)
    narrow_part = local_width // seq_count
    wide_part = up_bias.shape[0] // seq_count
    norm_part = model_width // (seq_count * lax.axis_size("tp"))

    def cuts(vector, widths):
        begin = 0
        pieces = []
        for width in widths:
            pieces.append(vector[begin : begin + width])
            begin += width
        return pieces

    (
        upbias_grad,
        hiddengain_grad,
        hiddenbias_grad,
        mixedgain_grad,
        mixedbias_grad,
        q_bias,
        k_bias,
        v_bias,
        middlegain_grad,
        middlebias_grad,
        outbias_grad,
        downbias_grad,
        inputgain_grad,
        inputbias_grad,
    ) = cuts(vector_sums, (wide_part,) * 3 + (narrow_part,) * 5 + (norm_part,) * 6)
    return (
        layer_out,
        input_grad,
        qkv_grad,
        jnp.stack([q_bias, k_bias, v_bias]),
        out_grad,
        outbias_grad,
        up_grad,
        upbias_grad,
        down_grad,
        downbias_grad,
        inputgain_grad,
        inputbias_grad,
        mixedgain_grad,
        mixedbias_grad,
        middlegain_grad,
        middlebias_grad,
        hiddengain_grad,
        hiddenbias_grad,
        qkv_new,
        out_new,
        up_new,
        down_new,
    )


def solution(mesh):
    in_specs = (
        P(("seq", "tp"), None),
        P("seq"),
        P(("seq", "tp"), None),
        P(None, None, "tp"),
        P(None, "tp"),
        P("tp", None),
        P(),
        P(None, "tp"),
        P("tp"),
        P("tp", None),
        P(),
        P(),
        P(),
        P("tp"),
        P("tp"),
        P(),
        P(),
        P("tp"),
        P("tp"),
        P(None, "seq", "tp"),
        P("tp", "seq"),
        P("seq", "tp"),
        P("tp", "seq"),
        P(),
    )
    out_specs = (
        P(("seq", "tp"), None),
        P(("seq", "tp"), None),
        P(None, "seq", "tp"),
        P(None, ("tp", "seq")),
        P("tp", "seq"),
        P(("seq", "tp")),
        P("seq", "tp"),
        P(("tp", "seq")),
        P("tp", "seq"),
        P(("seq", "tp")),
        P(("seq", "tp")),
        P(("seq", "tp")),
        P(("tp", "seq")),
        P(("tp", "seq")),
        P(("seq", "tp")),
        P(("seq", "tp")),
        P(("tp", "seq")),
        P(("tp", "seq")),
        P(None, "seq", "tp"),
        P("tp", "seq"),
        P("seq", "tp"),
        P("tp", "seq"),
    )
    return jax.shard_map(shards, mesh=mesh, in_specs=in_specs, out_specs=out_specs, check_vma=False)
```
